32 devices in a mesh: fsdp: 2 (over y), ctx: 4 (over x, core), tp: 4 (over z).
Axes of the slice: x: 2, y: 2, z: 4, core: 2. Of those that a mesh axis runs over, the one named last changes fastest.
Arguments:
- tokens: bfloat16 [3, 2, 1024, 2560], P(None, 'fsdp', 'ctx'), may hold values from -6 to 6
- out_cotangent: bfloat16 [3, 2, 1024, 2560], P(None, 'fsdp', 'ctx'), may hold values from -6 to 6
- seq_lengths: int32 [3, 2], P(None, 'fsdp'), may hold values from 256 to 1024, as said below
- span_order: int32 [3, 2, 8], P(None, 'fsdp'), may hold values from 0 to 7, each once within a row
- attention_input_weight: float32 [2560, 3840], P(('fsdp', 'ctx'), 'tp'), may hold values from -0.125 to 0.125
- attention_input_first: float32 [2560, 3840], P(('fsdp', 'ctx'), 'tp'), may hold values from -20 to 20
- attention_input_squared: float32 [2560, 3840], P(('fsdp', 'ctx'), 'tp'), may hold values from 26.25792 to 420.3264
- attend_out: float32 [2560, 2560], P('tp', ('fsdp', 'ctx')), may hold values from -1 to 1
- attend_out_moment: float32 [2560, 2560], P('tp', ('fsdp', 'ctx')), may hold values from -4 to 4
- attend_out_second: float32 [2560, 2560], P('tp', ('fsdp', 'ctx')), may hold values from 1.0503168 to 16.813057
- gate_up: float32 [2560, 14336], P(('fsdp', 'ctx'), 'tp'), may hold values from -0.125 to 0.125
- gate_up_moment: float32 [2560, 14336], P(('fsdp', 'ctx'), 'tp'), may hold values from -16 to 16
- gate_up_second: float32 [2560, 14336], P(('fsdp', 'ctx'), 'tp'), may hold values from 13.654119 to 218.56973
- down_weight: float32 [7168, 2560], P('tp', ('fsdp', 'ctx')), may hold values from -0.0625 to 0.0625
- down_weight_moment: float32 [7168, 2560], P('tp', ('fsdp', 'ctx')), may hold values from -24 to 24
- down_weight_second: float32 [7168, 2560], P('tp', ('fsdp', 'ctx')), may hold values from 37.811405 to 605.27
- norm_gains: float32 [2, 2560], P(None, ('fsdp', 'ctx')), may hold values from 0.5 to 1.5
- norm_gains_moment: float32 [2, 2560], P(None, ('fsdp', 'ctx')), may hold values from -40 to 40
- norm_gains_second: float32 [2, 2560], P(None, ('fsdp', 'ctx')), may hold values from 105.03168 to 1681.3055
Outputs:
- mixed: bfloat16 [3, 2, 1024, 2560], P(None, 'fsdp', 'ctx')
- input_grad: float32 [3, 2, 1024, 2560], P(None, 'fsdp', 'ctx')
- attend_in_moment_new: float32 [2560, 3840], P(('fsdp', 'ctx'), 'tp')
- attend_in_second_new: float32 [2560, 3840], P(('fsdp', 'ctx'), 'tp')
- attend_in_new: float32 [2560, 3840], P(('fsdp', 'ctx'), 'tp')
- attend_in_copy: bfloat16 [2560, 3840], P(('fsdp', 'ctx'), 'tp')
- attend_out_moment_new: float32 [2560, 2560], P('tp', ('fsdp', 'ctx'))
- attend_out_second_new: float32 [2560, 2560], P('tp', ('fsdp', 'ctx'))
- attend_out_new: float32 [2560, 2560], P('tp', ('fsdp', 'ctx'))
- attend_out_copy: bfloat16 [2560, 2560], P('tp', ('fsdp', 'ctx'))
- gate_up_moment_new: float32 [2560, 14336], P(('fsdp', 'ctx'), 'tp')
- gate_up_second_new: float32 [2560, 14336], P(('fsdp', 'ctx'), 'tp')
- gate_up_new: float32 [2560, 14336], P(('fsdp', 'ctx'), 'tp')
- gate_up_copy: bfloat16 [2560, 14336], P(('fsdp', 'ctx'), 'tp')
- down_weight_moment_new: float32 [7168, 2560], P('tp', ('fsdp', 'ctx'))
- down_weight_second_new: float32 [7168, 2560], P('tp', ('fsdp', 'ctx'))
- down_weight_new: float32 [7168, 2560], P('tp', ('fsdp', 'ctx'))
- down_weight_copy: bfloat16 [7168, 2560], P('tp', ('fsdp', 'ctx'))
- norm_gains_moment_new: float32 [2, 2560], P(None, ('fsdp', 'ctx'))
- norm_gains_second_new: float32 [2, 2560], P(None, ('fsdp', 'ctx'))
- norm_gains_new: float32 [2, 2560], P(None, ('fsdp', 'ctx'))
The draws below stay inside these ranges and needn't reach their ends.
Inputs may be any that keep to these rules, and one draw needn't show every extreme that they name: `seq_lengths`: for every slot index, one micro-batch drawn from the seed has length 1024; lengths are at least 256, reached in some slot. `span_order`: each row is a permutation of the span numbers.
All inputs are finite; a program needn't handle non-finite values.
Results may differ from the reference program's by a relative error of at most 0.025.
Values may be sent and summed in bfloat16 or wider, within the bound.
A program may use at most 320 MiB of HBM per device.

```python
import math
import jax
import jax.numpy as jnp
from jax import lax

MODEL_DIMENSION = 2560
QUERY_HEADS = 32
KEY_VALUE_HEADS = 8
HEAD_DIMENSION = 80
FF = 7168
SLOT_POSITIONS = 1024
MICRO_BATCHES = 3
STEP = 10
SLOTS_PER_BATCH = 2
N_CTX = 4
N_TP = 4


def draw_seq_lengths(key, part):
    key = jax.random.fold_in(key, 7)
    base_key, pick_key = jax.random.split(key)
    base_draw = jax.random.randint(base_key, (MICRO_BATCHES, SLOTS_PER_BATCH), SLOT_POSITIONS // 4, SLOT_POSITIONS + 1)
    chosen = jax.random.randint(pick_key, (SLOTS_PER_BATCH,), 0, MICRO_BATCHES)
    micro_ids = jnp.arange(MICRO_BATCHES, dtype=jnp.int32)[:, None]
    slot_ids = jnp.arange(SLOTS_PER_BATCH, dtype=jnp.int32)[None, :]
    shortest = (micro_ids == (chosen[None, :] + 1) % MICRO_BATCHES) & (slot_ids == 0)
    drawn = jnp.where(micro_ids == chosen[None, :], SLOT_POSITIONS, jnp.where(shortest, SLOT_POSITIONS // 4, base_draw))
    return drawn.astype(jnp.int32)


def level_of(stream_key, extent, cuts, low, high):
    def one(axis_at, parts):
        heights = jax.random.uniform(jax.random.fold_in(jax.random.fold_in(stream_key, 6), axis_at), (parts,), jnp.float32, low / len(cuts), high / len(cuts))
        return jnp.repeat(jnp.exp(heights), extent[axis_at] // parts).reshape((-1,) + (1,) * (len(extent) - axis_at - 1))

    gain = one(*cuts[0])
    for cut in cuts[1:]:
        gain = gain * one(*cut)
    return gain


def centred(rng, shape, spread, limit, cuts=(), kind=jnp.bfloat16):
    factor_of = level_of(rng, shape, cuts, -0.22, 0.18) if cuts else 1.0
    values = jax.random.normal(rng, shape, jnp.float32) * spread * factor_of
    return jnp.minimum(jnp.maximum(values, -limit), limit).astype(kind)


def setup_inputs(seed: int = 0) -> dict:
    keys = jax.random.split(jax.random.key(seed), 20)
    tokens = centred(keys[0], (MICRO_BATCHES, SLOTS_PER_BATCH, SLOT_POSITIONS, MODEL_DIMENSION), 1.0, 6.0, ((1, 2), (2, 4)))
    out_cotangent = centred(keys[1], (MICRO_BATCHES, SLOTS_PER_BATCH, SLOT_POSITIONS, MODEL_DIMENSION), 1.0, 6.0, ((1, 2), (2, 4)))
    seq_lengths = draw_seq_lengths(jax.random.fold_in(keys[19], 71), 0)
    span_order = jax.vmap(lambda own: jax.random.permutation(own, 2 * N_CTX))(jax.random.split(keys[3], MICRO_BATCHES * SLOTS_PER_BATCH)).reshape((MICRO_BATCHES, SLOTS_PER_BATCH, 2 * N_CTX)).astype(jnp.int32)
    attention_input_weight = centred(keys[4], (MODEL_DIMENSION, KEY_VALUE_HEADS * (QUERY_HEADS // KEY_VALUE_HEADS + 2) * HEAD_DIMENSION), MODEL_DIMENSION ** -0.5, 0.125, ((0, 8), (1, 4)), jnp.float32)
    attention_input_first = centred(keys[5], (MODEL_DIMENSION, KEY_VALUE_HEADS * (QUERY_HEADS // KEY_VALUE_HEADS + 2) * HEAD_DIMENSION), (0.111 * 0.5 * (MICRO_BATCHES * SLOTS_PER_BATCH * SLOT_POSITIONS * 0.65) ** 0.5), 20.0, ((0, 8), (1, 4)), jnp.float32)
    attention_input_squared = jnp.clip(jnp.exp(math.log(420.3264) - 2.773064 * jax.random.uniform(keys[6], (MODEL_DIMENSION, KEY_VALUE_HEADS * (QUERY_HEADS // KEY_VALUE_HEADS + 2) * HEAD_DIMENSION), jnp.float32) ** level_of(keys[6], (MODEL_DIMENSION, KEY_VALUE_HEADS * (QUERY_HEADS // KEY_VALUE_HEADS + 2) * HEAD_DIMENSION), ((0, 8), (1, 4)), -0.2, 0.2)), 26.25792, 420.3264)
    attend_out = centred(keys[7], (QUERY_HEADS * HEAD_DIMENSION, MODEL_DIMENSION), (QUERY_HEADS * HEAD_DIMENSION // 64) ** -0.5, 1.0, ((0, 4), (1, 8)), jnp.float32)
    attend_out_moment = centred(keys[8], (QUERY_HEADS * HEAD_DIMENSION, MODEL_DIMENSION), (0.111 * 0.1 * (MICRO_BATCHES * SLOTS_PER_BATCH * SLOT_POSITIONS * 0.65) ** 0.5), 4.0, ((0, 4), (1, 8)), jnp.float32)
    attend_out_second = jnp.clip(jnp.exp(math.log(16.813057) - 2.773064 * jax.random.uniform(keys[9], (QUERY_HEADS * HEAD_DIMENSION, MODEL_DIMENSION), jnp.float32) ** level_of(keys[9], (QUERY_HEADS * HEAD_DIMENSION, MODEL_DIMENSION), ((0, 4), (1, 8)), -0.2, 0.2)), 1.0503168, 16.813057)
    gate_up = centred(keys[10], (MODEL_DIMENSION, 2 * FF), MODEL_DIMENSION ** -0.5, 0.125, ((0, 8), (1, 4)), jnp.float32)
    gate_up_moment = centred(keys[11], (MODEL_DIMENSION, 2 * FF), (0.111 * 0.36 * (MICRO_BATCHES * SLOTS_PER_BATCH * SLOT_POSITIONS * 0.65) ** 0.5), 16.0, ((0, 8), (1, 4)), jnp.float32)
    gate_up_second = jnp.clip(jnp.exp(math.log(218.56973) - 2.773064 * jax.random.uniform(keys[12], (MODEL_DIMENSION, 2 * FF), jnp.float32) ** level_of(keys[12], (MODEL_DIMENSION, 2 * FF), ((0, 8), (1, 4)), -0.2, 0.2)), 13.654119, 218.56973)
    down_weight = centred(keys[13], (FF, MODEL_DIMENSION), FF ** -0.5, 0.0625, ((0, 4), (1, 8)), jnp.float32)
    down_weight_moment = centred(keys[14], (FF, MODEL_DIMENSION), (0.111 * 0.6 * (MICRO_BATCHES * SLOTS_PER_BATCH * SLOT_POSITIONS * 0.65) ** 0.5), 24.0, ((0, 4), (1, 8)), jnp.float32)
    down_weight_second = jnp.clip(jnp.exp(math.log(605.27) - 2.773064 * jax.random.uniform(keys[15], (FF, MODEL_DIMENSION), jnp.float32) ** level_of(keys[15], (FF, MODEL_DIMENSION), ((0, 4), (1, 8)), -0.2, 0.2)), 37.811405, 605.27)
    norm_gains = jnp.clip(1.0 + 0.1 * jax.random.normal(keys[16], (2, MODEL_DIMENSION), jnp.float32), 0.5, 1.5)
    norm_gains_moment = centred(keys[17], (2, MODEL_DIMENSION), (0.111 * (MICRO_BATCHES * SLOTS_PER_BATCH * SLOT_POSITIONS * 0.65) ** 0.5), 40.0, ((1, 8),), jnp.float32)
    norm_gains_second = jnp.clip(jnp.exp(math.log(1681.3055) - 2.773064 * jax.random.uniform(keys[18], (2, MODEL_DIMENSION), jnp.float32) ** level_of(keys[18], (2, MODEL_DIMENSION), ((1, 8),), -0.2, 0.2)), 105.03168, 1681.3055)
    return dict(tokens=tokens, out_cotangent=out_cotangent, seq_lengths=seq_lengths, span_order=span_order, attention_input_weight=attention_input_weight, attention_input_first=attention_input_first, attention_input_squared=attention_input_squared, attend_out=attend_out, attend_out_moment=attend_out_moment, attend_out_second=attend_out_second, gate_up=gate_up, gate_up_moment=gate_up_moment, gate_up_second=gate_up_second, down_weight=down_weight, down_weight_moment=down_weight_moment, down_weight_second=down_weight_second, norm_gains=norm_gains, norm_gains_moment=norm_gains_moment, norm_gains_second=norm_gains_second)


@jax.custom_vjp
def lower_precision(v):
    return lax.optimization_barrier(v.astype(jnp.bfloat16)).astype(jnp.float32)

@jax.custom_vjp
def low_back(v):
    return v

def low_keep(v):
    return (lower_precision(v), None)

def low_pass(kept, grad):
    return (grad,)

def back_keep(v):
    return (v, None)

def back_low(kept, grad):
    return (lower_precision(grad),)
lower_precision.defvjp(low_keep, low_pass)
low_back.defvjp(back_keep, back_low)
rope_base = 1000000.0
norm_eps = 1e-05
beta_one = 0.9
beta_two = 0.95
adam_eps = 1e-08
weight_decay = 0.1
learn_rates = (0.1, 0.5, 0.05, 0.04, 0.8)
decay_flags = (1.0, 1.0, 1.0, 1.0, 0.0)
neg_big = -1e+30
highest_precision = lax.Precision.HIGHEST

def rope_tables(token_positions):
    half_width = HEAD_DIMENSION // 2
    inverse = rope_base ** (-(jnp.arange(half_width, dtype=jnp.float32) * 2.0 / HEAD_DIMENSION))
    angles = token_positions.astype(jnp.float32)[..., None] * inverse
    return (jnp.cos(angles), jnp.sin(angles))

def rotate(values, cosine_table, sine_table):
    half_width = values.shape[-1] // 2
    first_half = values[..., :half_width]
    second_half = values[..., half_width:]
    return jnp.concatenate([first_half * cosine_table - second_half * sine_table, second_half * cosine_table + first_half * sine_table], -1)

def normalize(values, gain_row):
    return values * lax.rsqrt(lax.optimization_barrier(jnp.mean(values * values, -1, keepdims=True)) + norm_eps) * gain_row

def adam_update(weight, moment, second, gradient, learn_rate, decay_flag):
    moment = beta_one * moment + (1.0 - beta_one) * gradient
    second = beta_two * second + (1.0 - beta_two) * gradient * gradient
    moment_hat = moment / (1.0 - beta_one ** STEP)
    second_hat = second / (1.0 - beta_two ** STEP)
    weight = weight - learn_rate * (moment_hat / (jnp.sqrt(second_hat) + adam_eps) + decay_flag * weight_decay * weight)
    return (moment, second, weight)

def layer_forward(params, tokens_seq, token_positions, length):
    attention_input_weight, attend_out, gate_up, down_weight, norm_gains = params
    gain_row_stack = lower_precision(norm_gains)
    sequence_length = tokens_seq.shape[0]
    query_group_width = QUERY_HEADS // KEY_VALUE_HEADS
    first_normalized = lower_precision(normalize(tokens_seq, gain_row_stack[0]))
    projected_output = jnp.dot(first_normalized, lower_precision(attention_input_weight), precision=highest_precision).reshape(sequence_length, KEY_VALUE_HEADS, query_group_width + 2, HEAD_DIMENSION)
    cosine_table, sine_table = rope_tables(token_positions)
    query_row_block = lower_precision(rotate(low_back(projected_output[:, :, :query_group_width]), cosine_table[:, None, None, :], sine_table[:, None, None, :]))
    keys_all = lower_precision(rotate(low_back(projected_output[:, :, query_group_width]), cosine_table[:, None, :], sine_table[:, None, :]))
    values_all = lower_precision(low_back(projected_output[:, :, query_group_width + 1]))
    rows_per_block = min(512, sequence_length)
    number_of_blocks = sequence_length // rows_per_block
    score_scale = HEAD_DIMENSION ** (-0.5)

    def attention_block(block_inputs):
        query_block, query_pos = block_inputs
        scores = low_back(jnp.einsum('rgha,nga->ghrn', query_block, keys_all, precision=highest_precision) * score_scale)
        allowed = (token_positions[None, :] <= query_pos[:, None]) & (token_positions[None, :] < length)
        scores = jnp.where(allowed[None, None], scores, neg_big)
        weights = jax.nn.softmax(scores, axis=-1)
        return jnp.einsum('ghrn,nga->rgha', lower_precision(weights), values_all, precision=highest_precision)
    attention_output = lax.map(jax.checkpoint(attention_block), (query_row_block.reshape(number_of_blocks, rows_per_block, KEY_VALUE_HEADS, query_group_width, HEAD_DIMENSION), token_positions.reshape(number_of_blocks, rows_per_block)))
    attention_output = lower_precision(low_back(attention_output.reshape(sequence_length, QUERY_HEADS * HEAD_DIMENSION)))
    residual_stream = tokens_seq + low_back(jnp.dot(attention_output, lower_precision(attend_out), precision=highest_precision))
    second_normalized = lower_precision(normalize(residual_stream, gain_row_stack[1]))
    hidden_pair = jnp.dot(second_normalized, lower_precision(gate_up), precision=highest_precision).reshape(sequence_length, N_TP, 2, FF // N_TP)
    gate_value = low_back(hidden_pair[:, :, 0].reshape(sequence_length, FF))
    up_value = low_back(hidden_pair[:, :, 1].reshape(sequence_length, FF))
    inner_act = lower_precision(jax.nn.silu(gate_value) * up_value)
    return residual_stream + low_back(jnp.dot(inner_act, lower_precision(down_weight), precision=highest_precision))

def reference(tokens, out_cotangent, seq_lengths, span_order, attention_input_weight, attention_input_first, attention_input_squared, attend_out, attend_out_moment, attend_out_second, gate_up, gate_up_moment, gate_up_second, down_weight, down_weight_moment, down_weight_second, norm_gains, norm_gains_moment, norm_gains_second):
    params = (attention_input_weight, attend_out, gate_up, down_weight, norm_gains)
    firsts = (attention_input_first, attend_out_moment, gate_up_moment, down_weight_moment, norm_gains_moment)
    seconds = (attention_input_squared, attend_out_second, gate_up_second, down_weight_second, norm_gains_second)
    seq_count = MICRO_BATCHES * SLOTS_PER_BATCH
    span_len = SLOT_POSITIONS // (2 * N_CTX)
    within = jnp.arange(SLOT_POSITIONS, dtype=jnp.int32)
    orders = span_order.reshape(seq_count, 2 * N_CTX).astype(jnp.int32)
    token_positions = (jnp.take(orders, within // span_len, axis=1) * span_len + within % span_len).astype(jnp.int32)
    layer_inputs = tokens.reshape(seq_count, SLOT_POSITIONS, MODEL_DIMENSION).astype(jnp.float32)
    cotangents = out_cotangent.reshape(seq_count, SLOT_POSITIONS, MODEL_DIMENSION).astype(jnp.float32)
    lengths_flat = seq_lengths.reshape(seq_count).astype(jnp.int32)

    def one_sequence(totals, seq_item):
        tokens_seq, cotangent, position_row, length = seq_item
        result, pullback = jax.vjp(lambda weights, values: layer_forward(weights, values, position_row, length), params, tokens_seq)
        keep_mask = (position_row < length).astype(jnp.float32)[:, None]
        weight_grads, input_part = pullback(cotangent * keep_mask)
        totals = jax.tree.map(lambda left_sum, right_sum: left_sum + right_sum, totals, weight_grads)
        return (totals, (result.astype(jnp.bfloat16), input_part))
    zero_grads = jax.tree.map(jnp.zeros_like, params)
    totals, (results, input_parts) = lax.scan(one_sequence, zero_grads, (layer_inputs, cotangents, token_positions, lengths_flat))
    updated = [adam_update(weight, moment, second, gradient, learn_rate, decay_flag) for weight, moment, second, gradient, learn_rate, decay_flag in zip(params, firsts, seconds, totals, learn_rates, decay_flags)]
    return (results.reshape(MICRO_BATCHES, SLOTS_PER_BATCH, SLOT_POSITIONS, MODEL_DIMENSION), input_parts.reshape(MICRO_BATCHES, SLOTS_PER_BATCH, SLOT_POSITIONS, MODEL_DIMENSION), updated[0][0], updated[0][1], updated[0][2], updated[0][2].astype(jnp.bfloat16), updated[1][0], updated[1][1], updated[1][2], updated[1][2].astype(jnp.bfloat16), updated[2][0], updated[2][1], updated[2][2], updated[2][2].astype(jnp.bfloat16), updated[3][0], updated[3][1], updated[3][2], updated[3][2].astype(jnp.bfloat16), updated[4][0], updated[4][1], updated[4][2])
```

```python
import functools

import jax
import jax.numpy as jnp
from jax import lax
from jax.experimental import pallas as pl
from jax.experimental.pallas import tpu as pltpu
from jax.sharding import PartitionSpec as P

QUERY_HEADS = 32
KEY_VALUE_HEADS = 8
HEAD_DIMENSION = 80
STEP = 10
GROUP = QUERY_HEADS // KEY_VALUE_HEADS

rope_base = 1000000.0
norm_eps = 1e-05
beta_one = 0.9
beta_two = 0.95
adam_eps = 1e-08
weight_decay = 0.1
learn_rates = (0.1, 0.5, 0.05, 0.04, 0.8)
decay_flags = (1.0, 1.0, 1.0, 1.0, 0.0)
neg_big = -1e30
log2_e = 1.4426950408889634
MESH = pl.DeviceIdType.MESH
VMEM = pltpu.VMEM


def adam_update(weight, moment, second, gradient, learn_rate, decay_flag):
    moment = beta_one * moment + (1.0 - beta_one) * gradient
    second = beta_two * second + (1.0 - beta_two) * gradient * gradient
    moment_hat = moment / (1.0 - beta_one**STEP)
    second_hat = second / (1.0 - beta_two**STEP)
    weight = weight - learn_rate * (
        moment_hat / (jnp.sqrt(second_hat) + adam_eps) + decay_flag * weight_decay * weight
    )
    return (moment, second, weight)


def line_body(
    n, chunks, chunk_rows, lag, p_ref, o_ref, inbox, red_send, red_recv, back_send, back_recv
):
    z = lax.axis_index("tp")
    half = chunks * chunk_rows
    barrier = pltpu.get_barrier_semaphore()

    @pl.when(z > 0)
    def _():
        pl.semaphore_signal(barrier, inc=1, device_id={"tp": z - 1}, device_id_type=MESH)

    @pl.when(z < n - 1)
    def _():
        pl.semaphore_signal(barrier, inc=1, device_id={"tp": z + 1}, device_id_type=MESH)

    pl.semaphore_wait(barrier, (z > 0).astype(jnp.int32) + (z < n - 1).astype(jnp.int32))

    def rows_of(flow, k):
        return pl.ds(pl.multiple_of(flow * half + k * chunk_rows, chunk_rows), chunk_rows)

    def hop_of(flow):
        return (n - 1 - z) if flow == 0 else z

    def onward(flow):
        return {"tp": jnp.maximum(z - 1, 0) if flow == 0 else jnp.minimum(z + 1, n - 1)}

    def backward(flow):
        return {"tp": jnp.minimum(z + 1, n - 1) if flow == 0 else jnp.maximum(z - 1, 0)}

    def reduce_copy(flow, k, source):
        return pltpu.make_async_remote_copy(
            src_ref=source,
            dst_ref=inbox.at[rows_of(flow, k)],
            send_sem=red_send.at[flow, k],
            recv_sem=red_recv.at[flow, k],
            device_id=onward(flow),
            device_id_type=MESH,
        )

    def back_copy(flow, k):
        rows = rows_of(flow, k)
        return pltpu.make_async_remote_copy(
            src_ref=o_ref.at[rows],
            dst_ref=o_ref.at[rows],
            send_sem=back_send.at[flow, k],
            recv_sem=back_recv.at[flow, k],
            device_id=backward(flow),
            device_id_type=MESH,
        )

    def added(rows):
        return (inbox[rows, :].astype(jnp.float32) + p_ref[rows, :].astype(jnp.float32)).astype(
            jnp.bfloat16
        )

    def step(t, carry):
        for flow in (0, 1):
            hop = hop_of(flow)
            k = t - hop * lag

            @pl.when((k >= 0) & (k < chunks))
            def _():
                rows = rows_of(flow, k)

                @pl.when(hop == 0)
                def _():
                    reduce_copy(flow, k, p_ref.at[rows]).start()

                @pl.when((hop > 0) & (hop < n - 1))
                def _():
                    reduce_copy(flow, k, p_ref.at[rows]).wait_recv()
                    inbox[rows, :] = added(rows)
                    reduce_copy(flow, k, inbox.at[rows]).start()

                @pl.when(hop == n - 1)
                def _():
                    reduce_copy(flow, k, p_ref.at[rows]).wait_recv()
                    o_ref[rows, :] = added(rows)
                    back_copy(flow, k).start()

        for flow in (0, 1):
            hop = hop_of(flow)
            k2 = t - (n - 1) * lag - (n - 1 - hop) * lag

            @pl.when((k2 >= 0) & (k2 < chunks) & (hop < n - 1))
            def _():
                back_copy(flow, k2).wait_recv()

                @pl.when(hop > 0)
                def _():
                    back_copy(flow, k2).start()

        return carry

    lax.fori_loop(0, chunks + 2 * (n - 1) * lag, step, 0)

    def drain(k, carry):
        for flow in (0, 1):
            hop = hop_of(flow)

            @pl.when(hop < n - 1)
            def _():
                reduce_copy(flow, k, p_ref.at[rows_of(flow, k)]).wait_send()

            @pl.when(hop > 0)
            def _():
                back_copy(flow, k).wait_send()

        return carry

    lax.fori_loop(0, chunks, drain, 0)


def line_sum(part, n, ident, chunk_rows=16, lag=2):
    rows, width = part.shape
    chunks = rows // 2 // chunk_rows
    return pl.pallas_call(
        functools.partial(line_body, n, chunks, chunk_rows, lag),
        out_shape=jax.ShapeDtypeStruct((rows, width), jnp.bfloat16),
        in_specs=[pl.BlockSpec(memory_space=VMEM)],
        out_specs=pl.BlockSpec(memory_space=VMEM),
        scratch_shapes=[VMEM((rows, width), jnp.bfloat16)]
        + [pltpu.SemaphoreType.DMA((2, chunks))] * 4,
        compiler_params=pltpu.CompilerParams(
            collective_id=ident, has_side_effects=True, vmem_limit_bytes=48 * 2**20
        ),
        cost_estimate=pl.CostEstimate(
            flops=rows * width, bytes_accessed=80 * rows * width, transcendentals=0
        ),
        name="line_sum",
    )(part)


def greet(n):
    me = lax.axis_index("ctx")
    barrier = pltpu.get_barrier_semaphore()
    for step in range(1, n):
        pl.semaphore_signal(
            barrier, inc=1, device_id={"ctx": lax.rem(me + step, n)}, device_id_type=MESH
        )
    pl.semaphore_wait(barrier, n - 1)
    return me


def turn(first, second, cosine, sine):
    return jnp.concatenate([first * cosine - second * sine, second * cosine + first * sine], 0)


def turn_back(first, second, cosine, sine):
    return jnp.concatenate([first * cosine + second * sine, second * cosine - first * sine], 0)


def mask_bias(key_position, query_position, length):
    allowed = (key_position <= query_position) & (key_position < length)
    return jnp.where(allowed, 0.0, neg_big)


def attend_body(
    n,
    groups,
    proj_ref,
    cos_ref,
    sin_ref,
    key_pos_ref,
    query_pos_ref,
    length_ref,
    q_ref,
    kv_ref,
    full_ref,
    low_ref,
    log_ref,
    bias,
    send_sem,
    recv_sem,
):
    me = greet(n)
    seqs, _, rows = q_ref.shape
    dim = HEAD_DIMENSION
    half = dim // 2
    group_width = (GROUP + 2) * dim

    def block(m, col):
        return proj_ref[m, col : col + half, :], proj_ref[m, col + half : col + dim, :]

    def copy(m, step):
        return pltpu.make_async_remote_copy(
            src_ref=kv_ref.at[m, me],
            dst_ref=kv_ref.at[m, me],
            send_sem=send_sem.at[m, step - 1],
            recv_sem=recv_sem.at[m, step - 1],
            device_id={"ctx": lax.rem(me + step, n)},
            device_id_type=MESH,
        )

    def spread(m, carry):
        for g in range(groups):
            col = g * group_width + GROUP * dim
            kv_ref[m, me, g, :dim, :] = turn(*block(m, col), cos_ref[m], sin_ref[m]).astype(
                jnp.bfloat16
            )
            kv_ref[m, me, g, dim:, :] = proj_ref[m, col + dim : col + 2 * dim, :].astype(
                jnp.bfloat16
            )
        for step in range(1, n):
            copy(m, step).start()
        return carry

    lax.fori_loop(0, seqs, spread, 0)

    def sequence(m, carry):
        for g in range(groups):
            for h in range(GROUP):
                low = (g * GROUP + h) * dim
                q_ref[m, low : low + dim, :] = turn(
                    *block(m, g * group_width + h * dim), cos_ref[m], sin_ref[m]
                ).astype(jnp.bfloat16)
        bias[...] = mask_bias(key_pos_ref[m], query_pos_ref[m], length_ref[m])
        for step in range(1, n):
            copy(m, step).wait_recv()
        for g in range(groups):
            for h in range(GROUP):
                low = (g * GROUP + h) * dim
                query = q_ref[m, low : low + dim, :]
                scores = [
                    lax.dot_general(
                        kv_ref[m, j, g, :dim, :],
                        query,
                        (((0,), (0,)), ((), ())),
                        preferred_element_type=jnp.float32,
                    )
                    * (log2_e * dim**-0.5)
                    + bias[j * rows : (j + 1) * rows, :]
                    for j in range(n)
                ]
                top = functools.reduce(
                    jnp.maximum, [jnp.max(s, axis=0, keepdims=True) for s in scores]
                )
                total = jnp.zeros_like(top)
                out = jnp.zeros((dim, rows), jnp.float32)
                for j in range(n):
                    weights = jnp.exp2(scores[j] - top)
                    total += jnp.sum(weights, axis=0, keepdims=True)
                    out += jnp.dot(
                        kv_ref[m, j, g, dim:, :],
                        weights.astype(jnp.bfloat16),
                        preferred_element_type=jnp.float32,
                    )
                out = out / total
                full_ref[m, low : low + dim, :] = out
                low_ref[m, low : low + dim, :] = out.astype(jnp.bfloat16)
                log_ref[m, g * GROUP + h : g * GROUP + h + 1, :] = top + jnp.log2(total)
        return carry

    lax.fori_loop(0, seqs, sequence, 0)

    def drain(m, carry):
        for step in range(1, n):
            copy(m, step).wait_send()
        return carry

    lax.fori_loop(0, seqs, drain, 0)


def attend(projected, cosine, sine, key_pos, query_pos, lengths, n, ident):
    seqs, width, rows = projected.shape
    groups = width // ((GROUP + 2) * HEAD_DIMENSION)
    heads = groups * GROUP
    shape = jax.ShapeDtypeStruct
    vmem = pl.BlockSpec(memory_space=VMEM)
    return pl.pallas_call(
        functools.partial(attend_body, n, groups),
        out_shape=(
            shape((seqs, heads * HEAD_DIMENSION, rows), jnp.bfloat16),
            shape((seqs, n, groups, 2 * HEAD_DIMENSION, rows), jnp.bfloat16),
            shape((seqs, heads * HEAD_DIMENSION, rows), jnp.float32),
            shape((seqs, heads * HEAD_DIMENSION, rows), jnp.bfloat16),
            shape((seqs, heads, rows), jnp.float32),
        ),
        in_specs=[vmem] * 6,
        out_specs=(vmem,) * 5,
        scratch_shapes=[
            VMEM((n * rows, rows), jnp.float32),
            pltpu.SemaphoreType.DMA((seqs, n - 1)),
            pltpu.SemaphoreType.DMA((seqs, n - 1)),
        ],
        compiler_params=pltpu.CompilerParams(
            collective_id=ident, has_side_effects=True, vmem_limit_bytes=56 * 2**20
        ),
        name="attend",
    )(projected, cosine, sine, key_pos, query_pos, lengths)


def attend_back_body(
    n,
    groups,
    q_ref,
    kv_ref,
    full_ref,
    log_ref,
    grad_ref,
    cos_ref,
    sin_ref,
    key_pos_ref,
    query_pos_ref,
    length_ref,
    out_ref,
    bias,
    outbox,
    inbox,
    send_sem,
    recv_sem,
):
    me = greet(n)
    seqs, _, rows = q_ref.shape
    dim = HEAD_DIMENSION
    half = dim // 2
    scale = dim**-0.5
    group_width = (GROUP + 2) * dim

    def copy(m, step):
        to = lax.rem(me + step, n)
        return pltpu.make_async_remote_copy(
            src_ref=outbox.at[m, to],
            dst_ref=inbox.at[m, step - 1],
            send_sem=send_sem.at[m, step - 1],
            recv_sem=recv_sem.at[m, step - 1],
            device_id={"ctx": to},
            device_id_type=MESH,
        )

    def sequence(m, carry):
        bias[...] = mask_bias(key_pos_ref[m], query_pos_ref[m], length_ref[m])
        for g in range(groups):
            key_sums = [jnp.zeros((dim, rows), jnp.float32) for _ in range(n)]
            value_sums = [jnp.zeros((dim, rows), jnp.float32) for _ in range(n)]
            for h in range(GROUP):
                low = (g * GROUP + h) * dim
                query = q_ref[m, low : low + dim, :]
                grad = grad_ref[m, low : low + dim, :]
                delta = jnp.sum(
                    grad.astype(jnp.float32) * full_ref[m, low : low + dim, :],
                    axis=0,
                    keepdims=True,
                )
                log_total = log_ref[m, g * GROUP + h : g * GROUP + h + 1, :]
                query_sum = jnp.zeros((dim, rows), jnp.float32)
                for j in range(n):
                    keys = kv_ref[m, j, g, :dim, :]
                    values = kv_ref[m, j, g, dim:, :]
                    scores = lax.dot_general(
                        keys, query, (((0,), (0,)), ((), ())), preferred_element_type=jnp.float32
                    )
                    probs = jnp.exp2(
                        scores * (log2_e * scale)
                        + (bias[j * rows : (j + 1) * rows, :] - log_total)
                    )
                    grad_probs = lax.dot_general(
                        values, grad, (((0,), (0,)), ((), ())), preferred_element_type=jnp.float32
                    )
                    grad_scores = (probs * (grad_probs - delta)).astype(jnp.bfloat16)
                    query_sum += jnp.dot(keys, grad_scores, preferred_element_type=jnp.float32)
                    key_sums[j] += lax.dot_general(
                        query,
                        grad_scores,
                        (((1,), (1,)), ((), ())),
                        preferred_element_type=jnp.float32,
                    )
                    value_sums[j] += lax.dot_general(
                        grad,
                        probs.astype(jnp.bfloat16),
                        (((1,), (1,)), ((), ())),
                        preferred_element_type=jnp.float32,
                    )
                query_sum = query_sum * scale
                col = g * group_width + h * dim
                out_ref[m, col : col + dim, :] = turn_back(
                    query_sum[:half], query_sum[half:], cos_ref[m], sin_ref[m]
                ).astype(jnp.bfloat16)
            for j in range(n):
                outbox[m, j, g, :dim, :] = (key_sums[j] * scale).astype(jnp.bfloat16)
                outbox[m, j, g, dim:, :] = value_sums[j].astype(jnp.bfloat16)
        for step in range(1, n):
            copy(m, step).start()
        return carry

    lax.fori_loop(0, seqs, sequence, 0)

    def gather(m, carry):
        for step in range(1, n):
            copy(m, step).wait_recv()
        for g in range(groups):
            total = outbox[m, me, g].astype(jnp.float32)
            for step in range(1, n):
                total += inbox[m, step - 1, g].astype(jnp.float32)
            col = g * group_width + GROUP * dim
            out_ref[m, col : col + dim, :] = turn_back(
                total[:half], total[half:dim], cos_ref[m], sin_ref[m]
            ).astype(jnp.bfloat16)
            out_ref[m, col + dim : col + 2 * dim, :] = total[dim:].astype(jnp.bfloat16)
        for step in range(1, n):
            copy(m, step).wait_send()
        return carry

    lax.fori_loop(0, seqs, gather, 0)


def attend_back(
    queries, key_values, full, log_total, grads, cosine, sine, key_pos, query_pos, lengths, n, ident
):
    seqs, width, rows = queries.shape
    groups = key_values.shape[2]
    vmem = pl.BlockSpec(memory_space=VMEM)
    return pl.pallas_call(
        functools.partial(attend_back_body, n, groups),
        out_shape=jax.ShapeDtypeStruct(
            (seqs, groups * (GROUP + 2) * HEAD_DIMENSION, rows), jnp.bfloat16
        ),
        in_specs=[vmem] * 10,
        out_specs=vmem,
        scratch_shapes=[
            VMEM((n * rows, rows), jnp.float32),
            VMEM((seqs, n, groups, 2 * HEAD_DIMENSION, rows), jnp.bfloat16),
            VMEM((seqs, n - 1, groups, 2 * HEAD_DIMENSION, rows), jnp.bfloat16),
            pltpu.SemaphoreType.DMA((seqs, n - 1)),
            pltpu.SemaphoreType.DMA((seqs, n - 1)),
        ],
        compiler_params=pltpu.CompilerParams(
            collective_id=ident, has_side_effects=True, vmem_limit_bytes=56 * 2**20
        ),
        name="attend_back",
    )(queries, key_values, full, log_total, grads, cosine, sine, key_pos, query_pos, lengths)


def grads_body(rows_last, left_ref, right_ref, *rest):
    out_ref, turned = rest[-2:]

    @pl.when(pl.program_id(0) == 0)
    def _():
        turned[...] = left_ref[...].T

    contract = (((1,), (1 if rows_last else 0,)), ((), ()))
    width = turned.shape[0]
    part = 512 if width % 512 == 0 else width
    for low in range(0, width, part):
        out_ref[low : low + part, :] = lax.dot_general(
            turned[low : low + part, :],
            right_ref[...],
            contract,
            preferred_element_type=jnp.float32,
        ).astype(out_ref.dtype)


def grads_into(buffer, columns, first, left, right, rows_last, tile):
    rows, width = left.shape
    n = right.shape[0] if rows_last else right.shape[1]
    in_specs = [
        pl.BlockSpec(memory_space=VMEM),
        pl.BlockSpec((tile, rows), lambda i: (i, 0))
        if rows_last
        else pl.BlockSpec((rows, tile), lambda i: (0, i)),
    ]
    operands = [left, right]
    aliases = {}
    if buffer is not None:
        in_specs.append(pl.BlockSpec(memory_space=pl.ANY))
        operands.append(buffer)
        aliases = {2: 0}
    return pl.pallas_call(
        functools.partial(grads_body, rows_last),
        grid=(n // tile,),
        out_shape=jax.ShapeDtypeStruct((width, columns), jnp.bfloat16),
        in_specs=in_specs,
        out_specs=pl.BlockSpec((width, tile), lambda i: (0, first // tile + i)),
        scratch_shapes=[VMEM((width, rows), jnp.bfloat16)],
        input_output_aliases=aliases,
        compiler_params=pltpu.CompilerParams(vmem_limit_bytes=48 * 2**20),
        cost_estimate=pl.CostEstimate(
            flops=2 * rows * width * n,
            bytes_accessed=2 * (rows * width + rows * n + width * n),
            transcendentals=0,
        ),
        name="weight_grads",
    )(*operands)


def gain_body(ctx_size, x_ref, o_ref, inbox, send_sem, recv_sem):
    shards = x_ref.shape[0]
    me = lax.axis_index("fsdp") * ctx_size + lax.axis_index("ctx")

    def to(step):
        other = lax.rem(me + step, shards)
        return other, {"fsdp": other // ctx_size, "ctx": lax.rem(other, ctx_size)}

    barrier = pltpu.get_barrier_semaphore()
    for step in range(1, shards):
        pl.semaphore_signal(barrier, inc=1, device_id=to(step)[1], device_id_type=MESH)
    pl.semaphore_wait(barrier, shards - 1)

    def copy(step):
        other, where = to(step)
        return pltpu.make_async_remote_copy(
            src_ref=x_ref.at[other],
            dst_ref=inbox.at[step - 1],
            send_sem=send_sem.at[step - 1],
            recv_sem=recv_sem.at[step - 1],
            device_id=where,
            device_id_type=MESH,
        )

    for step in range(1, shards):
        copy(step).start()
    total = x_ref[me]
    for step in range(1, shards):
        copy(step).wait()
        total += inbox[step - 1]
    o_ref[...] = total


def gain_sum(partial, shards, ctx_size, ident):
    two, width = partial.shape
    own = width // shards
    padded = -(-own // 128) * 128
    pieces = jnp.pad(
        partial.reshape(two, shards, own).transpose(1, 0, 2),
        ((0, 0), (0, 8 - two), (0, padded - own)),
    )
    total = pl.pallas_call(
        functools.partial(gain_body, ctx_size),
        out_shape=jax.ShapeDtypeStruct((8, padded), jnp.float32),
        in_specs=[pl.BlockSpec(memory_space=VMEM)],
        out_specs=pl.BlockSpec(memory_space=VMEM),
        scratch_shapes=[
            VMEM((shards - 1, 8, padded), jnp.float32),
            pltpu.SemaphoreType.DMA((shards - 1,)),
            pltpu.SemaphoreType.DMA((shards - 1,)),
        ],
        compiler_params=pltpu.CompilerParams(collective_id=ident, has_side_effects=True),
        name="gain_sum",
    )(pieces)
    return total[:two, :own]


def dot(spec, left, right):
    return jnp.einsum(spec, left, right, preferred_element_type=jnp.float32)


def on_device(
    tokens,
    out_cotangent,
    seq_lengths,
    span_order,
    attention_input_weight,
    attention_input_first,
    attention_input_squared,
    attend_out,
    attend_out_moment,
    attend_out_second,
    gate_up,
    gate_up_moment,
    gate_up_second,
    down_weight,
    down_weight_moment,
    down_weight_second,
    norm_gains,
    norm_gains_moment,
    norm_gains_second,
):
    low = jnp.bfloat16
    micro_count, slot_count, row_count, model_width = tokens.shape
    seqs = micro_count * slot_count
    ctx_size = lax.axis_size("ctx")
    tp_size = lax.axis_size("tp")
    sequence_length = row_count * ctx_size
    span_len = sequence_length // (2 * ctx_size)
    hidden = down_weight.shape[0]
    out_width = attend_out.shape[0]
    in_width = attention_input_weight.shape[1]
    shards = ("fsdp", "ctx")

    first_pack = jnp.concatenate([attend_out.T, attention_input_weight], 1).astype(low)
    second_pack = jnp.concatenate([gate_up, down_weight.T], 1).astype(low)
    first_whole = lax.all_gather(first_pack, shards, axis=0, tiled=True)
    gains = lax.all_gather(norm_gains.astype(low), shards, axis=1, tiled=True).astype(jnp.float32)
    second_whole = lax.all_gather(second_pack, shards, axis=0, tiled=True)
    out_proj = first_whole[:, :out_width]
    in_proj = first_whole[:, out_width:]
    pair_proj = second_whole[:, : 2 * hidden]
    down_proj = second_whole[:, 2 * hidden :]

    orders = span_order.reshape(seqs, 2 * ctx_size)
    lengths = seq_lengths.reshape(seqs)
    within = jnp.arange(sequence_length, dtype=jnp.int32)
    block_ids = jnp.arange(2 * ctx_size, dtype=jnp.int32)
    table = jnp.where(
        block_ids[None, None, :] == (within // span_len)[None, :, None], orders[:, None, :], 0
    )
    pos_all = jnp.sum(table, -1) * span_len + within % span_len
    pos_here = lax.dynamic_slice_in_dim(pos_all, lax.axis_index("ctx") * row_count, row_count, 1)
    half_width = HEAD_DIMENSION // 2
    inverse = rope_base ** (-(jnp.arange(half_width, dtype=jnp.float32) * 2.0 / HEAD_DIMENSION))
    angles = pos_here.astype(jnp.float32)[:, None, :] * inverse[None, :, None]
    cosine, sine = jnp.cos(angles), jnp.sin(angles)
    key_pos = pos_all[:, :, None]
    query_pos = pos_here[:, None, :]
    length_row = jnp.broadcast_to(lengths[:, None, None], query_pos.shape)
    where = (cosine, sine, key_pos, query_pos, length_row)

    layer_inputs = tokens.reshape(seqs, row_count, model_width).astype(jnp.float32)
    first_root = lax.rsqrt(jnp.mean(layer_inputs * layer_inputs, -1, keepdims=True) + norm_eps)
    first_standard = layer_inputs * first_root
    first_normal = (first_standard * gains[0]).astype(low)
    projected = dot("dc,mrd->mcr", in_proj, first_normal)
    queries, key_values, attended_full, attended, log_total = attend(
        projected, *where, ctx_size, 1
    )

    def over_tp(part, ident):
        flat = part.astype(low).reshape(seqs * row_count, model_width)
        return line_sum(flat, tp_size, ident).reshape(part.shape).astype(jnp.float32)

    residual = layer_inputs + over_tp(dot("mcr,dc->mrd", attended, out_proj), 2)

    second_root = lax.rsqrt(jnp.mean(residual * residual, -1, keepdims=True) + norm_eps)
    second_standard = residual * second_root
    second_normal = (second_standard * gains[1]).astype(low)
    gate = dot("mrd,dc->mrc", second_normal, pair_proj[:, :hidden])
    up = dot("mrd,dc->mrc", second_normal, pair_proj[:, hidden:])
    sigmoid = jax.nn.sigmoid(gate)
    silu = gate * sigmoid
    inner = (silu * up).astype(low)
    keep = (pos_here < lengths[:, None]).astype(jnp.float32)[..., None]
    grad_out = out_cotangent.reshape(seqs, row_count, model_width).astype(jnp.float32) * keep
    grad_out_low = grad_out.astype(low)
    grad_inner = dot("mrd,dc->mrc", grad_out_low, down_proj)
    grad_gate = (grad_inner * up * sigmoid * (1.0 + gate * (1.0 - sigmoid))).astype(low)
    grad_up = (grad_inner * silu).astype(low)
    grad_pair = jnp.concatenate([grad_gate, grad_up], -1)
    all_rows = seqs * row_count
    pair_flat = grad_pair.reshape(all_rows, 2 * hidden)
    second_grads = grads_into(
        None, 3 * hidden, 0, second_normal.reshape(all_rows, model_width), pair_flat, False, 256
    )
    second_grads = grads_into(
        second_grads,
        3 * hidden,
        2 * hidden,
        grad_out_low.reshape(all_rows, model_width),
        inner.reshape(all_rows, hidden),
        False,
        256,
    )
    grad_pair, second_grads = lax.optimization_barrier((grad_pair, second_grads))
    second_share = lax.psum_scatter(second_grads, shards, scatter_dimension=0, tiled=True)
    grad_normal_two = over_tp(dot("mrc,dc->mrd", grad_pair, pair_proj), 3)
    second_gain = jnp.sum(grad_normal_two * second_standard, (0, 1))
    scaled = grad_normal_two * gains[1]
    grad_residual = grad_out + second_root * (
        scaled - second_standard * jnp.mean(scaled * second_standard, -1, keepdims=True)
    )
    grad_residual_low = grad_residual.astype(low)

    grad_attended = dot("dc,mrd->mcr", out_proj, grad_residual_low).astype(low)
    grad_projected = attend_back(
        queries, key_values, attended_full, log_total, grad_attended, *where, ctx_size, 4
    )
    first_grads = jnp.concatenate(
        [
            dot("mrd,mcr->dc", grad_residual_low, attended).astype(low),
            dot("mrd,mcr->dc", first_normal, grad_projected).astype(low),
        ],
        1,
    )
    grad_projected, first_grads, second_share = lax.optimization_barrier(
        (grad_projected, first_grads, second_share)
    )
    first_share = lax.psum_scatter(first_grads, shards, scatter_dimension=0, tiled=True)
    grad_normal_one = over_tp(dot("mcr,dc->mrd", grad_projected, in_proj), 5)
    first_gain = jnp.sum(grad_normal_one * first_standard, (0, 1))
    gain_share = gain_sum(
        jnp.stack([first_gain, second_gain]),
        lax.axis_size("fsdp") * ctx_size,
        ctx_size,
        7,
    )
    scaled = grad_normal_one * gains[0]
    input_grad = grad_residual + first_root * (
        scaled - first_standard * jnp.mean(scaled * first_standard, -1, keepdims=True)
    )
    mixed = (residual + over_tp(dot("mrc,dc->mrd", inner, down_proj), 6)).astype(low)

    gradients = (
        first_share[:, out_width:],
        first_share[:, :out_width].T,
        second_share[:, : 2 * hidden],
        second_share[:, 2 * hidden :].T,
        gain_share,
    )
    masters = (attention_input_weight, attend_out, gate_up, down_weight, norm_gains)
    firsts = (
        attention_input_first,
        attend_out_moment,
        gate_up_moment,
        down_weight_moment,
        norm_gains_moment,
    )
    seconds = (
        attention_input_squared,
        attend_out_second,
        gate_up_second,
        down_weight_second,
        norm_gains_second,
    )
    results = [mixed.reshape(tokens.shape), input_grad.reshape(tokens.shape)]
    for at in range(5):
        updated = adam_update(
            masters[at],
            firsts[at],
            seconds[at],
            gradients[at].astype(jnp.float32),
            learn_rates[at],
            decay_flags[at],
        )
        results.extend(updated)
        if at < 4:
            results.append(updated[2].astype(low))
    return tuple(results)


def solution(mesh):
    rows = P(None, "fsdp", "ctx", None)
    upper = P(("fsdp", "ctx"), "tp")
    lower = P("tp", ("fsdp", "ctx"))
    gain = P(None, ("fsdp", "ctx"))
    return jax.shard_map(
        on_device,
        mesh=mesh,
        in_specs=(rows, rows, P(None, "fsdp"), P(None, "fsdp", None))
        + (upper,) * 3
        + (lower,) * 3
        + (upper,) * 3
        + (lower,) * 3
        + (gain,) * 3,
        out_specs=(rows, rows)
        + (upper,) * 4
        + (lower,) * 4
        + (upper,) * 4
        + (lower,) * 4
        + (gain,) * 3,
        check_vma=False,
    )
```

```python
import functools

import jax
import jax.numpy as jnp
from jax import lax
from jax.experimental import pallas as pl
from jax.experimental.pallas import tpu as pltpu
from jax.sharding import PartitionSpec as P

QUERY_HEADS = 32
KEY_VALUE_HEADS = 8
HEAD_DIMENSION = 80
STEP = 10
GROUP = QUERY_HEADS // KEY_VALUE_HEADS

rope_base = 1000000.0
norm_eps = 1e-05
beta_one = 0.9
beta_two = 0.95
adam_eps = 1e-08
weight_decay = 0.1
learn_rates = (0.1, 0.5, 0.05, 0.04, 0.8)
decay_flags = (1.0, 1.0, 1.0, 1.0, 0.0)
neg_big = -1e30
log2_e = 1.4426950408889634
MESH = pl.DeviceIdType.MESH
VMEM = pltpu.VMEM
CHUNK = 16
LAG = 2


def adam_update(weight, moment, second, gradient, learn_rate, decay_flag):
    moment = beta_one * moment + (1.0 - beta_one) * gradient
    second = beta_two * second + (1.0 - beta_two) * gradient * gradient
    moment_hat = moment / (1.0 - beta_one**STEP)
    second_hat = second / (1.0 - beta_two**STEP)
    weight = weight - learn_rate * (
        moment_hat / (jnp.sqrt(second_hat) + adam_eps) + decay_flag * weight_decay * weight
    )
    return (moment, second, weight)


def line_greet(n, z):
    barrier = pltpu.get_barrier_semaphore()

    @pl.when(z > 0)
    def _():
        pl.semaphore_signal(barrier, inc=1, device_id={"tp": z - 1}, device_id_type=MESH)

    @pl.when(z < n - 1)
    def _():
        pl.semaphore_signal(barrier, inc=1, device_id={"tp": z + 1}, device_id_type=MESH)

    return (z > 0).astype(jnp.int32) + (z < n - 1).astype(jnp.int32)


class Line:
    def __init__(self, n, z, segments, segment_rows, parts, inbox, out, sems, finish):
        self.n, self.z = n, z
        self.segment_rows = segment_rows
        self.per_segment = segment_rows // (2 * CHUNK)
        self.chunks = segments * self.per_segment
        self.parts, self.inbox, self.out = parts, inbox, out
        self.red_send, self.red_recv, self.back_send, self.back_recv = sems
        self.finish = finish
        self.ticks = self.chunks + 2 * (n - 1) * LAG

    def ready(self, segments):
        return segments * self.per_segment + 2 * (self.n - 1) * LAG

    def rows(self, flow, g):
        start = (
            (g // self.per_segment) * self.segment_rows
            + flow * (self.segment_rows // 2)
            + (g % self.per_segment) * CHUNK
        )
        return pl.ds(pl.multiple_of(start, CHUNK), CHUNK)

    def hop(self, flow):
        return (self.n - 1 - self.z) if flow == 0 else self.z

    def neighbour(self, up):
        z = jnp.minimum(self.z + 1, self.n - 1) if up else jnp.maximum(self.z - 1, 0)
        return {"tp": z}

    def reduce_copy(self, flow, g, source):
        return pltpu.make_async_remote_copy(
            src_ref=source,
            dst_ref=self.inbox.at[self.rows(flow, g)],
            send_sem=self.red_send.at[flow, g],
            recv_sem=self.red_recv.at[flow, g],
            device_id=self.neighbour(flow == 1),
            device_id_type=MESH,
        )

    def back_copy(self, flow, g):
        rows = self.rows(flow, g)
        return pltpu.make_async_remote_copy(
            src_ref=self.out.at[rows],
            dst_ref=self.out.at[rows],
            send_sem=self.back_send.at[flow, g],
            recv_sem=self.back_recv.at[flow, g],
            device_id=self.neighbour(flow == 0),
            device_id_type=MESH,
        )

    def tick(self, t):
        n = self.n
        for flow in (0, 1):
            hop = self.hop(flow)
            g = t - hop * LAG

            @pl.when((g >= 0) & (g < self.chunks))
            def _():
                rows = self.rows(flow, g)

                @pl.when(hop == 0)
                def _():
                    self.reduce_copy(flow, g, self.parts.at[rows]).start()

                @pl.when(hop > 0)
                def _():
                    self.reduce_copy(flow, g, self.parts.at[rows]).wait_recv()
                    total = self.inbox[rows, :].astype(jnp.float32) + self.parts[rows, :].astype(
                        jnp.float32
                    )

                    @pl.when(hop < n - 1)
                    def _():
                        self.inbox[rows, :] = total.astype(jnp.bfloat16)
                        self.reduce_copy(flow, g, self.inbox.at[rows]).start()

                    @pl.when(hop == n - 1)
                    def _():
                        self.finish(g // self.per_segment, rows, total)
                        self.back_copy(flow, g).start()

        for flow in (0, 1):
            hop = self.hop(flow)
            back = t - (n - 1) * LAG - (n - 1 - hop) * LAG

            @pl.when((back >= 0) & (back < self.chunks) & (hop < n - 1))
            def _():
                self.back_copy(flow, back).wait_recv()

                @pl.when(hop > 0)
                def _():
                    self.back_copy(flow, back).start()

    def run(self, first, last):
        def step(t, carry):
            self.tick(t)
            return carry

        lax.fori_loop(first, last, step, 0)

    def drain(self):
        def step(g, carry):
            for flow in (0, 1):
                hop = self.hop(flow)

                @pl.when(hop < self.n - 1)
                def _():
                    self.reduce_copy(flow, g, self.parts.at[self.rows(flow, g)]).wait_send()

                @pl.when(hop > 0)
                def _():
                    self.back_copy(flow, g).wait_send()

            return carry

        lax.fori_loop(0, self.chunks, step, 0)


def line_scratch(rows, width, segments, segment_rows):
    chunks = segments * (segment_rows // (2 * CHUNK))
    return [VMEM((rows, width), jnp.bfloat16)] + [pltpu.SemaphoreType.DMA((2, chunks))] * 4


def line_body(n, segments, p_ref, o_ref, inbox, *sems):
    z = lax.axis_index("tp")
    pl.semaphore_wait(pltpu.get_barrier_semaphore(), line_greet(n, z))

    def finish(segment, rows, total):
        o_ref[rows, :] = total.astype(jnp.bfloat16)

    line = Line(n, z, segments, p_ref.shape[0] // segments, p_ref, inbox, o_ref, sems, finish)
    line.run(0, line.ticks)
    line.drain()


def line_cost(rows, width):
    return pl.CostEstimate(flops=rows * width, bytes_accessed=80 * rows * width, transcendentals=0)


def line_sum(part, n, segments, ident):
    rows, width = part.shape
    return pl.pallas_call(
        functools.partial(line_body, n, segments),
        out_shape=jax.ShapeDtypeStruct((rows, width), jnp.bfloat16),
        in_specs=[pl.BlockSpec(memory_space=VMEM)],
        out_specs=pl.BlockSpec(memory_space=VMEM),
        scratch_shapes=line_scratch(rows, width, segments, rows // segments),
        compiler_params=pltpu.CompilerParams(
            collective_id=ident, has_side_effects=True, vmem_limit_bytes=48 * 2**20
        ),
        cost_estimate=line_cost(rows, width),
        name="line_sum",
    )(part)


def mean_of(values):
    return jnp.mean(values, axis=-1, keepdims=True)


def norm_back(total, values, gain, gain_sums):
    root = lax.rsqrt(mean_of(values * values) + norm_eps)
    standard = values * root
    terms = total * standard
    gain_sums[...] += functools.reduce(
        lambda a, b: a + b, [terms[low : low + 8] for low in range(0, CHUNK, 8)]
    )
    scaled = total * gain
    return root * (scaled - standard * mean_of(scaled * standard))


def greet(n):
    me = lax.axis_index("ctx")
    barrier = pltpu.get_barrier_semaphore()
    for step in range(1, n):
        pl.semaphore_signal(
            barrier, inc=1, device_id={"ctx": lax.rem(me + step, n)}, device_id_type=MESH
        )
    pl.semaphore_wait(barrier, n - 1)
    return me


def turn(first, second, cosine, sine):
    return jnp.concatenate([first * cosine - second * sine, second * cosine + first * sine], 0)


def turn_back(first, second, cosine, sine):
    return jnp.concatenate([first * cosine + second * sine, second * cosine - first * sine], 0)


def mask_bias(key_position, query_position, length):
    allowed = (key_position <= query_position) & (key_position < length)
    return jnp.where(allowed, 0.0, neg_big)


def attend_body(
    n,
    groups,
    proj_ref,
    cos_ref,
    sin_ref,
    key_pos_ref,
    query_pos_ref,
    length_ref,
    q_ref,
    kv_ref,
    full_ref,
    low_ref,
    log_ref,
    bias,
    send_sem,
    recv_sem,
):
    me = greet(n)
    seqs, _, rows = q_ref.shape
    dim = HEAD_DIMENSION
    half = dim // 2
    group_width = (GROUP + 2) * dim

    def block(m, col):
        return proj_ref[m, col : col + half, :], proj_ref[m, col + half : col + dim, :]

    def copy(m, step):
        return pltpu.make_async_remote_copy(
            src_ref=kv_ref.at[m, me],
            dst_ref=kv_ref.at[m, me],
            send_sem=send_sem.at[m, step - 1],
            recv_sem=recv_sem.at[m, step - 1],
            device_id={"ctx": lax.rem(me + step, n)},
            device_id_type=MESH,
        )

    def spread(m, carry):
        for g in range(groups):
            col = g * group_width + GROUP * dim
            kv_ref[m, me, g, :dim, :] = turn(*block(m, col), cos_ref[m], sin_ref[m]).astype(
                jnp.bfloat16
            )
            kv_ref[m, me, g, dim:, :] = proj_ref[m, col + dim : col + 2 * dim, :].astype(
                jnp.bfloat16
            )
        for step in range(1, n):
            copy(m, step).start()
        return carry

    lax.fori_loop(0, seqs, spread, 0)

    def sequence(m, carry):
        for g in range(groups):
            for h in range(GROUP):
                low = (g * GROUP + h) * dim
                q_ref[m, low : low + dim, :] = turn(
                    *block(m, g * group_width + h * dim), cos_ref[m], sin_ref[m]
                ).astype(jnp.bfloat16)
        bias[...] = mask_bias(key_pos_ref[m], query_pos_ref[m], length_ref[m])
        for step in range(1, n):
            copy(m, step).wait_recv()
        for g in range(groups):
            for h in range(GROUP):
                low = (g * GROUP + h) * dim
                query = q_ref[m, low : low + dim, :]
                scores = [
                    lax.dot_general(
                        kv_ref[m, j, g, :dim, :],
                        query,
                        (((0,), (0,)), ((), ())),
                        preferred_element_type=jnp.float32,
                    )
                    * (log2_e * dim**-0.5)
                    + bias[j * rows : (j + 1) * rows, :]
                    for j in range(n)
                ]
                top = functools.reduce(
                    jnp.maximum, [jnp.max(s, axis=0, keepdims=True) for s in scores]
                )
                total = jnp.zeros_like(top)
                out = jnp.zeros((dim, rows), jnp.float32)
                for j in range(n):
                    weights = jnp.exp2(scores[j] - top)
                    total += jnp.sum(weights, axis=0, keepdims=True)
                    out += jnp.dot(
                        kv_ref[m, j, g, dim:, :],
                        weights.astype(jnp.bfloat16),
                        preferred_element_type=jnp.float32,
                    )
                out = out / total
                full_ref[m, low : low + dim, :] = out
                low_ref[low : low + dim, pl.ds(pl.multiple_of(m * rows, 128), rows)] = out.astype(
                    jnp.bfloat16
                )
                log_ref[m, g * GROUP + h : g * GROUP + h + 1, :] = top + jnp.log2(total)
        return carry

    lax.fori_loop(0, seqs, sequence, 0)

    def drain(m, carry):
        for step in range(1, n):
            copy(m, step).wait_send()
        return carry

    lax.fori_loop(0, seqs, drain, 0)


def attend(projected, cosine, sine, key_pos, query_pos, lengths, n, ident):
    seqs, width, rows = projected.shape
    groups = width // ((GROUP + 2) * HEAD_DIMENSION)
    heads = groups * GROUP
    shape = jax.ShapeDtypeStruct
    vmem = pl.BlockSpec(memory_space=VMEM)
    return pl.pallas_call(
        functools.partial(attend_body, n, groups),
        out_shape=(
            shape((seqs, heads * HEAD_DIMENSION, rows), jnp.bfloat16),
            shape((seqs, n, groups, 2 * HEAD_DIMENSION, rows), jnp.bfloat16),
            shape((seqs, heads * HEAD_DIMENSION, rows), jnp.float32),
            shape((heads * HEAD_DIMENSION, seqs * rows), jnp.bfloat16),
            shape((seqs, heads, rows), jnp.float32),
        ),
        in_specs=[vmem] * 6,
        out_specs=(vmem,) * 5,
        scratch_shapes=[
            VMEM((n * rows, rows), jnp.float32),
            pltpu.SemaphoreType.DMA((seqs, n - 1)),
            pltpu.SemaphoreType.DMA((seqs, n - 1)),
        ],
        compiler_params=pltpu.CompilerParams(
            collective_id=ident, has_side_effects=True, vmem_limit_bytes=56 * 2**20
        ),
        name="attend",
    )(projected, cosine, sine, key_pos, query_pos, lengths)


def back_one_body(
    n,
    tp,
    groups,
    normal_ref,
    mixed_ref,
    residual_ref,
    grad_out_ref,
    gain_ref,
    weight_ref,
    q_ref,
    kv_ref,
    full_ref,
    log_ref,
    cos_ref,
    sin_ref,
    key_pos_ref,
    query_pos_ref,
    length_ref,
    out_ref,
    proj_ref,
    gain_sums,
    parts,
    out_proj,
    grads,
    sums,
    bias,
    outbox,
    kv_inbox,
    load_sem,
    send_sem,
    recv_sem,
    inbox,
    *sems,
):
    z = lax.axis_index("tp")
    me = lax.axis_index("ctx")
    seqs, _, rows = q_ref.shape
    all_rows = seqs * rows
    loads = [
        pltpu.make_async_copy(normal_ref, parts.at[pl.ds(0, all_rows)], load_sem.at[0]),
        pltpu.make_async_copy(mixed_ref, parts.at[pl.ds(all_rows, all_rows)], load_sem.at[1]),
        pltpu.make_async_copy(
            weight_ref.at[:, pl.ds(0, out_proj.shape[1])], out_proj, load_sem.at[2]
        ),
    ]
    for load in loads:
        load.start()
    peers = line_greet(tp, z)
    barrier = pltpu.get_barrier_semaphore()
    for step in range(1, n):
        pl.semaphore_signal(
            barrier, inc=1, device_id={"ctx": lax.rem(me + step, n)}, device_id_type=MESH
        )
    pl.semaphore_wait(barrier, peers + n - 1)

    dim = HEAD_DIMENSION
    half = dim // 2
    scale = dim**-0.5
    group_width = (GROUP + 2) * dim
    heads = groups * GROUP
    gain_sums[...] = jnp.zeros_like(gain_sums)

    def finish(segment, at, total):
        @pl.when(segment < seqs)
        def _():
            grad = norm_back(total, residual_ref[at, :], gain_ref[1:2, :], gain_sums)
            out_ref[at, :] = (grad_out_ref[at, :].astype(jnp.float32) + grad).astype(jnp.bfloat16)

        @pl.when(segment >= seqs)
        def _():
            start = pl.multiple_of(at.start - all_rows, CHUNK)
            out_ref[at, :] = (residual_ref[pl.ds(start, CHUNK), :] + total).astype(jnp.bfloat16)

    line = Line(tp, z, 2 * seqs, rows, parts, inbox, out_ref, sems, finish)

    def copy(m, step):
        to = lax.rem(me + step, n)
        return pltpu.make_async_remote_copy(
            src_ref=outbox.at[m, to],
            dst_ref=kv_inbox.at[m, step - 1],
            send_sem=send_sem.at[m, step - 1],
            recv_sem=recv_sem.at[m, step - 1],
            device_id={"ctx": to},
            device_id_type=MESH,
        )

    def columns(m):
        return pl.ds(pl.multiple_of(m * rows, 128), rows)

    def attended_grads(m):
        grads[...] = (
            jnp.dot(
                out_ref[pl.ds(pl.multiple_of(m * rows, CHUNK), rows), :],
                out_proj[...],
                preferred_element_type=jnp.float32,
            )
            .T.astype(jnp.bfloat16)
        )
        bias[...] = mask_bias(key_pos_ref[m], query_pos_ref[m], length_ref[m])

    def head(m, at):
        g = at // GROUP
        h = at % GROUP
        low = pl.ds(pl.multiple_of(at * dim, 16), dim)
        query = q_ref[m, low, :]
        grad = grads[low, :]
        delta = jnp.sum(
            grad.astype(jnp.float32) * full_ref[m, low, :], axis=0, keepdims=True
        )
        log_total = log_ref[m, at]
        query_sum = jnp.zeros((dim, rows), jnp.float32)

        @pl.when(h == 0)
        def _():
            sums[...] = jnp.zeros_like(sums)

        for j in range(n):
            keys = kv_ref[m, j, g, :dim, :]
            values = kv_ref[m, j, g, dim:, :]
            scores = lax.dot_general(
                keys, query, (((0,), (0,)), ((), ())), preferred_element_type=jnp.float32
            )
            probs = jnp.exp2(
                scores * (log2_e * scale) + (bias[j * rows : (j + 1) * rows, :] - log_total)
            )
            grad_probs = lax.dot_general(
                values, grad, (((0,), (0,)), ((), ())), preferred_element_type=jnp.float32
            )
            grad_scores = (probs * (grad_probs - delta)).astype(jnp.bfloat16)
            query_sum += jnp.dot(keys, grad_scores, preferred_element_type=jnp.float32)
            sums[j, :dim, :] += lax.dot_general(
                query, grad_scores, (((1,), (1,)), ((), ())), preferred_element_type=jnp.float32
            )
            sums[j, dim:, :] += lax.dot_general(
                grad,
                probs.astype(jnp.bfloat16),
                (((1,), (1,)), ((), ())),
                preferred_element_type=jnp.float32,
            )
        query_sum = query_sum * scale
        col = pl.ds(pl.multiple_of(g * group_width + h * dim, 16), dim)
        proj_ref[col, columns(m)] = turn_back(
            query_sum[:half], query_sum[half:], cos_ref[m], sin_ref[m]
        ).astype(jnp.bfloat16)

        @pl.when(h == GROUP - 1)
        def _():
            for j in range(n):
                outbox[m, j, g, :dim, :] = (sums[j, :dim, :] * scale).astype(jnp.bfloat16)
                outbox[m, j, g, dim:, :] = sums[j, dim:, :].astype(jnp.bfloat16)

    def gather(m):
        for step in range(1, n):
            copy(m, step).wait_recv()
        for g in range(groups):
            total = outbox[m, me, g].astype(jnp.float32)
            for step in range(1, n):
                total += kv_inbox[m, step - 1, g].astype(jnp.float32)
            col = g * group_width + GROUP * dim
            proj_ref[col : col + dim, columns(m)] = turn_back(
                total[:half], total[half:dim], cos_ref[m], sin_ref[m]
            ).astype(jnp.bfloat16)
            proj_ref[col + dim : col + 2 * dim, columns(m)] = total[dim:].astype(jnp.bfloat16)
        for step in range(1, n):
            copy(m, step).wait_send()

    loads[0].wait()
    line.run(0, line.ready(1))
    loads[1].wait()
    loads[2].wait()

    def sequence(m, carry):
        first = line.ready(1) + m * (heads + 1)
        line.tick(first)
        attended_grads(m)

        def item(at, inner):
            line.tick(first + 1 + at)
            head(m, at)
            return inner

        lax.fori_loop(0, heads, item, 0)
        for step in range(1, n):
            copy(m, step).start()
        return carry

    lax.fori_loop(0, seqs, sequence, 0)
    line.run(line.ready(1) + seqs * (heads + 1), line.ticks)

    def collect(m, carry):
        gather(m)
        return carry

    lax.fori_loop(0, seqs, collect, 0)
    line.drain()


def back_one(
    normal_part,
    mixed_part,
    residual,
    grad_out,
    gains,
    first_whole,
    queries,
    key_values,
    full,
    log_total,
    where,
    n,
    tp,
    ident,
):
    seqs, width, rows = queries.shape
    groups = key_values.shape[2]
    all_rows, model_width = normal_part.shape
    vmem = pl.BlockSpec(memory_space=VMEM)
    hbm = pl.BlockSpec(memory_space=pl.ANY)
    shape = jax.ShapeDtypeStruct
    return pl.pallas_call(
        functools.partial(back_one_body, n, tp, groups),
        out_shape=(
            shape((2 * all_rows, model_width), jnp.bfloat16),
            shape((groups * (GROUP + 2) * HEAD_DIMENSION, all_rows), jnp.bfloat16),
            shape((8, model_width), jnp.float32),
        ),
        in_specs=[hbm, hbm, vmem, vmem, vmem, hbm] + [vmem] * 9,
        out_specs=(vmem,) * 3,
        scratch_shapes=[
            VMEM((2 * all_rows, model_width), jnp.bfloat16),
            VMEM((model_width, width), jnp.bfloat16),
            VMEM((width, rows), jnp.bfloat16),
            VMEM((n, 2 * HEAD_DIMENSION, rows), jnp.float32),
            VMEM((n * rows, rows), jnp.float32),
            VMEM((seqs, n, groups, 2 * HEAD_DIMENSION, rows), jnp.bfloat16),
            VMEM((seqs, n - 1, groups, 2 * HEAD_DIMENSION, rows), jnp.bfloat16),
            pltpu.SemaphoreType.DMA((3,)),
            pltpu.SemaphoreType.DMA((seqs, n - 1)),
            pltpu.SemaphoreType.DMA((seqs, n - 1)),
        ]
        + line_scratch(2 * all_rows, model_width, 2 * seqs, rows),
        compiler_params=pltpu.CompilerParams(
            collective_id=ident, has_side_effects=True, vmem_limit_bytes=60 * 2**20
        ),
        cost_estimate=line_cost(2 * all_rows, model_width),
        name="back_one",
    )(
        normal_part,
        mixed_part,
        residual,
        grad_out,
        gains,
        first_whole,
        queries,
        key_values,
        full,
        log_total,
        *where,
    )


def back_two_body(
    tp,
    seqs,
    proj_ref,
    weight_ref,
    token_ref,
    residual_grad_ref,
    gain_ref,
    out_ref,
    gain_sums,
    parts,
    inbox,
    *sems,
):
    z = lax.axis_index("tp")
    pl.semaphore_wait(pltpu.get_barrier_semaphore(), line_greet(tp, z))
    gain_sums[...] = jnp.zeros_like(gain_sums)
    rows = token_ref.shape[0] // seqs
    skip = weight_ref.shape[1] - proj_ref.shape[0]
    width = weight_ref.shape[0]
    tile = 512 if width % 512 == 0 else width

    def finish(segment, at, total):
        values = token_ref[at, :].astype(jnp.float32)
        grad = norm_back(total, values, gain_ref[0:1, :], gain_sums)
        out_ref[at, :] = (residual_grad_ref[at, :].astype(jnp.float32) + grad).astype(jnp.bfloat16)

    line = Line(tp, z, seqs, rows, parts, inbox, out_ref, sems, finish)

    def product(m):
        left = proj_ref[:, m * rows : (m + 1) * rows].T
        for low in range(0, width, tile):
            parts[m * rows : (m + 1) * rows, low : low + tile] = lax.dot_general(
                left,
                weight_ref[low : low + tile, skip:],
                (((1,), (1,)), ((), ())),
                preferred_element_type=jnp.float32,
            ).astype(jnp.bfloat16)

    for m in range(seqs):
        product(m)
        line.run(2 * m, 2 * m + 2)
    line.run(2 * seqs, line.ticks)
    line.drain()


def back_two(projected, first_whole, tokens, residual_grad, gains, seqs, tp, ident):
    rows, width = tokens.shape
    vmem = pl.BlockSpec(memory_space=VMEM)
    shape = jax.ShapeDtypeStruct
    return pl.pallas_call(
        functools.partial(back_two_body, tp, seqs),
        out_shape=(shape((rows, width), jnp.bfloat16), shape((8, width), jnp.float32)),
        in_specs=[vmem] * 5,
        out_specs=(vmem,) * 2,
        scratch_shapes=[VMEM((rows, width), jnp.bfloat16)]
        + line_scratch(rows, width, seqs, rows // seqs),
        compiler_params=pltpu.CompilerParams(
            collective_id=ident, has_side_effects=True, vmem_limit_bytes=56 * 2**20
        ),
        cost_estimate=line_cost(rows, width),
        name="back_two",
    )(projected, first_whole, tokens, residual_grad, gains)


def grads_body(rows_last, left_ref, right_ref, *rest):
    out_ref, turned = rest[-2:]

    @pl.when(pl.program_id(0) == 0)
    def _():
        turned[...] = left_ref[...].T

    contract = (((1,), (1 if rows_last else 0,)), ((), ()))
    width = turned.shape[0]
    part = 512 if width % 512 == 0 else width
    for low in range(0, width, part):
        out_ref[low : low + part, :] = lax.dot_general(
            turned[low : low + part, :],
            right_ref[...],
            contract,
            preferred_element_type=jnp.float32,
        ).astype(out_ref.dtype)


def grads_into(buffer, columns, first, left, right, rows_last, tile):
    rows, width = left.shape
    n = right.shape[0] if rows_last else right.shape[1]
    in_specs = [
        pl.BlockSpec(memory_space=VMEM),
        pl.BlockSpec((tile, rows), lambda i: (i, 0))
        if rows_last
        else pl.BlockSpec((rows, tile), lambda i: (0, i)),
    ]
    operands = [left, right]
    aliases = {}
    if buffer is not None:
        in_specs.append(pl.BlockSpec(memory_space=pl.ANY))
        operands.append(buffer)
        aliases = {2: 0}
    return pl.pallas_call(
        functools.partial(grads_body, rows_last),
        grid=(n // tile,),
        out_shape=jax.ShapeDtypeStruct((width, columns), jnp.bfloat16),
        in_specs=in_specs,
        out_specs=pl.BlockSpec((width, tile), lambda i: (0, first // tile + i)),
        scratch_shapes=[VMEM((width, rows), jnp.bfloat16)],
        input_output_aliases=aliases,
        compiler_params=pltpu.CompilerParams(vmem_limit_bytes=48 * 2**20),
        cost_estimate=pl.CostEstimate(
            flops=2 * rows * width * n,
            bytes_accessed=2 * (rows * width + rows * n + width * n),
            transcendentals=0,
        ),
        name="weight_grads",
    )(*operands)


def first_grads_body(normal_ref, proj_ref, residual_ref, attended_ref, out_ref):
    width = out_ref.shape[0]
    split = attended_ref.shape[0]
    tile = 512 if width % 512 == 0 else width
    contract = (((1,), (1,)), ((), ()))
    for low in range(0, width, tile):
        out_ref[low : low + tile, :split] = lax.dot_general(
            residual_ref[:, low : low + tile].T,
            attended_ref[...],
            contract,
            preferred_element_type=jnp.float32,
        ).astype(jnp.bfloat16)
        out_ref[low : low + tile, split:] = lax.dot_general(
            normal_ref[:, low : low + tile].T,
            proj_ref[...],
            contract,
            preferred_element_type=jnp.float32,
        ).astype(jnp.bfloat16)


def first_grads_of(normal, projected, residual_grad, attended):
    rows, width = normal.shape
    columns = projected.shape[0] + attended.shape[0]
    vmem = pl.BlockSpec(memory_space=VMEM)
    return pl.pallas_call(
        first_grads_body,
        out_shape=jax.ShapeDtypeStruct((width, columns), jnp.bfloat16),
        in_specs=[vmem] * 4,
        out_specs=vmem,
        compiler_params=pltpu.CompilerParams(vmem_limit_bytes=48 * 2**20),
        cost_estimate=pl.CostEstimate(
            flops=2 * rows * width * columns,
            bytes_accessed=2 * (2 * rows * width + (rows + width) * columns),
            transcendentals=0,
        ),
        name="first_grads",
    )(normal, projected, residual_grad, attended)


def gain_body(ctx_size, tp, x_ref, o_ref, inbox, tp_inbox, send_sem, recv_sem, tp_send, tp_recv):
    shards = x_ref.shape[0]
    me = lax.axis_index("fsdp") * ctx_size + lax.axis_index("ctx")
    z = lax.axis_index("tp")

    def to(step):
        other = lax.rem(me + step, shards)
        return other, {"fsdp": other // ctx_size, "ctx": lax.rem(other, ctx_size)}

    barrier = pltpu.get_barrier_semaphore()
    for step in range(1, shards):
        pl.semaphore_signal(barrier, inc=1, device_id=to(step)[1], device_id_type=MESH)
    for step in range(1, tp):
        pl.semaphore_signal(
            barrier, inc=1, device_id={"tp": lax.rem(z + step, tp)}, device_id_type=MESH
        )
    pl.semaphore_wait(barrier, shards - 1 + tp - 1)

    def copy(step):
        other, where = to(step)
        return pltpu.make_async_remote_copy(
            src_ref=x_ref.at[other],
            dst_ref=inbox.at[step - 1],
            send_sem=send_sem.at[step - 1],
            recv_sem=recv_sem.at[step - 1],
            device_id=where,
            device_id_type=MESH,
        )

    def tp_copy(step):
        return pltpu.make_async_remote_copy(
            src_ref=tp_inbox.at[0],
            dst_ref=tp_inbox.at[step],
            send_sem=tp_send.at[step - 1],
            recv_sem=tp_recv.at[step - 1],
            device_id={"tp": lax.rem(z + step, tp)},
            device_id_type=MESH,
        )

    for step in range(1, shards):
        copy(step).start()
    total = x_ref[me]
    for step in range(1, shards):
        copy(step).wait()
        total += inbox[step - 1]
    tp_inbox[0] = total
    for step in range(1, tp):
        tp_copy(step).start()
    for step in range(1, tp):
        tp_copy(step).wait()
        total += tp_inbox[step]
    o_ref[...] = total


def gain_sum(partial, shards, ctx_size, tp, ident):
    two, width = partial.shape
    own = width // shards
    padded = -(-own // 128) * 128
    pieces = jnp.pad(
        partial.reshape(two, shards, own).transpose(1, 0, 2),
        ((0, 0), (0, 8 - two), (0, padded - own)),
    )
    total = pl.pallas_call(
        functools.partial(gain_body, ctx_size, tp),
        out_shape=jax.ShapeDtypeStruct((8, padded), jnp.float32),
        in_specs=[pl.BlockSpec(memory_space=VMEM)],
        out_specs=pl.BlockSpec(memory_space=VMEM),
        scratch_shapes=[
            VMEM((shards - 1, 8, padded), jnp.float32),
            VMEM((tp, 8, padded), jnp.float32),
            pltpu.SemaphoreType.DMA((shards - 1,)),
            pltpu.SemaphoreType.DMA((shards - 1,)),
            pltpu.SemaphoreType.DMA((tp - 1,)),
            pltpu.SemaphoreType.DMA((tp - 1,)),
        ],
        compiler_params=pltpu.CompilerParams(collective_id=ident, has_side_effects=True),
        name="gain_sum",
    )(pieces)
    return total[:two, :own]


def dot(spec, left, right):
    return jnp.einsum(spec, left, right, preferred_element_type=jnp.float32)


def on_device(
    tokens,
    out_cotangent,
    seq_lengths,
    span_order,
    attention_input_weight,
    attention_input_first,
    attention_input_squared,
    attend_out,
    attend_out_moment,
    attend_out_second,
    gate_up,
    gate_up_moment,
    gate_up_second,
    down_weight,
    down_weight_moment,
    down_weight_second,
    norm_gains,
    norm_gains_moment,
    norm_gains_second,
):
    low = jnp.bfloat16
    micro_count, slot_count, row_count, model_width = tokens.shape
    seqs = micro_count * slot_count
    ctx_size = lax.axis_size("ctx")
    tp_size = lax.axis_size("tp")
    sequence_length = row_count * ctx_size
    span_len = sequence_length // (2 * ctx_size)
    hidden = down_weight.shape[0]
    out_width = attend_out.shape[0]
    in_width = attention_input_weight.shape[1]
    shards = ("fsdp", "ctx")

    first_pack = jnp.concatenate([attend_out.T, attention_input_weight], 1).astype(low)
    second_pack = jnp.concatenate([gate_up, down_weight.T], 1).astype(low)
    first_whole = lax.all_gather(first_pack, shards, axis=0, tiled=True)
    gains = lax.all_gather(norm_gains.astype(low), shards, axis=1, tiled=True).astype(jnp.float32)
    second_whole = lax.all_gather(second_pack, shards, axis=0, tiled=True)
    out_proj = first_whole[:, :out_width]
    in_proj = first_whole[:, out_width:]
    pair_proj = second_whole[:, : 2 * hidden]
    down_proj = second_whole[:, 2 * hidden :]

    orders = span_order.reshape(seqs, 2 * ctx_size)
    lengths = seq_lengths.reshape(seqs)
    within = jnp.arange(sequence_length, dtype=jnp.int32)
    block_ids = jnp.arange(2 * ctx_size, dtype=jnp.int32)
    table = jnp.where(
        block_ids[None, None, :] == (within // span_len)[None, :, None], orders[:, None, :], 0
    )
    pos_all = jnp.sum(table, -1) * span_len + within % span_len
    pos_here = lax.dynamic_slice_in_dim(pos_all, lax.axis_index("ctx") * row_count, row_count, 1)
    half_width = HEAD_DIMENSION // 2
    inverse = rope_base ** (-(jnp.arange(half_width, dtype=jnp.float32) * 2.0 / HEAD_DIMENSION))
    angles = pos_here.astype(jnp.float32)[:, None, :] * inverse[None, :, None]
    cosine, sine = jnp.cos(angles), jnp.sin(angles)
    key_pos = pos_all[:, :, None]
    query_pos = pos_here[:, None, :]
    length_row = jnp.broadcast_to(lengths[:, None, None], query_pos.shape)
    where = (cosine, sine, key_pos, query_pos, length_row)

    layer_inputs = tokens.reshape(seqs, row_count, model_width).astype(jnp.float32)
    first_root = lax.rsqrt(jnp.mean(layer_inputs * layer_inputs, -1, keepdims=True) + norm_eps)
    first_standard = layer_inputs * first_root
    first_normal = (first_standard * gains[0]).astype(low)
    projected = dot("dc,mrd->mcr", in_proj, first_normal)
    queries, key_values, attended_full, attended, log_total = attend(
        projected, *where, ctx_size, 1
    )

    all_rows = seqs * row_count

    def over_tp(part, ident):
        flat = part.astype(low).reshape(all_rows, model_width)
        return line_sum(flat, tp_size, seqs, ident).reshape(part.shape).astype(jnp.float32)

    residual = layer_inputs + over_tp(
        dot("cr,dc->rd", attended, out_proj).reshape(layer_inputs.shape), 2
    )

    second_root = lax.rsqrt(jnp.mean(residual * residual, -1, keepdims=True) + norm_eps)
    second_standard = residual * second_root
    second_normal = (second_standard * gains[1]).astype(low)
    gate = dot("mrd,dc->mrc", second_normal, pair_proj[:, :hidden])
    up = dot("mrd,dc->mrc", second_normal, pair_proj[:, hidden:])
    sigmoid = jax.nn.sigmoid(gate)
    silu = gate * sigmoid
    inner = (silu * up).astype(low)
    keep = (pos_here < lengths[:, None]).astype(jnp.float32)[..., None]
    grad_out = out_cotangent.reshape(seqs, row_count, model_width).astype(jnp.float32) * keep
    grad_out_low = grad_out.astype(low)
    grad_inner = dot("mrd,dc->mrc", grad_out_low, down_proj)
    grad_gate = (grad_inner * up * sigmoid * (1.0 + gate * (1.0 - sigmoid))).astype(low)
    grad_up = (grad_inner * silu).astype(low)
    grad_pair = jnp.concatenate([grad_gate, grad_up], -1)
    pair_flat = grad_pair.reshape(all_rows, 2 * hidden)
    second_grads = grads_into(
        None, 3 * hidden, 0, second_normal.reshape(all_rows, model_width), pair_flat, False, 256
    )
    second_grads = grads_into(
        second_grads,
        3 * hidden,
        2 * hidden,
        grad_out_low.reshape(all_rows, model_width),
        inner.reshape(all_rows, hidden),
        False,
        256,
    )
    grad_pair, second_grads = lax.optimization_barrier((grad_pair, second_grads))
    second_share = lax.psum_scatter(second_grads, shards, scatter_dimension=0, tiled=True)
    normal_part = dot("mrc,dc->mrd", grad_pair, pair_proj).astype(low)
    mixed_part = dot("mrc,dc->mrd", inner, down_proj).astype(low)

    back, grad_projected, second_gain = back_one(
        normal_part.reshape(all_rows, model_width),
        mixed_part.reshape(all_rows, model_width),
        residual.reshape(all_rows, model_width),
        grad_out_low.reshape(all_rows, model_width),
        gains,
        first_whole,
        queries,
        key_values,
        attended_full,
        log_total[:, :, None, :],
        where,
        ctx_size,
        tp_size,
        4,
    )
    grad_residual_low = back[:all_rows]
    mixed = back[all_rows:]
    first_grads = first_grads_of(
        first_normal.reshape(all_rows, model_width), grad_projected, grad_residual_low, attended
    )
    grad_projected, first_grads, second_share = lax.optimization_barrier(
        (grad_projected, first_grads, second_share)
    )
    first_share = lax.psum_scatter(first_grads, shards, scatter_dimension=0, tiled=True)
    input_grad, first_gain = back_two(
        grad_projected,
        first_whole,
        tokens.reshape(all_rows, model_width),
        grad_residual_low,
        gains,
        seqs,
        tp_size,
        5,
    )
    gain_share = gain_sum(
        jnp.stack([first_gain.sum(0), second_gain.sum(0)]),
        lax.axis_size("fsdp") * ctx_size,
        ctx_size,
        tp_size,
        7,
    )

    gradients = (
        first_share[:, out_width:],
        first_share[:, :out_width].T,
        second_share[:, : 2 * hidden],
        second_share[:, 2 * hidden :].T,
        gain_share,
    )
    masters = (attention_input_weight, attend_out, gate_up, down_weight, norm_gains)
    firsts = (
        attention_input_first,
        attend_out_moment,
        gate_up_moment,
        down_weight_moment,
        norm_gains_moment,
    )
    seconds = (
        attention_input_squared,
        attend_out_second,
        gate_up_second,
        down_weight_second,
        norm_gains_second,
    )
    results = [mixed.reshape(tokens.shape), input_grad.reshape(tokens.shape).astype(jnp.float32)]
    for at in range(5):
        updated = adam_update(
            masters[at],
            firsts[at],
            seconds[at],
            gradients[at].astype(jnp.float32),
            learn_rates[at],
            decay_flags[at],
        )
        results.extend(updated)
        if at < 4:
            results.append(updated[2].astype(low))
    return tuple(results)


def solution(mesh):
    rows = P(None, "fsdp", "ctx", None)
    upper = P(("fsdp", "ctx"), "tp")
    lower = P("tp", ("fsdp", "ctx"))
    gain = P(None, ("fsdp", "ctx"))
    return jax.shard_map(
        on_device,
        mesh=mesh,
        in_specs=(rows, rows, P(None, "fsdp"), P(None, "fsdp", None))
        + (upper,) * 3
        + (lower,) * 3
        + (upper,) * 3
        + (lower,) * 3
        + (gain,) * 3,
        out_specs=(rows, rows)
        + (upper,) * 4
        + (lower,) * 4
        + (upper,) * 4
        + (lower,) * 4
        + (gain,) * 3,
        check_vma=False,
    )
```

```python
import functools

import jax
import jax.numpy as jnp
from jax import lax
from jax.experimental import pallas as pl
from jax.experimental.pallas import tpu as pltpu
from jax.sharding import PartitionSpec as P

QUERY_HEADS = 32
KEY_VALUE_HEADS = 8
HEAD_DIMENSION = 80
STEP = 10
GROUP = QUERY_HEADS // KEY_VALUE_HEADS

rope_base = 1000000.0
norm_eps = 1e-05
beta_one = 0.9
beta_two = 0.95
adam_eps = 1e-08
weight_decay = 0.1
learn_rates = (0.1, 0.5, 0.05, 0.04, 0.8)
decay_flags = (1.0, 1.0, 1.0, 1.0, 0.0)
neg_big = -1e30
log2_e = 1.4426950408889634
MESH = pl.DeviceIdType.MESH
VMEM = pltpu.VMEM
CHUNK = 16
LAG = 2


def adam_update(weight, moment, second, gradient, learn_rate, decay_flag):
    moment = beta_one * moment + (1.0 - beta_one) * gradient
    second = beta_two * second + (1.0 - beta_two) * gradient * gradient
    moment_hat = moment / (1.0 - beta_one**STEP)
    second_hat = second / (1.0 - beta_two**STEP)
    weight = weight - learn_rate * (
        moment_hat / (jnp.sqrt(second_hat) + adam_eps) + decay_flag * weight_decay * weight
    )
    return (moment, second, weight)


def line_greet(n, z):
    barrier = pltpu.get_barrier_semaphore()

    @pl.when(z > 0)
    def _():
        pl.semaphore_signal(barrier, inc=1, device_id={"tp": z - 1}, device_id_type=MESH)

    @pl.when(z < n - 1)
    def _():
        pl.semaphore_signal(barrier, inc=1, device_id={"tp": z + 1}, device_id_type=MESH)

    return (z > 0).astype(jnp.int32) + (z < n - 1).astype(jnp.int32)


class Line:
    def __init__(self, n, z, segments, segment_rows, parts, inbox, out, sems, finish):
        self.n, self.z = n, z
        self.segment_rows = segment_rows
        self.per_segment = segment_rows // (2 * CHUNK)
        self.chunks = segments * self.per_segment
        self.parts, self.inbox, self.out = parts, inbox, out
        self.red_send, self.red_recv, self.back_send, self.back_recv = sems
        self.finish = finish
        self.ticks = self.chunks + 2 * (n - 1) * LAG

    def ready(self, segments):
        return segments * self.per_segment + 2 * (self.n - 1) * LAG

    def rows(self, flow, g):
        start = (
            (g // self.per_segment) * self.segment_rows
            + flow * (self.segment_rows // 2)
            + (g % self.per_segment) * CHUNK
        )
        return pl.ds(pl.multiple_of(start, CHUNK), CHUNK)

    def hop(self, flow):
        return (self.n - 1 - self.z) if flow == 0 else self.z

    def neighbour(self, up):
        z = jnp.minimum(self.z + 1, self.n - 1) if up else jnp.maximum(self.z - 1, 0)
        return {"tp": z}

    def reduce_copy(self, flow, g, source):
        return pltpu.make_async_remote_copy(
            src_ref=source,
            dst_ref=self.inbox.at[self.rows(flow, g)],
            send_sem=self.red_send.at[flow, g],
            recv_sem=self.red_recv.at[flow, g],
            device_id=self.neighbour(flow == 1),
            device_id_type=MESH,
        )

    def back_copy(self, flow, g):
        rows = self.rows(flow, g)
        return pltpu.make_async_remote_copy(
            src_ref=self.out.at[rows],
            dst_ref=self.out.at[rows],
            send_sem=self.back_send.at[flow, g],
            recv_sem=self.back_recv.at[flow, g],
            device_id=self.neighbour(flow == 0),
            device_id_type=MESH,
        )

    def tick(self, t):
        n = self.n
        for flow in (0, 1):
            hop = self.hop(flow)
            g = t - hop * LAG

            @pl.when((g >= 0) & (g < self.chunks))
            def _():
                rows = self.rows(flow, g)

                @pl.when(hop == 0)
                def _():
                    self.reduce_copy(flow, g, self.parts.at[rows]).start()

                @pl.when(hop > 0)
                def _():
                    self.reduce_copy(flow, g, self.parts.at[rows]).wait_recv()
                    total = self.inbox[rows, :].astype(jnp.float32) + self.parts[rows, :].astype(
                        jnp.float32
                    )

                    @pl.when(hop < n - 1)
                    def _():
                        self.inbox[rows, :] = total.astype(jnp.bfloat16)
                        self.reduce_copy(flow, g, self.inbox.at[rows]).start()

                    @pl.when(hop == n - 1)
                    def _():
                        self.finish(g // self.per_segment, rows, total)
                        self.back_copy(flow, g).start()

        for flow in (0, 1):
            hop = self.hop(flow)
            back = t - (n - 1) * LAG - (n - 1 - hop) * LAG

            @pl.when((back >= 0) & (back < self.chunks) & (hop < n - 1))
            def _():
                self.back_copy(flow, back).wait_recv()

                @pl.when(hop > 0)
                def _():
                    self.back_copy(flow, back).start()

    def run(self, first, last):
        def step(t, carry):
            self.tick(t)
            return carry

        lax.fori_loop(first, last, step, 0)

    def drain(self):
        def step(g, carry):
            for flow in (0, 1):
                hop = self.hop(flow)

                @pl.when(hop < self.n - 1)
                def _():
                    self.reduce_copy(flow, g, self.parts.at[self.rows(flow, g)]).wait_send()

                @pl.when(hop > 0)
                def _():
                    self.back_copy(flow, g).wait_send()

            return carry

        lax.fori_loop(0, self.chunks, step, 0)


def line_scratch(rows, width, segments, segment_rows):
    chunks = segments * (segment_rows // (2 * CHUNK))
    return [VMEM((rows, width), jnp.bfloat16)] + [pltpu.SemaphoreType.DMA((2, chunks))] * 4


def line_cost(rows, width):
    return pl.CostEstimate(flops=rows * width, bytes_accessed=80 * rows * width, transcendentals=0)


def mean_of(values):
    return jnp.mean(values, axis=-1, keepdims=True)


def norm_back(total, values, gain, gain_sums):
    root = lax.rsqrt(mean_of(values * values) + norm_eps)
    standard = values * root
    terms = total * standard
    gain_sums[...] += functools.reduce(
        lambda a, b: a + b, [terms[low : low + 8] for low in range(0, CHUNK, 8)]
    )
    scaled = total * gain
    return root * (scaled - standard * mean_of(scaled * standard))


def turn(first, second, cosine, sine):
    return jnp.concatenate([first * cosine - second * sine, second * cosine + first * sine], 0)


def turn_back(first, second, cosine, sine):
    return jnp.concatenate([first * cosine + second * sine, second * cosine - first * sine], 0)


def mask_bias(key_position, query_position, length):
    allowed = (key_position <= query_position) & (key_position < length)
    return jnp.where(allowed, 0.0, neg_big)


def cut(rows, parts):
    tiles = rows // 16
    ends = [tiles * i // parts * 16 for i in range(parts + 1)]
    return [(low, high - low) for low, high in zip(ends[:-1], ends[1:])]


class Gather:
    def __init__(self, source, whole, low, length, block_rows, fsdp, n, sems):
        self.source, self.whole = source, whole
        self.low, self.length, self.block_rows = low, length, block_rows
        self.fsdp, self.n = fsdp, n
        self.f, self.me = lax.axis_index("fsdp"), lax.axis_index("ctx")
        self.across = lax.rem(self.me + n // 2, n)
        self.other = self.me + 1 - 2 * lax.rem(self.me, 2)
        self.sems = sems
        self.first = length // 32 * 16

    def at(self, f, ctx, low=0, length=None):
        start = (f * self.n + ctx) * self.block_rows + self.low + low
        return self.whole.at[
            pl.ds(pl.multiple_of(start, 16), self.length if length is None else length)
        ]

    def copy(self, kind, source, target, where):
        return pltpu.make_async_remote_copy(
            src_ref=source,
            dst_ref=target,
            send_sem=self.sems.at[0, kind],
            recv_sem=self.sems.at[1, kind],
            device_id=where,
            device_id_type=MESH,
        )

    def own(self):
        return self.source.at[pl.ds(self.low, self.length)]

    def ahead(self, j):
        return lax.rem(self.f + j, self.fsdp)

    def behind(self, j):
        return lax.rem(self.f + self.fsdp - j, self.fsdp)

    def to_across(self):
        return self.copy(0, self.own(), self.at(self.f, self.me), {"ctx": self.across})

    def to_other(self):
        return self.copy(1, self.own(), self.at(self.f, self.me), {"ctx": self.other})

    def across_to_other(self):
        at = self.at(self.f, self.across)
        return self.copy(2, at, at, {"ctx": self.other})

    def to_ahead(self, j):
        return self.copy(3 * j, self.own(), self.at(self.f, self.me), {"fsdp": self.ahead(j)})

    def behind_to_other(self, j):
        at = self.at(self.behind(j), self.me)
        return self.copy(3 * j + 1, at, at, {"ctx": self.other})

    def corner_to_other(self, j):
        at = self.at(self.behind(j), self.across)
        return self.copy(3 * j + 2, at, at, {"ctx": self.other})

    def across_to_ahead(self, j):
        at = self.at(self.f, self.across, 0, self.first)
        return self.copy(3 * self.fsdp + 2 * j - 2, at, at, {"fsdp": self.ahead(j)})

    def behind_to_across(self, j):
        at = self.at(self.behind(j), self.me, self.first, self.length - self.first)
        return self.copy(3 * self.fsdp + 2 * j - 1, at, at, {"ctx": self.across})

    def local(self):
        return pltpu.make_async_copy(self.own(), self.at(self.f, self.me), self.sems.at[2, 0])

    def start(self):
        self.to_across().start()
        for j in range(1, self.fsdp):
            self.to_ahead(j).start()
        self.to_other().start()
        self.local().start()

    def forward(self):
        self.to_across().wait_recv()
        for j in range(1, self.fsdp):
            self.across_to_ahead(j).start()
        self.across_to_other().start()
        for j in range(1, self.fsdp):
            self.to_ahead(j).wait_recv()
            self.behind_to_across(j).start()
            self.behind_to_other(j).start()

    def corner(self):
        for j in range(1, self.fsdp):
            self.across_to_ahead(j).wait_recv()
            self.behind_to_across(j).wait_recv()
            self.corner_to_other(j).start()

    def finish(self):
        self.local().wait()
        self.to_other().wait_recv()
        self.across_to_other().wait_recv()
        for j in range(1, self.fsdp):
            self.behind_to_other(j).wait_recv()
            self.corner_to_other(j).wait_recv()

    def drain(self):
        self.to_across().wait_send()
        self.to_other().wait_send()
        self.across_to_other().wait_send()
        for j in range(1, self.fsdp):
            self.to_ahead(j).wait_send()
            self.behind_to_other(j).wait_send()
            self.corner_to_other(j).wait_send()
            self.across_to_ahead(j).wait_send()
            self.behind_to_across(j).wait_send()


def gather_sems(fsdp):
    return pltpu.SemaphoreType.DMA((3, 5 * fsdp - 2))


FIRST_PIECES = 2
SECOND_PIECES = 4


def front_body(
    n,
    tp,
    fsdp,
    groups,
    out_width,
    token_ref,
    first_ref,
    second_ref,
    cos_ref,
    sin_ref,
    key_pos_ref,
    query_pos_ref,
    length_ref,
    first_whole,
    second_whole,
    normal_ref,
    gain_ref,
    q_ref,
    kv_ref,
    full_ref,
    low_ref,
    log_ref,
    residual_ref,
    out_ref,
    proj,
    bias,
    parts,
    send_sem,
    recv_sem,
    first_sems,
    second_sems,
    inbox,
    *sems,
):
    z = lax.axis_index("tp")
    f = lax.axis_index("fsdp")
    me = lax.axis_index("ctx")
    peers = line_greet(tp, z)
    barrier = pltpu.get_barrier_semaphore()
    for step in range(1, n):
        pl.semaphore_signal(
            barrier, inc=1, device_id={"ctx": lax.rem(me + step, n)}, device_id_type=MESH
        )
    for step in range(1, fsdp):
        pl.semaphore_signal(
            barrier, inc=1, device_id={"fsdp": lax.rem(f + step, fsdp)}, device_id_type=MESH
        )
    pl.semaphore_wait(barrier, peers + n - 1 + fsdp - 1)

    seqs, _, rows = q_ref.shape
    dim = HEAD_DIMENSION
    half = dim // 2
    group_width = (GROUP + 2) * dim
    in_width = groups * group_width
    heads = groups * GROUP
    width = token_ref.shape[1]
    tile = 512 if width % 512 == 0 else width

    def gathers(source, whole, pieces, sems):
        block = source.shape[0]
        return [
            Gather(source, whole, low, length, block, fsdp, n, sems.at[i])
            for i, (low, length) in enumerate(cut(block, pieces))
        ]

    first = gathers(first_ref, first_whole, FIRST_PIECES, first_sems)
    second = gathers(second_ref, second_whole, SECOND_PIECES, second_sems)
    for piece in first:
        piece.start()
    for piece in first:
        piece.forward()
    for piece in first:
        piece.corner()
    second[0].start()
    for piece in first:
        piece.finish()

    columns = out_width + in_width
    base = columns // 128 * 128
    turned = first_whole[:, base : base + 128].astype(jnp.float32).T
    gain_ref[...] = turned[columns - base : columns - base + 8]

    def columns_of(m):
        return pl.ds(pl.multiple_of(m * rows, 128), rows)

    def rows_of(m):
        return pl.ds(pl.multiple_of(m * rows, CHUNK), rows)

    def copy(m, step):
        return pltpu.make_async_remote_copy(
            src_ref=kv_ref.at[m, me],
            dst_ref=kv_ref.at[m, me],
            send_sem=send_sem.at[m, step - 1],
            recv_sem=recv_sem.at[m, step - 1],
            device_id={"ctx": lax.rem(me + step, n)},
            device_id_type=MESH,
        )

    def project(m, carry):
        values = token_ref[rows_of(m), :].astype(jnp.float32)
        root = lax.rsqrt(mean_of(values * values) + norm_eps)
        normal_ref[rows_of(m), :] = (values * root * gain_ref[0:1, :]).astype(jnp.bfloat16)
        proj[m] = jnp.dot(
            normal_ref[rows_of(m), :],
            first_whole[:, out_width : out_width + in_width],
            preferred_element_type=jnp.float32,
        ).T
        for g in range(groups):
            col = g * group_width + GROUP * dim
            kv_ref[m, me, g, :dim, :] = turn(
                proj[m, col : col + half, :],
                proj[m, col + half : col + dim, :],
                cos_ref[m],
                sin_ref[m],
            ).astype(jnp.bfloat16)
            kv_ref[m, me, g, dim:, :] = proj[m, col + dim : col + 2 * dim, :].astype(jnp.bfloat16)
        for step in range(1, n):
            copy(m, step).start()
        return carry

    lax.fori_loop(0, seqs, project, 0)
    for piece in second[1:]:
        piece.start()

    def finish(segment, at, total):
        values = token_ref[at, :].astype(jnp.float32) + total
        residual_ref[at, :] = values
        root = lax.rsqrt(mean_of(values * values) + norm_eps)
        out_ref[at, :] = (values * root * gain_ref[1:2, :]).astype(jnp.bfloat16)

    line = Line(tp, z, seqs, rows, parts, inbox, out_ref, sems, finish)

    def head(m, at):
        g = at // GROUP
        h = at % GROUP
        low = pl.ds(pl.multiple_of(at * dim, 16), dim)
        col = pl.multiple_of(g * group_width + h * dim, 8)
        query = turn(
            proj[m, pl.ds(col, half), :],
            proj[m, pl.ds(pl.multiple_of(col + half, 8), half), :],
            cos_ref[m],
            sin_ref[m],
        ).astype(jnp.bfloat16)
        q_ref[m, low, :] = query
        scores = [
            lax.dot_general(
                kv_ref[m, j, g, :dim, :],
                query,
                (((0,), (0,)), ((), ())),
                preferred_element_type=jnp.float32,
            )
            * (log2_e * dim**-0.5)
            + bias[j * rows : (j + 1) * rows, :]
            for j in range(n)
        ]
        top = functools.reduce(jnp.maximum, [jnp.max(s, axis=0, keepdims=True) for s in scores])
        total = jnp.zeros_like(top)
        out = jnp.zeros((dim, rows), jnp.float32)
        for j in range(n):
            weights = jnp.exp2(scores[j] - top)
            total += jnp.sum(weights, axis=0, keepdims=True)
            out += jnp.dot(
                kv_ref[m, j, g, dim:, :],
                weights.astype(jnp.bfloat16),
                preferred_element_type=jnp.float32,
            )
        out = out / total
        full_ref[m, low, :] = out
        low_ref[low, columns_of(m)] = out.astype(jnp.bfloat16)
        log_ref[m, at] = top + jnp.log2(total)

    def ready(m):
        bias[...] = mask_bias(key_pos_ref[m], query_pos_ref[m], length_ref[m])
        for step in range(1, n):
            copy(m, step).wait_recv()

    def product(m):
        left = low_ref[:, columns_of(m)].T
        for low in range(0, width, tile):
            parts[rows_of(m), low : low + tile] = lax.dot_general(
                left,
                first_whole[low : low + tile, :out_width],
                (((1,), (1,)), ((), ())),
                preferred_element_type=jnp.float32,
            ).astype(jnp.bfloat16)

    def sequence(m, carry):
        ready(m)

        def item(at, inner):
            line.tick((m - 1) * heads + at)
            head(m, at)
            return inner

        lax.fori_loop(0, heads, item, 0)
        product(m)
        return carry

    def opening(at, carry):
        head(0, at)
        return carry

    ready(0)
    lax.fori_loop(0, heads, opening, 0)
    product(0)
    second[0].forward()
    lax.fori_loop(1, 2, sequence, 0)
    second[1].forward()
    lax.fori_loop(2, seqs, sequence, 0)
    for piece in second[2:]:
        piece.forward()
    at = (seqs - 1) * heads
    line.run(at, at + 4)
    for piece in second[:2]:
        piece.corner()
    line.run(at + 4, at + 10)
    for piece in second[2:]:
        piece.corner()
    line.run(at + 10, line.ticks)
    for piece in second:
        piece.finish()
    line.drain()
    for piece in first + second:
        piece.drain()

    def drain(m, carry):
        for step in range(1, n):
            copy(m, step).wait_send()
        return carry

    lax.fori_loop(0, seqs, drain, 0)


def front(tokens, first_pack, second_pack, where, seqs, out_width, in_width, n, tp, fsdp, ident):
    all_rows, model_width = tokens.shape
    rows = all_rows // seqs
    groups = in_width // ((GROUP + 2) * HEAD_DIMENSION)
    heads = groups * GROUP
    shards = n * fsdp
    dim = HEAD_DIMENSION
    shape = jax.ShapeDtypeStruct
    low, wide = jnp.bfloat16, jnp.float32
    vmem = pl.BlockSpec(memory_space=VMEM)
    hbm = pl.BlockSpec(memory_space=pl.ANY)
    return pl.pallas_call(
        functools.partial(front_body, n, tp, fsdp, groups, out_width),
        out_shape=(
            shape((shards * first_pack.shape[0], first_pack.shape[1]), low),
            shape((shards * second_pack.shape[0], second_pack.shape[1]), low),
            shape((all_rows, model_width), low),
            shape((8, model_width), wide),
            shape((seqs, heads * dim, rows), low),
            shape((seqs, n, groups, 2 * dim, rows), low),
            shape((seqs, heads * dim, rows), wide),
            shape((heads * dim, all_rows), low),
            shape((seqs, heads, 1, rows), wide),
            shape((all_rows, model_width), wide),
            shape((all_rows, model_width), low),
        ),
        in_specs=[vmem, hbm, hbm] + [vmem] * 5,
        out_specs=(vmem, hbm) + (vmem,) * 9,
        scratch_shapes=[
            VMEM((seqs, in_width, rows), wide),
            VMEM((n * rows, rows), wide),
            VMEM((all_rows, model_width), low),
            pltpu.SemaphoreType.DMA((seqs, n - 1)),
            pltpu.SemaphoreType.DMA((seqs, n - 1)),
            pltpu.SemaphoreType.DMA((FIRST_PIECES, 3, 5 * fsdp - 2)),
            pltpu.SemaphoreType.DMA((SECOND_PIECES, 3, 5 * fsdp - 2)),
        ]
        + line_scratch(all_rows, model_width, seqs, rows),
        compiler_params=pltpu.CompilerParams(
            collective_id=ident, has_side_effects=True, vmem_limit_bytes=60 * 2**20
        ),
        cost_estimate=line_cost(all_rows, model_width),
        name="front",
    )(tokens, first_pack, second_pack, *where)


def back_one_body(
    n,
    tp,
    groups,
    normal_ref,
    mixed_ref,
    residual_ref,
    grad_out_ref,
    gain_ref,
    weight_ref,
    q_ref,
    kv_ref,
    full_ref,
    log_ref,
    cos_ref,
    sin_ref,
    key_pos_ref,
    query_pos_ref,
    length_ref,
    out_ref,
    proj_ref,
    gain_sums,
    parts,
    out_proj,
    grads,
    sums,
    bias,
    outbox,
    kv_inbox,
    load_sem,
    send_sem,
    recv_sem,
    inbox,
    *sems,
):
    z = lax.axis_index("tp")
    me = lax.axis_index("ctx")
    seqs, _, rows = q_ref.shape
    all_rows = seqs * rows
    loads = [
        pltpu.make_async_copy(normal_ref, parts.at[pl.ds(0, all_rows)], load_sem.at[0]),
        pltpu.make_async_copy(mixed_ref, parts.at[pl.ds(all_rows, all_rows)], load_sem.at[1]),
        pltpu.make_async_copy(
            weight_ref.at[:, pl.ds(0, out_proj.shape[1])], out_proj, load_sem.at[2]
        ),
    ]
    for load in loads:
        load.start()
    peers = line_greet(tp, z)
    barrier = pltpu.get_barrier_semaphore()
    for step in range(1, n):
        pl.semaphore_signal(
            barrier, inc=1, device_id={"ctx": lax.rem(me + step, n)}, device_id_type=MESH
        )
    pl.semaphore_wait(barrier, peers + n - 1)

    dim = HEAD_DIMENSION
    half = dim // 2
    scale = dim**-0.5
    group_width = (GROUP + 2) * dim
    heads = groups * GROUP
    gain_sums[...] = jnp.zeros_like(gain_sums)

    def finish(segment, at, total):
        @pl.when(segment < seqs)
        def _():
            grad = norm_back(total, residual_ref[at, :], gain_ref[1:2, :], gain_sums)
            out_ref[at, :] = (grad_out_ref[at, :].astype(jnp.float32) + grad).astype(jnp.bfloat16)

        @pl.when(segment >= seqs)
        def _():
            start = pl.multiple_of(at.start - all_rows, CHUNK)
            out_ref[at, :] = (residual_ref[pl.ds(start, CHUNK), :] + total).astype(jnp.bfloat16)

    line = Line(tp, z, 2 * seqs, rows, parts, inbox, out_ref, sems, finish)

    def copy(m, step):
        to = lax.rem(me + step, n)
        return pltpu.make_async_remote_copy(
            src_ref=outbox.at[m, to],
            dst_ref=kv_inbox.at[m, step - 1],
            send_sem=send_sem.at[m, step - 1],
            recv_sem=recv_sem.at[m, step - 1],
            device_id={"ctx": to},
            device_id_type=MESH,
        )

    def columns(m):
        return pl.ds(pl.multiple_of(m * rows, 128), rows)

    def attended_grads(m):
        grads[...] = (
            jnp.dot(
                out_ref[pl.ds(pl.multiple_of(m * rows, CHUNK), rows), :],
                out_proj[...],
                preferred_element_type=jnp.float32,
            )
            .T.astype(jnp.bfloat16)
        )
        bias[...] = mask_bias(key_pos_ref[m], query_pos_ref[m], length_ref[m])

    def head(m, at):
        g = at // GROUP
        h = at % GROUP
        low = pl.ds(pl.multiple_of(at * dim, 16), dim)
        query = q_ref[m, low, :]
        grad = grads[low, :]
        delta = jnp.sum(
            grad.astype(jnp.float32) * full_ref[m, low, :], axis=0, keepdims=True
        )
        log_total = log_ref[m, at]
        query_sum = jnp.zeros((dim, rows), jnp.float32)

        @pl.when(h == 0)
        def _():
            sums[...] = jnp.zeros_like(sums)

        for j in range(n):
            keys = kv_ref[m, j, g, :dim, :]
            values = kv_ref[m, j, g, dim:, :]
            scores = lax.dot_general(
                keys, query, (((0,), (0,)), ((), ())), preferred_element_type=jnp.float32
            )
            probs = jnp.exp2(
                scores * (log2_e * scale) + (bias[j * rows : (j + 1) * rows, :] - log_total)
            )
            grad_probs = lax.dot_general(
                values, grad, (((0,), (0,)), ((), ())), preferred_element_type=jnp.float32
            )
            grad_scores = (probs * (grad_probs - delta)).astype(jnp.bfloat16)
            query_sum += jnp.dot(keys, grad_scores, preferred_element_type=jnp.float32)
            sums[j, :dim, :] += lax.dot_general(
                query, grad_scores, (((1,), (1,)), ((), ())), preferred_element_type=jnp.float32
            )
            sums[j, dim:, :] += lax.dot_general(
                grad,
                probs.astype(jnp.bfloat16),
                (((1,), (1,)), ((), ())),
                preferred_element_type=jnp.float32,
            )
        query_sum = query_sum * scale
        col = pl.ds(pl.multiple_of(g * group_width + h * dim, 16), dim)
        proj_ref[col, columns(m)] = turn_back(
            query_sum[:half], query_sum[half:], cos_ref[m], sin_ref[m]
        ).astype(jnp.bfloat16)

        @pl.when(h == GROUP - 1)
        def _():
            for j in range(n):
                outbox[m, j, g, :dim, :] = (sums[j, :dim, :] * scale).astype(jnp.bfloat16)
                outbox[m, j, g, dim:, :] = sums[j, dim:, :].astype(jnp.bfloat16)

    def gather(m):
        for step in range(1, n):
            copy(m, step).wait_recv()
        for g in range(groups):
            total = outbox[m, me, g].astype(jnp.float32)
            for step in range(1, n):
                total += kv_inbox[m, step - 1, g].astype(jnp.float32)
            col = g * group_width + GROUP * dim
            proj_ref[col : col + dim, columns(m)] = turn_back(
                total[:half], total[half:dim], cos_ref[m], sin_ref[m]
            ).astype(jnp.bfloat16)
            proj_ref[col + dim : col + 2 * dim, columns(m)] = total[dim:].astype(jnp.bfloat16)
        for step in range(1, n):
            copy(m, step).wait_send()

    loads[0].wait()
    line.run(0, line.ready(1))
    loads[1].wait()
    loads[2].wait()

    def sequence(m, carry):
        first = line.ready(1) + m * (heads + 1)
        line.tick(first)
        attended_grads(m)

        def item(at, inner):
            line.tick(first + 1 + at)
            head(m, at)
            return inner

        lax.fori_loop(0, heads, item, 0)
        for step in range(1, n):
            copy(m, step).start()
        return carry

    lax.fori_loop(0, seqs, sequence, 0)
    line.run(line.ready(1) + seqs * (heads + 1), line.ticks)

    def collect(m, carry):
        gather(m)
        return carry

    lax.fori_loop(0, seqs, collect, 0)
    line.drain()


def back_one(
    normal_part,
    mixed_part,
    residual,
    grad_out,
    gains,
    first_whole,
    queries,
    key_values,
    full,
    log_total,
    where,
    n,
    tp,
    ident,
):
    seqs, width, rows = queries.shape
    groups = key_values.shape[2]
    all_rows, model_width = normal_part.shape
    vmem = pl.BlockSpec(memory_space=VMEM)
    hbm = pl.BlockSpec(memory_space=pl.ANY)
    shape = jax.ShapeDtypeStruct
    return pl.pallas_call(
        functools.partial(back_one_body, n, tp, groups),
        out_shape=(
            shape((2 * all_rows, model_width), jnp.bfloat16),
            shape((groups * (GROUP + 2) * HEAD_DIMENSION, all_rows), jnp.bfloat16),
            shape((8, model_width), jnp.float32),
        ),
        in_specs=[hbm, hbm, vmem, vmem, vmem, hbm] + [vmem] * 9,
        out_specs=(vmem,) * 3,
        scratch_shapes=[
            VMEM((2 * all_rows, model_width), jnp.bfloat16),
            VMEM((model_width, width), jnp.bfloat16),
            VMEM((width, rows), jnp.bfloat16),
            VMEM((n, 2 * HEAD_DIMENSION, rows), jnp.float32),
            VMEM((n * rows, rows), jnp.float32),
            VMEM((seqs, n, groups, 2 * HEAD_DIMENSION, rows), jnp.bfloat16),
            VMEM((seqs, n - 1, groups, 2 * HEAD_DIMENSION, rows), jnp.bfloat16),
            pltpu.SemaphoreType.DMA((3,)),
            pltpu.SemaphoreType.DMA((seqs, n - 1)),
            pltpu.SemaphoreType.DMA((seqs, n - 1)),
        ]
        + line_scratch(2 * all_rows, model_width, 2 * seqs, rows),
        compiler_params=pltpu.CompilerParams(
            collective_id=ident, has_side_effects=True, vmem_limit_bytes=60 * 2**20
        ),
        cost_estimate=line_cost(2 * all_rows, model_width),
        name="back_one",
    )(
        normal_part,
        mixed_part,
        residual,
        grad_out,
        gains,
        first_whole,
        queries,
        key_values,
        full,
        log_total,
        *where,
    )


def back_two_body(
    tp,
    seqs,
    skip,
    proj_ref,
    weight_ref,
    token_ref,
    residual_grad_ref,
    gain_ref,
    out_ref,
    gain_sums,
    parts,
    inbox,
    *sems,
):
    z = lax.axis_index("tp")
    pl.semaphore_wait(pltpu.get_barrier_semaphore(), line_greet(tp, z))
    gain_sums[...] = jnp.zeros_like(gain_sums)
    rows = token_ref.shape[0] // seqs
    width = weight_ref.shape[0]
    tile = 512 if width % 512 == 0 else width

    def finish(segment, at, total):
        values = token_ref[at, :].astype(jnp.float32)
        grad = norm_back(total, values, gain_ref[0:1, :], gain_sums)
        out_ref[at, :] = (residual_grad_ref[at, :].astype(jnp.float32) + grad).astype(jnp.bfloat16)

    line = Line(tp, z, seqs, rows, parts, inbox, out_ref, sems, finish)

    def product(m):
        left = proj_ref[:, m * rows : (m + 1) * rows].T
        for low in range(0, width, tile):
            parts[m * rows : (m + 1) * rows, low : low + tile] = lax.dot_general(
                left,
                weight_ref[low : low + tile, skip : skip + proj_ref.shape[0]],
                (((1,), (1,)), ((), ())),
                preferred_element_type=jnp.float32,
            ).astype(jnp.bfloat16)

    for m in range(seqs):
        product(m)
        line.run(2 * m, 2 * m + 2)
    line.run(2 * seqs, line.ticks)
    line.drain()


def back_two(projected, first_whole, tokens, residual_grad, gains, skip, seqs, tp, ident):
    rows, width = tokens.shape
    vmem = pl.BlockSpec(memory_space=VMEM)
    shape = jax.ShapeDtypeStruct
    return pl.pallas_call(
        functools.partial(back_two_body, tp, seqs, skip),
        out_shape=(shape((rows, width), jnp.bfloat16), shape((8, width), jnp.float32)),
        in_specs=[vmem] * 5,
        out_specs=(vmem,) * 2,
        scratch_shapes=[VMEM((rows, width), jnp.bfloat16)]
        + line_scratch(rows, width, seqs, rows // seqs),
        compiler_params=pltpu.CompilerParams(
            collective_id=ident, has_side_effects=True, vmem_limit_bytes=56 * 2**20
        ),
        cost_estimate=line_cost(rows, width),
        name="back_two",
    )(projected, first_whole, tokens, residual_grad, gains)


def hidden_body(
    normal_ref, grad_out_ref, gate_ref, up_ref, down_ref, inner_ref, grad_gate_ref, grad_up_ref
):
    def product(left, right):
        return jnp.dot(left[...], right[...], preferred_element_type=jnp.float32)

    gate = product(normal_ref, gate_ref)
    up = product(normal_ref, up_ref)
    grad_inner = product(grad_out_ref, down_ref)
    sigmoid = jax.nn.sigmoid(gate)
    silu = gate * sigmoid
    inner_ref[...] = (silu * up).astype(jnp.bfloat16)
    grad_gate_ref[...] = (
        grad_inner * up * sigmoid * (1.0 + gate * (1.0 - sigmoid))
    ).astype(jnp.bfloat16)
    grad_up_ref[...] = (grad_inner * silu).astype(jnp.bfloat16)


def hidden_units(normal, grad_out, whole, tile=256):
    rows, width = normal.shape
    columns = whole.shape[1]
    units = columns // 3
    steps = units // tile
    vmem = pl.BlockSpec(memory_space=VMEM)
    return pl.pallas_call(
        hidden_body,
        grid=(steps,),
        out_shape=(jax.ShapeDtypeStruct((rows, units), jnp.bfloat16),) * 3,
        in_specs=[vmem, vmem]
        + [
            pl.BlockSpec((width, tile), functools.partial(lambda k, i: (0, k * steps + i), k))
            for k in range(3)
        ],
        out_specs=[pl.BlockSpec((rows, tile), lambda i: (0, i))] * 3,
        compiler_params=pltpu.CompilerParams(vmem_limit_bytes=56 * 2**20),
        cost_estimate=pl.CostEstimate(
            flops=2 * rows * width * columns,
            bytes_accessed=2 * (rows + width) * columns,
            transcendentals=rows * units,
        ),
        name="hidden_units",
    )(normal, grad_out, whole, whole, whole)


def leave_body(inner_ref, grad_gate_ref, grad_up_ref, weight_ref, normal_ref, mixed_ref):
    units = inner_ref.shape[1]

    def product(left, k):
        return lax.dot_general(
            left[...],
            weight_ref[:, k * units : (k + 1) * units],
            (((1,), (1,)), ((), ())),
            preferred_element_type=jnp.float32,
        )

    normal_ref[...] = (product(grad_gate_ref, 0) + product(grad_up_ref, 1)).astype(jnp.bfloat16)
    mixed_ref[...] = product(inner_ref, 2).astype(jnp.bfloat16)


def leave(inner, grad_gate, grad_up, whole, tile=256):
    rows, units = inner.shape
    width, columns = whole.shape
    low = jnp.bfloat16
    vmem = pl.BlockSpec(memory_space=VMEM)
    return pl.pallas_call(
        leave_body,
        grid=(width // tile,),
        out_shape=(jax.ShapeDtypeStruct((rows, width), low),) * 2,
        in_specs=[vmem] * 3 + [pl.BlockSpec((tile, columns), lambda i: (i, 0))],
        out_specs=[pl.BlockSpec((rows, tile), lambda i: (0, i))] * 2,
        compiler_params=pltpu.CompilerParams(vmem_limit_bytes=56 * 2**20),
        cost_estimate=pl.CostEstimate(
            flops=2 * rows * width * columns,
            bytes_accessed=2 * (rows + width) * columns,
            transcendentals=0,
        ),
        name="leave",
    )(inner, grad_gate, grad_up, whole)


def grads_body(rows_last, left_ref, right_ref, *rest):
    out_ref, turned = rest[-2:]

    @pl.when(pl.program_id(0) == 0)
    def _():
        turned[...] = left_ref[...].T

    contract = (((1,), (1 if rows_last else 0,)), ((), ()))
    width = turned.shape[0]
    part = 512 if width % 512 == 0 else width
    for low in range(0, width, part):
        out_ref[low : low + part, :] = lax.dot_general(
            turned[low : low + part, :],
            right_ref[...],
            contract,
            preferred_element_type=jnp.float32,
        ).astype(out_ref.dtype)


def grads_into(buffer, columns, first, left, right, rows_last, tile):
    rows, width = left.shape
    n = right.shape[0] if rows_last else right.shape[1]
    in_specs = [
        pl.BlockSpec(memory_space=VMEM),
        pl.BlockSpec((tile, rows), lambda i: (i, 0))
        if rows_last
        else pl.BlockSpec((rows, tile), lambda i: (0, i)),
    ]
    operands = [left, right]
    aliases = {}
    if buffer is not None:
        in_specs.append(pl.BlockSpec(memory_space=pl.ANY))
        operands.append(buffer)
        aliases = {2: 0}
    return pl.pallas_call(
        functools.partial(grads_body, rows_last),
        grid=(n // tile,),
        out_shape=jax.ShapeDtypeStruct((width, columns), jnp.bfloat16),
        in_specs=in_specs,
        out_specs=pl.BlockSpec((width, tile), lambda i: (0, first // tile + i)),
        scratch_shapes=[VMEM((width, rows), jnp.bfloat16)],
        input_output_aliases=aliases,
        compiler_params=pltpu.CompilerParams(vmem_limit_bytes=48 * 2**20),
        cost_estimate=pl.CostEstimate(
            flops=2 * rows * width * n,
            bytes_accessed=2 * (rows * width + rows * n + width * n),
            transcendentals=0,
        ),
        name="weight_grads",
    )(*operands)


def first_grads_body(normal_ref, proj_ref, residual_ref, attended_ref, out_ref):
    width = out_ref.shape[0]
    split = attended_ref.shape[0]
    tile = 512 if width % 512 == 0 else width
    contract = (((1,), (1,)), ((), ()))
    for low in range(0, width, tile):
        out_ref[low : low + tile, :split] = lax.dot_general(
            residual_ref[:, low : low + tile].T,
            attended_ref[...],
            contract,
            preferred_element_type=jnp.float32,
        ).astype(jnp.bfloat16)
        out_ref[low : low + tile, split:] = lax.dot_general(
            normal_ref[:, low : low + tile].T,
            proj_ref[...],
            contract,
            preferred_element_type=jnp.float32,
        ).astype(jnp.bfloat16)


def first_grads_of(normal, projected, residual_grad, attended):
    rows, width = normal.shape
    columns = projected.shape[0] + attended.shape[0]
    vmem = pl.BlockSpec(memory_space=VMEM)
    return pl.pallas_call(
        first_grads_body,
        out_shape=jax.ShapeDtypeStruct((width, columns), jnp.bfloat16),
        in_specs=[vmem] * 4,
        out_specs=vmem,
        compiler_params=pltpu.CompilerParams(vmem_limit_bytes=48 * 2**20),
        cost_estimate=pl.CostEstimate(
            flops=2 * rows * width * columns,
            bytes_accessed=2 * (2 * rows * width + (rows + width) * columns),
            transcendentals=0,
        ),
        name="first_grads",
    )(normal, projected, residual_grad, attended)


def gain_body(ctx_size, tp, x_ref, o_ref, inbox, tp_inbox, send_sem, recv_sem, tp_send, tp_recv):
    shards = x_ref.shape[0]
    me = lax.axis_index("fsdp") * ctx_size + lax.axis_index("ctx")
    z = lax.axis_index("tp")

    def to(step):
        other = lax.rem(me + step, shards)
        return other, {"fsdp": other // ctx_size, "ctx": lax.rem(other, ctx_size)}

    barrier = pltpu.get_barrier_semaphore()
    for step in range(1, shards):
        pl.semaphore_signal(barrier, inc=1, device_id=to(step)[1], device_id_type=MESH)
    for step in range(1, tp):
        pl.semaphore_signal(
            barrier, inc=1, device_id={"tp": lax.rem(z + step, tp)}, device_id_type=MESH
        )
    pl.semaphore_wait(barrier, shards - 1 + tp - 1)

    def copy(step):
        other, where = to(step)
        return pltpu.make_async_remote_copy(
            src_ref=x_ref.at[other],
            dst_ref=inbox.at[step - 1],
            send_sem=send_sem.at[step - 1],
            recv_sem=recv_sem.at[step - 1],
            device_id=where,
            device_id_type=MESH,
        )

    def tp_copy(step):
        return pltpu.make_async_remote_copy(
            src_ref=tp_inbox.at[0],
            dst_ref=tp_inbox.at[step],
            send_sem=tp_send.at[step - 1],
            recv_sem=tp_recv.at[step - 1],
            device_id={"tp": lax.rem(z + step, tp)},
            device_id_type=MESH,
        )

    for step in range(1, shards):
        copy(step).start()
    total = x_ref[me]
    for step in range(1, shards):
        copy(step).wait()
        total += inbox[step - 1]
    tp_inbox[0] = total
    for step in range(1, tp):
        tp_copy(step).start()
    for step in range(1, tp):
        tp_copy(step).wait()
        total += tp_inbox[step]
    o_ref[...] = total


def gain_sum(partial, shards, ctx_size, tp, ident):
    two, width = partial.shape
    own = width // shards
    padded = -(-own // 128) * 128
    pieces = jnp.pad(
        partial.reshape(two, shards, own).transpose(1, 0, 2),
        ((0, 0), (0, 8 - two), (0, padded - own)),
    )
    total = pl.pallas_call(
        functools.partial(gain_body, ctx_size, tp),
        out_shape=jax.ShapeDtypeStruct((8, padded), jnp.float32),
        in_specs=[pl.BlockSpec(memory_space=VMEM)],
        out_specs=pl.BlockSpec(memory_space=VMEM),
        scratch_shapes=[
            VMEM((shards - 1, 8, padded), jnp.float32),
            VMEM((tp, 8, padded), jnp.float32),
            pltpu.SemaphoreType.DMA((shards - 1,)),
            pltpu.SemaphoreType.DMA((shards - 1,)),
            pltpu.SemaphoreType.DMA((tp - 1,)),
            pltpu.SemaphoreType.DMA((tp - 1,)),
        ],
        compiler_params=pltpu.CompilerParams(collective_id=ident, has_side_effects=True),
        name="gain_sum",
    )(pieces)
    return total[:two, :own]


def dot(spec, left, right):
    return jnp.einsum(spec, left, right, preferred_element_type=jnp.float32)


def on_device(
    tokens,
    out_cotangent,
    seq_lengths,
    span_order,
    attention_input_weight,
    attention_input_first,
    attention_input_squared,
    attend_out,
    attend_out_moment,
    attend_out_second,
    gate_up,
    gate_up_moment,
    gate_up_second,
    down_weight,
    down_weight_moment,
    down_weight_second,
    norm_gains,
    norm_gains_moment,
    norm_gains_second,
):
    low = jnp.bfloat16
    micro_count, slot_count, row_count, model_width = tokens.shape
    seqs = micro_count * slot_count
    ctx_size = lax.axis_size("ctx")
    tp_size = lax.axis_size("tp")
    sequence_length = row_count * ctx_size
    span_len = sequence_length // (2 * ctx_size)
    hidden = down_weight.shape[0]
    out_width = attend_out.shape[0]
    in_width = attention_input_weight.shape[1]
    shards = ("fsdp", "ctx")

    own = attention_input_weight.shape[0]
    used = out_width + in_width + 2
    padded = -(-used // 128) * 128
    first_pack = jnp.concatenate(
        [
            attend_out.T,
            attention_input_weight,
            norm_gains.T,
            jnp.zeros((own, padded - used), jnp.float32),
        ],
        1,
    ).astype(low)
    second_pack = jnp.concatenate([gate_up, down_weight.T], 1).astype(low)

    orders = span_order.reshape(seqs, 2 * ctx_size)
    lengths = seq_lengths.reshape(seqs)
    within = jnp.arange(sequence_length, dtype=jnp.int32)
    block_ids = jnp.arange(2 * ctx_size, dtype=jnp.int32)
    table = jnp.where(
        block_ids[None, None, :] == (within // span_len)[None, :, None], orders[:, None, :], 0
    )
    pos_all = jnp.sum(table, -1) * span_len + within % span_len
    pos_here = lax.dynamic_slice_in_dim(pos_all, lax.axis_index("ctx") * row_count, row_count, 1)
    half_width = HEAD_DIMENSION // 2
    inverse = rope_base ** (-(jnp.arange(half_width, dtype=jnp.float32) * 2.0 / HEAD_DIMENSION))
    angles = pos_here.astype(jnp.float32)[:, None, :] * inverse[None, :, None]
    cosine, sine = jnp.cos(angles), jnp.sin(angles)
    key_pos = pos_all[:, :, None]
    query_pos = pos_here[:, None, :]
    length_row = jnp.broadcast_to(lengths[:, None, None], query_pos.shape)
    where = (cosine, sine, key_pos, query_pos, length_row)

    all_rows = seqs * row_count
    token_rows = tokens.reshape(all_rows, model_width)
    (
        first_whole,
        second_whole,
        first_normal,
        gains,
        queries,
        key_values,
        attended_full,
        attended,
        log_total,
        residual,
        second_normal,
    ) = front(
        token_rows,
        first_pack,
        second_pack,
        where,
        seqs,
        out_width,
        in_width,
        ctx_size,
        tp_size,
        lax.axis_size("fsdp"),
        1,
    )

    keep = (pos_here < lengths[:, None]).astype(jnp.float32)[..., None]
    grad_out = out_cotangent.reshape(seqs, row_count, model_width).astype(jnp.float32) * keep
    grad_out = grad_out.astype(low).reshape(all_rows, model_width)
    inner, grad_gate, grad_up = hidden_units(second_normal, grad_out, second_whole)
    second_grads = None
    for at, (left, right) in enumerate(
        ((second_normal, grad_gate), (second_normal, grad_up), (grad_out, inner))
    ):
        second_grads = grads_into(
            second_grads, 3 * hidden, at * hidden, left, right, False, 256
        )
    inner, second_grads = lax.optimization_barrier((inner, second_grads))
    second_share = lax.psum_scatter(second_grads, shards, scatter_dimension=0, tiled=True)
    normal_part, mixed_part = leave(inner, grad_gate, grad_up, second_whole)

    back, grad_projected, second_gain = back_one(
        normal_part,
        mixed_part,
        residual,
        grad_out,
        gains,
        first_whole,
        queries,
        key_values,
        attended_full,
        log_total,
        where,
        ctx_size,
        tp_size,
        4,
    )
    grad_residual_low = back[:all_rows]
    mixed = back[all_rows:]
    first_grads = first_grads_of(
        first_normal, grad_projected, grad_residual_low, attended
    )
    grad_projected, first_grads, second_share = lax.optimization_barrier(
        (grad_projected, first_grads, second_share)
    )
    first_share = lax.psum_scatter(first_grads, shards, scatter_dimension=0, tiled=True)
    input_grad, first_gain = back_two(
        grad_projected,
        first_whole,
        token_rows,
        grad_residual_low,
        gains,
        out_width,
        seqs,
        tp_size,
        5,
    )
    gain_share = gain_sum(
        jnp.stack([first_gain.sum(0), second_gain.sum(0)]),
        lax.axis_size("fsdp") * ctx_size,
        ctx_size,
        tp_size,
        7,
    )

    gradients = (
        first_share[:, out_width:],
        first_share[:, :out_width].T,
        second_share[:, : 2 * hidden],
        second_share[:, 2 * hidden :].T,
        gain_share,
    )
    masters = (attention_input_weight, attend_out, gate_up, down_weight, norm_gains)
    firsts = (
        attention_input_first,
        attend_out_moment,
        gate_up_moment,
        down_weight_moment,
        norm_gains_moment,
    )
    seconds = (
        attention_input_squared,
        attend_out_second,
        gate_up_second,
        down_weight_second,
        norm_gains_second,
    )
    results = [mixed.reshape(tokens.shape), input_grad.reshape(tokens.shape).astype(jnp.float32)]
    for at in range(5):
        updated = adam_update(
            masters[at],
            firsts[at],
            seconds[at],
            gradients[at].astype(jnp.float32),
            learn_rates[at],
            decay_flags[at],
        )
        results.extend(updated)
        if at < 4:
            results.append(updated[2].astype(low))
    return tuple(results)


def solution(mesh):
    rows = P(None, "fsdp", "ctx", None)
    upper = P(("fsdp", "ctx"), "tp")
    lower = P("tp", ("fsdp", "ctx"))
    gain = P(None, ("fsdp", "ctx"))
    return jax.shard_map(
        on_device,
        mesh=mesh,
        in_specs=(rows, rows, P(None, "fsdp"), P(None, "fsdp", None))
        + (upper,) * 3
        + (lower,) * 3
        + (upper,) * 3
        + (lower,) * 3
        + (gain,) * 3,
        out_specs=(rows, rows)
        + (upper,) * 4
        + (lower,) * 4
        + (upper,) * 4
        + (lower,) * 4
        + (gain,) * 3,
        check_vma=False,
    )
```

```python
import functools

import jax
import jax.numpy as jnp
from jax import lax
from jax.experimental import pallas as pl
from jax.experimental.pallas import tpu as pltpu
from jax.sharding import PartitionSpec as P

QUERY_HEADS = 32
KEY_VALUE_HEADS = 8
HEAD_DIMENSION = 80
STEP = 10
GROUP = QUERY_HEADS // KEY_VALUE_HEADS

rope_base = 1000000.0
norm_eps = 1e-05
beta_one = 0.9
beta_two = 0.95
adam_eps = 1e-08
weight_decay = 0.1
learn_rates = (0.1, 0.5, 0.05, 0.04, 0.8)
decay_flags = (1.0, 1.0, 1.0, 1.0, 0.0)
neg_big = -1e30
log2_e = 1.4426950408889634
MESH = pl.DeviceIdType.MESH
VMEM = pltpu.VMEM
CHUNK = 16
LAG = 2


def adam_update(weight, moment, second, gradient, learn_rate, decay_flag):
    moment = beta_one * moment + (1.0 - beta_one) * gradient
    second = beta_two * second + (1.0 - beta_two) * gradient * gradient
    moment_hat = moment / (1.0 - beta_one**STEP)
    second_hat = second / (1.0 - beta_two**STEP)
    weight = weight - learn_rate * (
        moment_hat / (jnp.sqrt(second_hat) + adam_eps) + decay_flag * weight_decay * weight
    )
    return (moment, second, weight)


def line_greet(n, z):
    barrier = pltpu.get_barrier_semaphore()

    @pl.when(z > 0)
    def _():
        pl.semaphore_signal(barrier, inc=1, device_id={"tp": z - 1}, device_id_type=MESH)

    @pl.when(z < n - 1)
    def _():
        pl.semaphore_signal(barrier, inc=1, device_id={"tp": z + 1}, device_id_type=MESH)

    return (z > 0).astype(jnp.int32) + (z < n - 1).astype(jnp.int32)


class Line:
    def __init__(self, n, z, segments, segment_rows, parts, inbox, out, sems, finish):
        self.n, self.z = n, z
        self.segment_rows = segment_rows
        self.per_segment = segment_rows // (2 * CHUNK)
        self.chunks = segments * self.per_segment
        self.parts, self.inbox, self.out = parts, inbox, out
        self.red_send, self.red_recv, self.back_send, self.back_recv = sems
        self.finish = finish
        self.ticks = self.chunks + 2 * (n - 1) * LAG

    def ready(self, segments):
        return segments * self.per_segment + 2 * (self.n - 1) * LAG

    def rows(self, flow, g):
        start = (
            (g // self.per_segment) * self.segment_rows
            + flow * (self.segment_rows // 2)
            + (g % self.per_segment) * CHUNK
        )
        return pl.ds(pl.multiple_of(start, CHUNK), CHUNK)

    def hop(self, flow):
        return (self.n - 1 - self.z) if flow == 0 else self.z

    def neighbour(self, up):
        z = jnp.minimum(self.z + 1, self.n - 1) if up else jnp.maximum(self.z - 1, 0)
        return {"tp": z}

    def reduce_copy(self, flow, g, source):
        return pltpu.make_async_remote_copy(
            src_ref=source,
            dst_ref=self.inbox.at[self.rows(flow, g)],
            send_sem=self.red_send.at[flow, g],
            recv_sem=self.red_recv.at[flow, g],
            device_id=self.neighbour(flow == 1),
            device_id_type=MESH,
        )

    def back_copy(self, flow, g):
        rows = self.rows(flow, g)
        return pltpu.make_async_remote_copy(
            src_ref=self.out.at[rows],
            dst_ref=self.out.at[rows],
            send_sem=self.back_send.at[flow, g],
            recv_sem=self.back_recv.at[flow, g],
            device_id=self.neighbour(flow == 0),
            device_id_type=MESH,
        )

    def tick(self, t):
        n = self.n
        for flow in (0, 1):
            hop = self.hop(flow)
            g = t - hop * LAG

            @pl.when((g >= 0) & (g < self.chunks))
            def _():
                rows = self.rows(flow, g)

                @pl.when(hop == 0)
                def _():
                    self.reduce_copy(flow, g, self.parts.at[rows]).start()

                @pl.when(hop > 0)
                def _():
                    self.reduce_copy(flow, g, self.parts.at[rows]).wait_recv()
                    total = self.inbox[rows, :].astype(jnp.float32) + self.parts[rows, :].astype(
                        jnp.float32
                    )

                    @pl.when(hop < n - 1)
                    def _():
                        self.inbox[rows, :] = total.astype(jnp.bfloat16)
                        self.reduce_copy(flow, g, self.inbox.at[rows]).start()

                    @pl.when(hop == n - 1)
                    def _():
                        self.finish(g // self.per_segment, rows, total)
                        self.back_copy(flow, g).start()

        for flow in (0, 1):
            hop = self.hop(flow)
            back = t - (n - 1) * LAG - (n - 1 - hop) * LAG

            @pl.when((back >= 0) & (back < self.chunks) & (hop < n - 1))
            def _():
                self.back_copy(flow, back).wait_recv()

                @pl.when(hop > 0)
                def _():
                    self.back_copy(flow, back).start()

    def run(self, first, last):
        def step(t, carry):
            self.tick(t)
            return carry

        lax.fori_loop(first, last, step, 0)

    def drain(self):
        def step(g, carry):
            for flow in (0, 1):
                hop = self.hop(flow)

                @pl.when(hop < self.n - 1)
                def _():
                    self.reduce_copy(flow, g, self.parts.at[self.rows(flow, g)]).wait_send()

                @pl.when(hop > 0)
                def _():
                    self.back_copy(flow, g).wait_send()

            return carry

        lax.fori_loop(0, self.chunks, step, 0)


def line_scratch(rows, width, segments, segment_rows):
    chunks = segments * (segment_rows // (2 * CHUNK))
    return [VMEM((rows, width), jnp.bfloat16)] + [pltpu.SemaphoreType.DMA((2, chunks))] * 4


def line_cost(rows, width):
    return pl.CostEstimate(flops=rows * width, bytes_accessed=80 * rows * width, transcendentals=0)


def mean_of(values):
    return jnp.mean(values, axis=-1, keepdims=True)


def norm_back(total, values, gain, gain_sums):
    root = lax.rsqrt(mean_of(values * values) + norm_eps)
    standard = values * root
    terms = total * standard
    gain_sums[...] += functools.reduce(
        lambda a, b: a + b, [terms[low : low + 8] for low in range(0, CHUNK, 8)]
    )
    scaled = total * gain
    return root * (scaled - standard * mean_of(scaled * standard))


def turn(first, second, cosine, sine):
    return jnp.concatenate([first * cosine - second * sine, second * cosine + first * sine], 0)


def turn_back(first, second, cosine, sine):
    return jnp.concatenate([first * cosine + second * sine, second * cosine - first * sine], 0)


def fill_bias(bias, order_ref, length_ref, m, me, n):
    rows = bias.shape[1]
    span = rows // 2
    lane = lax.broadcasted_iota(jnp.int32, (1, rows), 1)
    query = jnp.where(
        lane < span,
        order_ref[m, 2 * me] * span + lane,
        order_ref[m, 2 * me + 1] * span + lane - span,
    )
    within = lax.broadcasted_iota(jnp.int32, (span, rows), 0)
    for block in range(2 * n):
        key = order_ref[m, block] * span + within
        allowed = (key <= query) & (key < length_ref[m])
        bias[block * span : (block + 1) * span, :] = jnp.where(allowed, 0.0, neg_big)


def cut(rows, parts):
    tiles = rows // 16
    ends = [tiles * i // parts * 16 for i in range(parts + 1)]
    return [(low, high - low) for low, high in zip(ends[:-1], ends[1:])]


class Gather:
    def __init__(self, source, whole, low, length, block_rows, fsdp, n, sems):
        self.source, self.whole = source, whole
        self.low, self.length, self.block_rows = low, length, block_rows
        self.fsdp, self.n = fsdp, n
        self.f, self.me = lax.axis_index("fsdp"), lax.axis_index("ctx")
        self.across = lax.rem(self.me + n // 2, n)
        self.other = self.me + 1 - 2 * lax.rem(self.me, 2)
        self.sems = sems
        self.first = max(16, min(length - 16, length * 6 // 160 * 16))

    def at(self, f, ctx, low=0, length=None):
        start = (f * self.n + ctx) * self.block_rows + self.low + low
        return self.whole.at[
            pl.ds(pl.multiple_of(start, 16), self.length if length is None else length)
        ]

    def copy(self, kind, source, target, where):
        return pltpu.make_async_remote_copy(
            src_ref=source,
            dst_ref=target,
            send_sem=self.sems.at[0, kind],
            recv_sem=self.sems.at[1, kind],
            device_id=where,
            device_id_type=MESH,
        )

    def own(self):
        return self.source.at[pl.ds(self.low, self.length)]

    def ahead(self, j):
        return lax.rem(self.f + j, self.fsdp)

    def behind(self, j):
        return lax.rem(self.f + self.fsdp - j, self.fsdp)

    def to_across(self):
        return self.copy(0, self.own(), self.at(self.f, self.me), {"ctx": self.across})

    def to_other(self):
        return self.copy(1, self.own(), self.at(self.f, self.me), {"ctx": self.other})

    def across_to_other(self):
        at = self.at(self.f, self.across)
        return self.copy(2, at, at, {"ctx": self.other})

    def to_ahead(self, j):
        return self.copy(3 * j, self.own(), self.at(self.f, self.me), {"fsdp": self.ahead(j)})

    def behind_to_other(self, j):
        at = self.at(self.behind(j), self.me)
        return self.copy(3 * j + 1, at, at, {"ctx": self.other})

    def corner_to_other(self, j):
        at = self.at(self.behind(j), self.across)
        return self.copy(3 * j + 2, at, at, {"ctx": self.other})

    def across_to_ahead(self, j):
        at = self.at(self.f, self.across, 0, self.first)
        return self.copy(3 * self.fsdp + 2 * j - 2, at, at, {"fsdp": self.ahead(j)})

    def behind_to_across(self, j):
        at = self.at(self.behind(j), self.me, self.first, self.length - self.first)
        return self.copy(3 * self.fsdp + 2 * j - 1, at, at, {"ctx": self.across})

    def local(self):
        return pltpu.make_async_copy(self.own(), self.at(self.f, self.me), self.sems.at[2, 0])

    def start(self):
        self.start_across()
        self.start_ahead()

    def start_across(self):
        self.to_across().start()

    def start_ahead(self):
        for j in range(1, self.fsdp):
            self.to_ahead(j).start()
        self.to_other().start()
        self.local().start()

    def forward(self):
        self.forward_across()
        self.forward_behind()

    def forward_across(self):
        self.to_across().wait_recv()
        for j in range(1, self.fsdp):
            self.across_to_ahead(j).start()
        self.across_to_other().start()

    def forward_behind(self):
        for j in range(1, self.fsdp):
            self.to_ahead(j).wait_recv()
            self.behind_to_across(j).start()
            self.behind_to_other(j).start()

    def corner(self):
        for j in range(1, self.fsdp):
            self.across_to_ahead(j).wait_recv()
            self.behind_to_across(j).wait_recv()
            self.corner_to_other(j).start()

    def finish(self):
        self.local().wait()
        self.to_other().wait_recv()
        self.across_to_other().wait_recv()
        for j in range(1, self.fsdp):
            self.behind_to_other(j).wait_recv()
            self.corner_to_other(j).wait_recv()

    def drain(self):
        self.to_across().wait_send()
        self.to_other().wait_send()
        self.across_to_other().wait_send()
        for j in range(1, self.fsdp):
            self.to_ahead(j).wait_send()
            self.behind_to_other(j).wait_send()
            self.corner_to_other(j).wait_send()
            self.across_to_ahead(j).wait_send()
            self.behind_to_across(j).wait_send()


def gather_sems(fsdp):
    return pltpu.SemaphoreType.DMA((3, 5 * fsdp - 2))


def front_body(
    n,
    tp,
    fsdp,
    groups,
    token_ref,
    in_ref,
    tail_ref,
    out_weight_ref,
    gate_up_ref,
    down_ref,
    cos_ref,
    sin_ref,
    order_ref,
    length_ref,
    in_whole_ref,
    out_whole_ref,
    pair_whole_ref,
    normal_out_ref,
    gain_ref,
    q_ref,
    kv_ref,
    full_ref,
    low_ref,
    log_ref,
    residual_ref,
    out_ref,
    in_whole,
    out_whole,
    normal_ref,
    in_pack,
    out_pack,
    pair_pack,
    staged,
    proj,
    bias,
    parts,
    load_sem,
    save_sem,
    send_sem,
    recv_sem,
    in_sems,
    out_sems,
    pair_sems,
    inbox,
    *sems,
):
    z = lax.axis_index("tp")
    f = lax.axis_index("fsdp")
    me = lax.axis_index("ctx")
    peers = line_greet(tp, z)
    barrier = pltpu.get_barrier_semaphore()
    for step in range(1, n):
        pl.semaphore_signal(
            barrier, inc=1, device_id={"ctx": lax.rem(me + step, n)}, device_id_type=MESH
        )
    for step in range(1, fsdp):
        pl.semaphore_signal(
            barrier, inc=1, device_id={"fsdp": lax.rem(f + step, fsdp)}, device_id_type=MESH
        )

    seqs, _, rows = q_ref.shape
    dim = HEAD_DIMENSION
    half = dim // 2
    group_width = (GROUP + 2) * dim
    in_width = groups * group_width
    heads = groups * GROUP
    width = token_ref.shape[1]
    tile = 512 if width % 512 == 0 else width
    block = in_ref.shape[0]
    pair_width = gate_up_ref.shape[1]
    whole_tiles = in_width // 128 * 128

    ranges = cut(block, pair_sems.shape[0])

    def loads(i):
        low, length = ranges[i]
        return [
            pltpu.make_async_copy(
                source.at[pl.ds(low, length)],
                staged.at[i % 2, pl.ds(0, length), pl.ds(first, source.shape[1])],
                load_sem.at[i % 2, at],
            )
            for at, (source, first) in enumerate(((gate_up_ref, 0), (down_ref, pair_width)))
        ]

    for load in loads(0):
        load.start()
    in_pack[:, :whole_tiles] = in_ref[:, :whole_tiles].astype(jnp.bfloat16)
    in_pack[:, whole_tiles:] = tail_ref[...]
    out_pack[...] = out_weight_ref[...].astype(jnp.bfloat16)
    pl.semaphore_wait(barrier, peers + n - 1 + fsdp - 1)

    def gathers(source, whole, sems):
        return [
            Gather(source, whole, low, length, block, fsdp, n, sems.at[i])
            for i, (low, length) in enumerate(cut(block, sems.shape[0]))
        ]

    first = gathers(in_pack, in_whole, in_sems)
    outer = gathers(out_pack, out_whole, out_sems)
    pair = gathers(pair_pack, pair_whole_ref, pair_sems)
    for piece in first:
        piece.start()
    for i, (low, length) in enumerate(ranges):
        if i + 1 < len(ranges):
            for load in loads(i + 1):
                load.start()
        for load in loads(i):
            load.wait()
        pair_pack[low : low + length, :] = staged[i % 2, :length, :].astype(jnp.bfloat16)
    for piece in first:
        piece.forward()
    for piece in outer:
        piece.start()
    for piece in first:
        piece.corner()
    for piece in first:
        piece.finish()
    for piece in outer:
        piece.forward()
    for piece in pair:
        piece.start_ahead()
    saves = [
        pltpu.make_async_copy(in_whole, in_whole_ref, save_sem.at[0]),
        pltpu.make_async_copy(normal_ref, normal_out_ref, save_sem.at[1]),
        pltpu.make_async_copy(out_whole, out_whole_ref, save_sem.at[2]),
    ]
    saves[0].start()

    turned = in_whole[:, whole_tiles : whole_tiles + 128].astype(jnp.float32).T
    gain_ref[...] = turned[in_width - whole_tiles : in_width - whole_tiles + 8]

    def columns_of(m):
        return pl.ds(pl.multiple_of(m * rows, 128), rows)

    def rows_of(m):
        return pl.ds(pl.multiple_of(m * rows, CHUNK), rows)

    def copy(m, step):
        return pltpu.make_async_remote_copy(
            src_ref=kv_ref.at[m, me],
            dst_ref=kv_ref.at[m, me],
            send_sem=send_sem.at[m, step - 1],
            recv_sem=recv_sem.at[m, step - 1],
            device_id={"ctx": lax.rem(me + step, n)},
            device_id_type=MESH,
        )

    def project(m, carry):
        values = token_ref[rows_of(m), :].astype(jnp.float32)
        root = lax.rsqrt(mean_of(values * values) + norm_eps)
        normal_ref[rows_of(m), :] = (values * root * gain_ref[0:1, :]).astype(jnp.bfloat16)
        proj[m] = jnp.dot(
            normal_ref[rows_of(m), :],
            in_whole[:, :in_width],
            preferred_element_type=jnp.float32,
        ).T
        for g in range(groups):
            col = g * group_width + GROUP * dim
            kv_ref[m, me, g, :dim, :] = turn(
                proj[m, col : col + half, :],
                proj[m, col + half : col + dim, :],
                cos_ref[m],
                sin_ref[m],
            ).astype(jnp.bfloat16)
            kv_ref[m, me, g, dim:, :] = proj[m, col + dim : col + 2 * dim, :].astype(jnp.bfloat16)
        for step in range(1, n):
            copy(m, step).start()
        return carry

    lax.fori_loop(0, seqs, project, 0)
    for piece in pair:
        piece.start_across()
    saves[1].start()

    def finish(segment, at, total):
        values = token_ref[at, :].astype(jnp.float32) + total
        residual_ref[at, :] = values.astype(jnp.bfloat16)
        root = lax.rsqrt(mean_of(values * values) + norm_eps)
        out_ref[at, :] = (values * root * gain_ref[1:2, :]).astype(jnp.bfloat16)

    line = Line(tp, z, seqs, rows, parts, inbox, out_ref, sems, finish)

    def head(m, at):
        g = at // GROUP
        h = at % GROUP
        low = pl.ds(pl.multiple_of(at * dim, 16), dim)
        col = pl.multiple_of(g * group_width + h * dim, 8)
        query = turn(
            proj[m, pl.ds(col, half), :],
            proj[m, pl.ds(pl.multiple_of(col + half, 8), half), :],
            cos_ref[m],
            sin_ref[m],
        ).astype(jnp.bfloat16)
        q_ref[m, low, :] = query
        scores = [
            lax.dot_general(
                kv_ref[m, j, g, :dim, :],
                query,
                (((0,), (0,)), ((), ())),
                preferred_element_type=jnp.float32,
            )
            * (log2_e * dim**-0.5)
            + bias[j * rows : (j + 1) * rows, :]
            for j in range(n)
        ]
        top = functools.reduce(jnp.maximum, [jnp.max(s, axis=0, keepdims=True) for s in scores])
        total = jnp.zeros_like(top)
        out = jnp.zeros((dim, rows), jnp.float32)
        for j in range(n):
            weights = jnp.exp2(scores[j] - top)
            total += jnp.sum(weights, axis=0, keepdims=True)
            out += jnp.dot(
                kv_ref[m, j, g, dim:, :],
                weights.astype(jnp.bfloat16),
                preferred_element_type=jnp.float32,
            )
        out = out / total
        full_ref[m, low, :] = out
        low_ref[low, columns_of(m)] = out.astype(jnp.bfloat16)
        log_ref[m, at] = top + jnp.log2(total)

    def ready(m):
        fill_bias(bias, order_ref, length_ref, m, me, n)
        for step in range(1, n):
            copy(m, step).wait_recv()

    def product(m):
        left = low_ref[:, columns_of(m)].T
        for low in range(0, width, tile):
            parts[rows_of(m), low : low + tile] = lax.dot_general(
                left,
                out_whole[low : low + tile, :],
                (((1,), (1,)), ((), ())),
                preferred_element_type=jnp.float32,
            ).astype(jnp.bfloat16)

    def sequence(m, carry):
        ready(m)

        def item(at, inner):
            line.tick((m - 1) * heads + at)
            head(m, at)
            return inner

        lax.fori_loop(0, heads, item, 0)
        product(m)
        return carry

    def opening(at, carry):
        head(0, at)
        return carry

    ready(0)
    lax.fori_loop(0, heads, opening, 0)
    for piece in outer:
        piece.corner()
    for piece in outer:
        piece.finish()
    saves[2].start()
    product(0)
    pair[0].forward_behind()
    lax.fori_loop(1, 2, sequence, 0)
    for piece in pair[1:2]:
        piece.forward_behind()
    lax.fori_loop(2, seqs, sequence, 0)
    at = (seqs - 1) * heads
    for piece in pair[2:3]:
        piece.forward_behind()
    pair[0].forward_across()
    line.run(at, at + 2)
    for piece in pair[3:]:
        piece.forward_behind()
    line.run(at + 2, at + 4)
    for piece in pair[1:2]:
        piece.forward_across()
    line.run(at + 4, at + 10)
    for piece in pair[2:3]:
        piece.forward_across()
    line.run(at + 10, at + 16)
    for piece in pair[3:]:
        piece.forward_across()
    line.run(at + 16, line.ticks)
    for piece in pair:
        piece.corner()
    for piece in pair:
        piece.finish()
    line.drain()
    for piece in first + outer + pair:
        piece.drain()
    for save in saves:
        save.wait()

    def drain(m, carry):
        for step in range(1, n):
            copy(m, step).wait_send()
        return carry

    lax.fori_loop(0, seqs, drain, 0)


def front(
    tokens, in_weight, tail, out_weight, gate_up, down, where, seqs, n, tp, fsdp, ident
):
    all_rows, model_width = tokens.shape
    rows = all_rows // seqs
    block, in_width = in_weight.shape
    groups = in_width // ((GROUP + 2) * HEAD_DIMENSION)
    heads = groups * GROUP
    shards = n * fsdp
    dim = HEAD_DIMENSION
    padded = in_width // 128 * 128 + tail.shape[1]
    out_width = out_weight.shape[1]
    pair_width = gate_up.shape[1] + down.shape[1]
    pieces = min(4, block // 32)
    longest = max(length for _, length in cut(block, pieces))
    shape = jax.ShapeDtypeStruct
    low, wide = jnp.bfloat16, jnp.float32
    vmem = pl.BlockSpec(memory_space=VMEM)
    hbm = pl.BlockSpec(memory_space=pl.ANY)
    smem = pl.BlockSpec(memory_space=pltpu.SMEM)
    dma = pltpu.SemaphoreType.DMA
    gather_sems = (3, 5 * fsdp - 2)
    return pl.pallas_call(
        functools.partial(front_body, n, tp, fsdp, groups),
        out_shape=(
            shape((shards * block, padded), low),
            shape((shards * block, out_width), low),
            shape((shards * block, pair_width), low),
            shape((all_rows, model_width), low),
            shape((8, model_width), wide),
            shape((seqs, heads * dim, rows), low),
            shape((seqs, n, groups, 2 * dim, rows), low),
            shape((seqs, heads * dim, rows), wide),
            shape((heads * dim, all_rows), low),
            shape((seqs, heads, 1, rows), wide),
            shape((all_rows, model_width), low),
            shape((all_rows, model_width), low),
        ),
        in_specs=[vmem] * 4 + [hbm] * 2 + [vmem] * 2 + [smem] * 2,
        out_specs=(hbm,) * 4 + (vmem,) * 8,
        scratch_shapes=[
            VMEM((shards * block, padded), low),
            VMEM((shards * block, out_width), low),
            VMEM((all_rows, model_width), low),
            VMEM((block, padded), low),
            VMEM((block, out_width), low),
            VMEM((block, pair_width), low),
            VMEM((2, longest, pair_width), wide),
            VMEM((seqs, in_width, rows), wide),
            VMEM((n * rows, rows), wide),
            VMEM((all_rows, model_width), low),
            dma((2, 2)),
            dma((3,)),
            dma((seqs, n - 1)),
            dma((seqs, n - 1)),
            dma((min(2, pieces),) + gather_sems),
            dma((1,) + gather_sems),
            dma((pieces,) + gather_sems),
        ]
        + line_scratch(all_rows, model_width, seqs, rows),
        compiler_params=pltpu.CompilerParams(
            collective_id=ident, has_side_effects=True, vmem_limit_bytes=60 * 2**20
        ),
        cost_estimate=line_cost(all_rows, model_width),
        name="front",
    )(tokens, in_weight, tail, out_weight, gate_up, down, *where)


def back_one_body(
    n,
    tp,
    groups,
    late,
    normal_ref,
    mixed_ref,
    residual_ref,
    grad_out_ref,
    gain_ref,
    weight_ref,
    q_ref,
    kv_ref,
    full_ref,
    log_ref,
    cos_ref,
    sin_ref,
    order_ref,
    length_ref,
    out_ref,
    proj_ref,
    gain_sums,
    parts,
    out_proj,
    grads,
    sums,
    bias,
    outbox,
    kv_inbox,
    load_sem,
    send_sem,
    recv_sem,
    inbox,
    *sems,
):
    z = lax.axis_index("tp")
    me = lax.axis_index("ctx")
    seqs, _, rows = q_ref.shape
    all_rows = seqs * rows
    loads = [
        pltpu.make_async_copy(normal_ref, parts.at[pl.ds(0, all_rows)], load_sem.at[0]),
        pltpu.make_async_copy(
            mixed_ref, parts.at[pl.ds(all_rows, late * rows)], load_sem.at[1]
        ),
        pltpu.make_async_copy(
            weight_ref.at[:, pl.ds(0, out_proj.shape[1])], out_proj, load_sem.at[2]
        ),
    ]
    for load in loads:
        load.start()
    peers = line_greet(tp, z)
    barrier = pltpu.get_barrier_semaphore()
    for step in range(1, n):
        pl.semaphore_signal(
            barrier, inc=1, device_id={"ctx": lax.rem(me + step, n)}, device_id_type=MESH
        )
    pl.semaphore_wait(barrier, peers + n - 1)

    dim = HEAD_DIMENSION
    half = dim // 2
    scale = dim**-0.5
    group_width = (GROUP + 2) * dim
    heads = groups * GROUP
    gain_sums[...] = jnp.zeros_like(gain_sums)

    def finish(segment, at, total):
        @pl.when(segment < seqs)
        def _():
            grad = norm_back(
                total, residual_ref[at, :].astype(jnp.float32), gain_ref[1:2, :], gain_sums
            )
            out_ref[at, :] = (grad_out_ref[at, :].astype(jnp.float32) + grad).astype(jnp.bfloat16)

        @pl.when(segment >= seqs)
        def _():
            start = pl.multiple_of(at.start - late * rows, CHUNK)
            out_ref[at, :] = (
                residual_ref[pl.ds(start, CHUNK), :].astype(jnp.float32) + total
            ).astype(jnp.bfloat16)

    line = Line(tp, z, seqs + late, rows, parts, inbox, out_ref, sems, finish)

    def copy(m, step):
        to = lax.rem(me + step, n)
        return pltpu.make_async_remote_copy(
            src_ref=outbox.at[m, to],
            dst_ref=kv_inbox.at[m, step - 1],
            send_sem=send_sem.at[m, step - 1],
            recv_sem=recv_sem.at[m, step - 1],
            device_id={"ctx": to},
            device_id_type=MESH,
        )

    def columns(m):
        return pl.ds(pl.multiple_of(m * rows, 128), rows)

    def attended_grads(m):
        grads[...] = (
            jnp.dot(
                out_ref[pl.ds(pl.multiple_of(m * rows, CHUNK), rows), :],
                out_proj[...],
                preferred_element_type=jnp.float32,
            )
            .T.astype(jnp.bfloat16)
        )
        fill_bias(bias, order_ref, length_ref, m, me, n)

    def head(m, at):
        g = at // GROUP
        h = at % GROUP
        low = pl.ds(pl.multiple_of(at * dim, 16), dim)
        query = q_ref[m, low, :]
        grad = grads[low, :]
        delta = jnp.sum(
            grad.astype(jnp.float32) * full_ref[m, low, :], axis=0, keepdims=True
        )
        log_total = log_ref[m, at]
        query_sum = jnp.zeros((dim, rows), jnp.float32)

        @pl.when(h == 0)
        def _():
            sums[...] = jnp.zeros_like(sums)

        for j in range(n):
            keys = kv_ref[m, j, g, :dim, :]
            values = kv_ref[m, j, g, dim:, :]
            scores = lax.dot_general(
                keys, query, (((0,), (0,)), ((), ())), preferred_element_type=jnp.float32
            )
            probs = jnp.exp2(
                scores * (log2_e * scale) + (bias[j * rows : (j + 1) * rows, :] - log_total)
            )
            grad_probs = lax.dot_general(
                values, grad, (((0,), (0,)), ((), ())), preferred_element_type=jnp.float32
            )
            grad_scores = (probs * (grad_probs - delta)).astype(jnp.bfloat16)
            query_sum += jnp.dot(keys, grad_scores, preferred_element_type=jnp.float32)
            sums[j, :dim, :] += lax.dot_general(
                query, grad_scores, (((1,), (1,)), ((), ())), preferred_element_type=jnp.float32
            )
            sums[j, dim:, :] += lax.dot_general(
                grad,
                probs.astype(jnp.bfloat16),
                (((1,), (1,)), ((), ())),
                preferred_element_type=jnp.float32,
            )
        query_sum = query_sum * scale
        col = pl.ds(pl.multiple_of(g * group_width + h * dim, 16), dim)
        proj_ref[col, columns(m)] = turn_back(
            query_sum[:half], query_sum[half:], cos_ref[m], sin_ref[m]
        ).astype(jnp.bfloat16)

        @pl.when(h == GROUP - 1)
        def _():
            for j in range(n):
                outbox[m, j, g, :dim, :] = (sums[j, :dim, :] * scale).astype(jnp.bfloat16)
                outbox[m, j, g, dim:, :] = sums[j, dim:, :].astype(jnp.bfloat16)

    def gather(m):
        for step in range(1, n):
            copy(m, step).wait_recv()
        for g in range(groups):
            total = outbox[m, me, g].astype(jnp.float32)
            for step in range(1, n):
                total += kv_inbox[m, step - 1, g].astype(jnp.float32)
            col = g * group_width + GROUP * dim
            proj_ref[col : col + dim, columns(m)] = turn_back(
                total[:half], total[half:dim], cos_ref[m], sin_ref[m]
            ).astype(jnp.bfloat16)
            proj_ref[col + dim : col + 2 * dim, columns(m)] = total[dim:].astype(jnp.bfloat16)
        for step in range(1, n):
            copy(m, step).wait_send()

    loads[0].wait()
    line.run(0, line.ready(1))
    loads[1].wait()
    loads[2].wait()

    def sequence(m, carry):
        first = line.ready(1) + m * (heads + 1)
        line.tick(first)
        attended_grads(m)

        def item(at, inner):
            line.tick(first + 1 + at)
            head(m, at)
            return inner

        lax.fori_loop(0, heads, item, 0)
        for step in range(1, n):
            copy(m, step).start()
        return carry

    lax.fori_loop(0, seqs, sequence, 0)
    line.run(line.ready(1) + seqs * (heads + 1), line.ticks)

    def collect(m, carry):
        gather(m)
        return carry

    lax.fori_loop(0, seqs, collect, 0)
    line.drain()


def back_one(
    normal_part,
    mixed_part,
    residual,
    grad_out,
    gains,
    out_whole,
    queries,
    key_values,
    full,
    log_total,
    where,
    n,
    tp,
    ident,
):
    seqs, width, rows = queries.shape
    groups = key_values.shape[2]
    all_rows, model_width = normal_part.shape
    late = mixed_part.shape[0] // rows
    line_rows = all_rows + late * rows
    vmem = pl.BlockSpec(memory_space=VMEM)
    hbm = pl.BlockSpec(memory_space=pl.ANY)
    smem = pl.BlockSpec(memory_space=pltpu.SMEM)
    shape = jax.ShapeDtypeStruct
    return pl.pallas_call(
        functools.partial(back_one_body, n, tp, groups, late),
        out_shape=(
            shape((line_rows, model_width), jnp.bfloat16),
            shape((groups * (GROUP + 2) * HEAD_DIMENSION, all_rows), jnp.bfloat16),
            shape((8, model_width), jnp.float32),
        ),
        in_specs=[hbm, hbm, vmem, vmem, vmem, hbm] + [vmem] * 6 + [smem] * 2,
        out_specs=(vmem,) * 3,
        scratch_shapes=[
            VMEM((line_rows, model_width), jnp.bfloat16),
            VMEM((model_width, width), jnp.bfloat16),
            VMEM((width, rows), jnp.bfloat16),
            VMEM((n, 2 * HEAD_DIMENSION, rows), jnp.float32),
            VMEM((n * rows, rows), jnp.float32),
            VMEM((seqs, n, groups, 2 * HEAD_DIMENSION, rows), jnp.bfloat16),
            VMEM((seqs, n - 1, groups, 2 * HEAD_DIMENSION, rows), jnp.bfloat16),
            pltpu.SemaphoreType.DMA((3,)),
            pltpu.SemaphoreType.DMA((seqs, n - 1)),
            pltpu.SemaphoreType.DMA((seqs, n - 1)),
        ]
        + line_scratch(line_rows, model_width, seqs + late, rows),
        compiler_params=pltpu.CompilerParams(
            collective_id=ident, has_side_effects=True, vmem_limit_bytes=60 * 2**20
        ),
        cost_estimate=line_cost(line_rows, model_width),
        name="back_one",
    )(
        normal_part,
        mixed_part,
        residual,
        grad_out,
        gains,
        out_whole,
        queries,
        key_values,
        full,
        log_total,
        *where,
    )


def back_two_body(
    tp,
    seqs,
    skip,
    proj_ref,
    weight_ref,
    token_ref,
    residual_grad_ref,
    gain_ref,
    out_ref,
    gain_sums,
    parts,
    inbox,
    *sems,
):
    z = lax.axis_index("tp")
    pl.semaphore_wait(pltpu.get_barrier_semaphore(), line_greet(tp, z))
    gain_sums[...] = jnp.zeros_like(gain_sums)
    rows = token_ref.shape[0] // seqs
    width = weight_ref.shape[0]
    tile = 512 if width % 512 == 0 else width

    def finish(segment, at, total):
        values = token_ref[at, :].astype(jnp.float32)
        grad = norm_back(total, values, gain_ref[0:1, :], gain_sums)
        out_ref[at, :] = (residual_grad_ref[at, :].astype(jnp.float32) + grad).astype(jnp.bfloat16)

    line = Line(tp, z, seqs, rows, parts, inbox, out_ref, sems, finish)

    def product(m):
        left = proj_ref[:, m * rows : (m + 1) * rows].T
        for low in range(0, width, tile):
            parts[m * rows : (m + 1) * rows, low : low + tile] = lax.dot_general(
                left,
                weight_ref[low : low + tile, skip : skip + proj_ref.shape[0]],
                (((1,), (1,)), ((), ())),
                preferred_element_type=jnp.float32,
            ).astype(jnp.bfloat16)

    for m in range(seqs):
        product(m)
        line.run(2 * m, 2 * m + 2)
    line.run(2 * seqs, line.ticks)
    line.drain()


def back_two(projected, first_whole, tokens, residual_grad, gains, skip, seqs, tp, ident):
    rows, width = tokens.shape
    vmem = pl.BlockSpec(memory_space=VMEM)
    shape = jax.ShapeDtypeStruct
    return pl.pallas_call(
        functools.partial(back_two_body, tp, seqs, skip),
        out_shape=(shape((rows, width), jnp.bfloat16), shape((8, width), jnp.float32)),
        in_specs=[vmem] * 5,
        out_specs=(vmem,) * 2,
        scratch_shapes=[VMEM((rows, width), jnp.bfloat16)]
        + line_scratch(rows, width, seqs, rows // seqs),
        compiler_params=pltpu.CompilerParams(
            collective_id=ident, has_side_effects=True, vmem_limit_bytes=56 * 2**20
        ),
        cost_estimate=line_cost(rows, width),
        name="back_two",
    )(projected, first_whole, tokens, residual_grad, gains)


def hidden_body(
    normal_ref, grad_out_ref, gate_ref, up_ref, down_ref, inner_ref, grad_gate_ref, grad_up_ref
):
    def product(left, right):
        return jnp.dot(left[...], right[...], preferred_element_type=jnp.float32)

    gate = product(normal_ref, gate_ref)
    up = product(normal_ref, up_ref)
    grad_inner = product(grad_out_ref, down_ref)
    sigmoid = jax.nn.sigmoid(gate)
    silu = gate * sigmoid
    inner_ref[...] = (silu * up).astype(jnp.bfloat16)
    grad_gate_ref[...] = (
        grad_inner * up * sigmoid * (1.0 + gate * (1.0 - sigmoid))
    ).astype(jnp.bfloat16)
    grad_up_ref[...] = (grad_inner * silu).astype(jnp.bfloat16)


def hidden_units(normal, grad_out, whole, tile=256):
    rows, width = normal.shape
    columns = whole.shape[1]
    units = columns // 3
    steps = units // tile
    vmem = pl.BlockSpec(memory_space=VMEM)
    return pl.pallas_call(
        hidden_body,
        grid=(steps,),
        out_shape=(jax.ShapeDtypeStruct((rows, units), jnp.bfloat16),) * 3,
        in_specs=[vmem, vmem]
        + [
            pl.BlockSpec((width, tile), functools.partial(lambda k, i: (0, k * steps + i), k))
            for k in range(3)
        ],
        out_specs=[pl.BlockSpec((rows, tile), lambda i: (0, i))] * 3,
        compiler_params=pltpu.CompilerParams(vmem_limit_bytes=56 * 2**20),
        cost_estimate=pl.CostEstimate(
            flops=2 * rows * width * columns,
            bytes_accessed=2 * (rows + width) * columns,
            transcendentals=rows * units,
        ),
        name="hidden_units",
    )(normal, grad_out, whole, whole, whole)


def mid_body(
    tp,
    seqs,
    early,
    normal_ref,
    grad_out_ref,
    inner_ref,
    gate_ref,
    up_ref,
    residual_ref,
    whole_ref,
    grads_ref,
    normal_part,
    late_part,
    out_ref,
    residual,
    turned,
    staged,
    weights,
    parts,
    load_sem,
    weight_sem,
    store_sem,
    inbox,
    *sems,
):
    z = lax.axis_index("tp")
    load = pltpu.make_async_copy(
        residual_ref.at[pl.ds(0, residual.shape[0])], residual, load_sem.at[0]
    )
    load.start()
    rows, units = inner_ref.shape
    width = normal_ref.shape[1]
    tile = staged.shape[2]
    pieces = width // tile
    steps = units // tile
    early_rows = parts.shape[0]
    contract = (((1,), (1,)), ((), ()))

    def fetch(at, first, columns):
        slot = lax.rem(at, 2)
        return pltpu.make_async_copy(
            whole_ref.at[pl.ds(pl.multiple_of(at * tile, tile), tile), pl.ds(first, columns)],
            weights.at[slot, :, pl.ds(0, columns)],
            weight_sem.at[slot],
        )

    def columns_of(at):
        return pl.ds(pl.multiple_of(at * tile, tile), tile)

    fetch(0, 2 * units, units).start()
    pl.semaphore_wait(pltpu.get_barrier_semaphore(), line_greet(tp, z))

    def expand(at, carry):
        @pl.when(at + 1 < pieces)
        def _():
            fetch(at + 1, 2 * units, units).start()

        fetch(at, 2 * units, units).wait()
        part = lax.dot_general(
            inner_ref[...],
            weights[lax.rem(at, 2), :, :units],
            contract,
            preferred_element_type=jnp.float32,
        ).astype(jnp.bfloat16)
        parts[:, columns_of(at)] = part[:early_rows]
        late_part[:, columns_of(at)] = part[early_rows:]
        return carry

    lax.fori_loop(0, pieces, expand, 0)
    load.wait()
    fetch(0, 0, 2 * units).start()
    turned[...] = normal_ref[...].T

    def finish(segment, at, total):
        out_ref[at, :] = (residual[at, :].astype(jnp.float32) + total).astype(jnp.bfloat16)

    line = Line(tp, z, early, rows // seqs, parts, inbox, out_ref, sems, finish)

    def store(kind, at):
        return pltpu.make_async_copy(
            staged.at[lax.rem(kind * steps + at, 2)],
            grads_ref.at[:, columns_of(kind * steps + at)],
            store_sem.at[lax.rem(kind * steps + at, 2)],
        )

    for kind, right in enumerate((gate_ref, up_ref, inner_ref)):
        if kind == 2:
            turned[...] = grad_out_ref[...].T

        def gradient(at, carry):
            line.tick(kind * steps + at)

            @pl.when(kind * steps + at >= 2)
            def _():
                store(kind, at - 2).wait()

            staged[lax.rem(kind * steps + at, 2)] = jnp.dot(
                turned[...], right[:, columns_of(at)], preferred_element_type=jnp.float32
            ).astype(jnp.bfloat16)
            store(kind, at).start()
            return carry

        lax.fori_loop(0, steps, gradient, 0)

    def leave(at, carry):
        line.tick(3 * steps + at)

        @pl.when(at + 1 < pieces)
        def _():
            fetch(at + 1, 0, 2 * units).start()

        fetch(at, 0, 2 * units).wait()
        slot = lax.rem(at, 2)
        normal_part[:, columns_of(at)] = (
            lax.dot_general(
                gate_ref[...],
                weights[slot, :, :units],
                contract,
                preferred_element_type=jnp.float32,
            )
            + lax.dot_general(
                up_ref[...],
                weights[slot, :, units:],
                contract,
                preferred_element_type=jnp.float32,
            )
        ).astype(jnp.bfloat16)
        return carry

    lax.fori_loop(0, pieces, leave, 0)
    store(2, steps - 2).wait()
    store(2, steps - 1).wait()
    line.run(3 * steps + pieces, line.ticks)
    line.drain()


def mid(normal, grad_out, inner, grad_gate, grad_up, residual, whole, seqs, early, tp, ident):
    all_rows, width = normal.shape
    units = inner.shape[1]
    columns = whole.shape[1]
    rows = all_rows // seqs
    tile = 256
    low = jnp.bfloat16
    shape = jax.ShapeDtypeStruct
    vmem = pl.BlockSpec(memory_space=VMEM)
    hbm = pl.BlockSpec(memory_space=pl.ANY)
    return pl.pallas_call(
        functools.partial(mid_body, tp, seqs, early),
        out_shape=(
            shape((width, columns), low),
            shape((all_rows, width), low),
            shape(((seqs - early) * rows, width), low),
            shape((early * rows, width), low),
        ),
        in_specs=[vmem] * 5 + [hbm] * 2,
        out_specs=(hbm,) + (vmem,) * 3,
        scratch_shapes=[
            VMEM((early * rows, width), low),
            VMEM((width, all_rows), low),
            VMEM((2, width, tile), low),
            VMEM((2, tile, 2 * units), low),
            VMEM((early * rows, width), low),
            pltpu.SemaphoreType.DMA((1,)),
            pltpu.SemaphoreType.DMA((2,)),
            pltpu.SemaphoreType.DMA((2,)),
        ]
        + line_scratch(early * rows, width, early, rows),
        compiler_params=pltpu.CompilerParams(
            collective_id=ident, has_side_effects=True, vmem_limit_bytes=60 * 2**20
        ),
        cost_estimate=pl.CostEstimate(
            flops=4 * all_rows * width * columns,
            bytes_accessed=40 * all_rows * width,
            transcendentals=0,
        ),
        name="mid",
    )(normal, grad_out, inner, grad_gate, grad_up, residual, whole)


def first_grads_body(normal_ref, proj_ref, residual_ref, attended_ref, out_ref):
    width = out_ref.shape[0]
    split = attended_ref.shape[0]
    tile = 512 if width % 512 == 0 else width
    contract = (((1,), (1,)), ((), ()))
    for low in range(0, width, tile):
        out_ref[low : low + tile, :split] = lax.dot_general(
            residual_ref[: normal_ref.shape[0], low : low + tile].T,
            attended_ref[...],
            contract,
            preferred_element_type=jnp.float32,
        ).astype(jnp.bfloat16)
        out_ref[low : low + tile, split:] = lax.dot_general(
            normal_ref[:, low : low + tile].T,
            proj_ref[...],
            contract,
            preferred_element_type=jnp.float32,
        ).astype(jnp.bfloat16)


def first_grads_of(normal, projected, residual_grad, attended):
    rows, width = normal.shape
    columns = projected.shape[0] + attended.shape[0]
    vmem = pl.BlockSpec(memory_space=VMEM)
    return pl.pallas_call(
        first_grads_body,
        out_shape=jax.ShapeDtypeStruct((width, columns), jnp.bfloat16),
        in_specs=[vmem] * 4,
        out_specs=vmem,
        compiler_params=pltpu.CompilerParams(vmem_limit_bytes=48 * 2**20),
        cost_estimate=pl.CostEstimate(
            flops=2 * rows * width * columns,
            bytes_accessed=2 * (2 * rows * width + (rows + width) * columns),
            transcendentals=0,
        ),
        name="first_grads",
    )(normal, projected, residual_grad, attended)


def gain_body(ctx_size, tp, x_ref, o_ref, inbox, tp_inbox, send_sem, recv_sem, tp_send, tp_recv):
    shards = x_ref.shape[0]
    me = lax.axis_index("fsdp") * ctx_size + lax.axis_index("ctx")
    z = lax.axis_index("tp")

    def to(step):
        other = lax.rem(me + step, shards)
        return other, {"fsdp": other // ctx_size, "ctx": lax.rem(other, ctx_size)}

    barrier = pltpu.get_barrier_semaphore()
    for step in range(1, shards):
        pl.semaphore_signal(barrier, inc=1, device_id=to(step)[1], device_id_type=MESH)
    for step in range(1, tp):
        pl.semaphore_signal(
            barrier, inc=1, device_id={"tp": lax.rem(z + step, tp)}, device_id_type=MESH
        )
    pl.semaphore_wait(barrier, shards - 1 + tp - 1)

    def copy(step):
        other, where = to(step)
        return pltpu.make_async_remote_copy(
            src_ref=x_ref.at[other],
            dst_ref=inbox.at[step - 1],
            send_sem=send_sem.at[step - 1],
            recv_sem=recv_sem.at[step - 1],
            device_id=where,
            device_id_type=MESH,
        )

    def tp_copy(step):
        return pltpu.make_async_remote_copy(
            src_ref=tp_inbox.at[0],
            dst_ref=tp_inbox.at[step],
            send_sem=tp_send.at[step - 1],
            recv_sem=tp_recv.at[step - 1],
            device_id={"tp": lax.rem(z + step, tp)},
            device_id_type=MESH,
        )

    for step in range(1, shards):
        copy(step).start()
    total = x_ref[me]
    for step in range(1, shards):
        copy(step).wait()
        total += inbox[step - 1]
    tp_inbox[0] = total
    for step in range(1, tp):
        tp_copy(step).start()
    for step in range(1, tp):
        tp_copy(step).wait()
        total += tp_inbox[step]
    o_ref[...] = total


def gain_sum(partial, shards, ctx_size, tp, ident):
    two, width = partial.shape
    own = width // shards
    padded = -(-own // 128) * 128
    pieces = jnp.pad(
        partial.reshape(two, shards, own).transpose(1, 0, 2),
        ((0, 0), (0, 8 - two), (0, padded - own)),
    )
    total = pl.pallas_call(
        functools.partial(gain_body, ctx_size, tp),
        out_shape=jax.ShapeDtypeStruct((8, padded), jnp.float32),
        in_specs=[pl.BlockSpec(memory_space=VMEM)],
        out_specs=pl.BlockSpec(memory_space=VMEM),
        scratch_shapes=[
            VMEM((shards - 1, 8, padded), jnp.float32),
            VMEM((tp, 8, padded), jnp.float32),
            pltpu.SemaphoreType.DMA((shards - 1,)),
            pltpu.SemaphoreType.DMA((shards - 1,)),
            pltpu.SemaphoreType.DMA((tp - 1,)),
            pltpu.SemaphoreType.DMA((tp - 1,)),
        ],
        compiler_params=pltpu.CompilerParams(collective_id=ident, has_side_effects=True),
        name="gain_sum",
    )(pieces)
    return total[:two, :own]


def dot(spec, left, right):
    return jnp.einsum(spec, left, right, preferred_element_type=jnp.float32)


def on_device(
    tokens,
    out_cotangent,
    seq_lengths,
    span_order,
    attention_input_weight,
    attention_input_first,
    attention_input_squared,
    attend_out,
    attend_out_moment,
    attend_out_second,
    gate_up,
    gate_up_moment,
    gate_up_second,
    down_weight,
    down_weight_moment,
    down_weight_second,
    norm_gains,
    norm_gains_moment,
    norm_gains_second,
):
    low = jnp.bfloat16
    micro_count, slot_count, row_count, model_width = tokens.shape
    seqs = micro_count * slot_count
    ctx_size = lax.axis_size("ctx")
    tp_size = lax.axis_size("tp")
    sequence_length = row_count * ctx_size
    span_len = sequence_length // (2 * ctx_size)
    hidden = down_weight.shape[0]
    out_width = attend_out.shape[0]
    in_width = attention_input_weight.shape[1]
    shards = ("fsdp", "ctx")

    ahead = in_width // 128 * 128
    tail = jnp.concatenate([attention_input_weight[:, ahead:], norm_gains.T], 1).astype(low)
    tail = jnp.pad(tail, ((0, 0), (0, -tail.shape[1] % 128)))

    orders = span_order.reshape(seqs, 2 * ctx_size)
    lengths = seq_lengths.reshape(seqs)
    within = jnp.arange(sequence_length, dtype=jnp.int32)
    block_ids = jnp.arange(2 * ctx_size, dtype=jnp.int32)
    table = jnp.where(
        block_ids[None, None, :] == (within // span_len)[None, :, None], orders[:, None, :], 0
    )
    pos_all = jnp.sum(table, -1) * span_len + within % span_len
    pos_here = lax.dynamic_slice_in_dim(pos_all, lax.axis_index("ctx") * row_count, row_count, 1)
    half_width = HEAD_DIMENSION // 2
    inverse = rope_base ** (-(jnp.arange(half_width, dtype=jnp.float32) * 2.0 / HEAD_DIMENSION))
    angles = pos_here.astype(jnp.float32)[:, None, :] * inverse[None, :, None]
    cosine, sine = jnp.cos(angles), jnp.sin(angles)
    where = (cosine, sine, orders, lengths)

    all_rows = seqs * row_count
    token_rows = tokens.reshape(all_rows, model_width)
    (
        in_whole,
        out_whole,
        pair_whole,
        first_normal,
        gains,
        queries,
        key_values,
        attended_full,
        attended,
        log_total,
        residual,
        second_normal,
    ) = front(
        token_rows,
        attention_input_weight,
        tail,
        attend_out.T,
        gate_up,
        down_weight.T,
        where,
        seqs,
        ctx_size,
        tp_size,
        lax.axis_size("fsdp"),
        1,
    )

    keep = (pos_here < lengths[:, None]).astype(jnp.float32)[..., None]
    grad_out = out_cotangent.reshape(seqs, row_count, model_width).astype(jnp.float32) * keep
    grad_out = grad_out.astype(low).reshape(all_rows, model_width)
    inner, grad_gate, grad_up = hidden_units(second_normal, grad_out, pair_whole)
    early = seqs - 1
    second_grads, normal_part, mixed_part, mixed_early = mid(
        second_normal,
        grad_out,
        inner,
        grad_gate,
        grad_up,
        residual,
        pair_whole,
        seqs,
        early,
        tp_size,
        2,
    )
    second_share = lax.psum_scatter(second_grads, shards, scatter_dimension=0, tiled=True)

    back, grad_projected, second_gain = back_one(
        normal_part,
        mixed_part,
        residual,
        grad_out,
        gains,
        out_whole,
        queries,
        key_values,
        attended_full,
        log_total,
        where,
        ctx_size,
        tp_size,
        4,
    )
    mixed = jnp.concatenate([mixed_early, back[all_rows:]], 0)
    first_grads = first_grads_of(
        first_normal, grad_projected, back, attended
    )
    grad_projected, first_grads, second_share = lax.optimization_barrier(
        (grad_projected, first_grads, second_share)
    )
    first_share = lax.psum_scatter(first_grads, shards, scatter_dimension=0, tiled=True)
    input_grad, first_gain = back_two(
        grad_projected,
        in_whole,
        token_rows,
        back,
        gains,
        0,
        seqs,
        tp_size,
        5,
    )
    gain_share = gain_sum(
        jnp.stack([first_gain.sum(0), second_gain.sum(0)]),
        lax.axis_size("fsdp") * ctx_size,
        ctx_size,
        tp_size,
        7,
    )

    gradients = (
        first_share[:, out_width:],
        first_share[:, :out_width].T,
        second_share[:, : 2 * hidden],
        second_share[:, 2 * hidden :].T,
        gain_share,
    )
    masters = (attention_input_weight, attend_out, gate_up, down_weight, norm_gains)
    firsts = (
        attention_input_first,
        attend_out_moment,
        gate_up_moment,
        down_weight_moment,
        norm_gains_moment,
    )
    seconds = (
        attention_input_squared,
        attend_out_second,
        gate_up_second,
        down_weight_second,
        norm_gains_second,
    )
    results = [mixed.reshape(tokens.shape), input_grad.reshape(tokens.shape).astype(jnp.float32)]
    for at in range(5):
        updated = adam_update(
            masters[at],
            firsts[at],
            seconds[at],
            gradients[at].astype(jnp.float32),
            learn_rates[at],
            decay_flags[at],
        )
        results.extend(updated)
        if at < 4:
            results.append(updated[2].astype(low))
    return tuple(results)


def solution(mesh):
    rows = P(None, "fsdp", "ctx", None)
    upper = P(("fsdp", "ctx"), "tp")
    lower = P("tp", ("fsdp", "ctx"))
    gain = P(None, ("fsdp", "ctx"))
    return jax.shard_map(
        on_device,
        mesh=mesh,
        in_specs=(rows, rows, P(None, "fsdp"), P(None, "fsdp", None))
        + (upper,) * 3
        + (lower,) * 3
        + (upper,) * 3
        + (lower,) * 3
        + (gain,) * 3,
        out_specs=(rows, rows)
        + (upper,) * 4
        + (lower,) * 4
        + (upper,) * 4
        + (lower,) * 4
        + (gain,) * 3,
        check_vma=False,
    )
```

```python
import functools

import jax
import jax.numpy as jnp
from jax import lax
from jax.experimental import pallas as pl
from jax.experimental.pallas import tpu as pltpu
from jax.sharding import PartitionSpec as P

QUERY_HEADS = 32
KEY_VALUE_HEADS = 8
HEAD_DIMENSION = 80
STEP = 10
GROUP = QUERY_HEADS // KEY_VALUE_HEADS

rope_base = 1000000.0
norm_eps = 1e-05
beta_one = 0.9
beta_two = 0.95
adam_eps = 1e-08
weight_decay = 0.1
learn_rates = (0.1, 0.5, 0.05, 0.04, 0.8)
decay_flags = (1.0, 1.0, 1.0, 1.0, 0.0)
neg_big = -1e30
log2_e = 1.4426950408889634
MESH = pl.DeviceIdType.MESH
VMEM = pltpu.VMEM
CHUNK = 16
LAG = 2


def adam_update(weight, moment, second, gradient, learn_rate, decay_flag):
    moment = beta_one * moment + (1.0 - beta_one) * gradient
    second = beta_two * second + (1.0 - beta_two) * gradient * gradient
    moment_hat = moment / (1.0 - beta_one**STEP)
    second_hat = second / (1.0 - beta_two**STEP)
    weight = weight - learn_rate * (
        moment_hat / (jnp.sqrt(second_hat) + adam_eps) + decay_flag * weight_decay * weight
    )
    return (moment, second, weight)


def line_greet(n, z):
    barrier = pltpu.get_barrier_semaphore()

    @pl.when(z > 0)
    def _():
        pl.semaphore_signal(barrier, inc=1, device_id={"tp": z - 1}, device_id_type=MESH)

    @pl.when(z < n - 1)
    def _():
        pl.semaphore_signal(barrier, inc=1, device_id={"tp": z + 1}, device_id_type=MESH)

    return (z > 0).astype(jnp.int32) + (z < n - 1).astype(jnp.int32)


class Line:
    def __init__(self, n, z, segments, segment_rows, parts, inbox, out, sems, finish):
        self.n, self.z = n, z
        self.segment_rows = segment_rows
        self.per_segment = segment_rows // (2 * CHUNK)
        self.chunks = segments * self.per_segment
        self.parts, self.inbox, self.out = parts, inbox, out
        self.red_send, self.red_recv, self.back_send, self.back_recv = sems
        self.finish = finish
        self.ticks = self.chunks + 2 * (n - 1) * LAG

    def ready(self, segments):
        return segments * self.per_segment + 2 * (self.n - 1) * LAG

    def rows(self, flow, g):
        start = (
            (g // self.per_segment) * self.segment_rows
            + flow * (self.segment_rows // 2)
            + (g % self.per_segment) * CHUNK
        )
        return pl.ds(pl.multiple_of(start, CHUNK), CHUNK)

    def hop(self, flow):
        return (self.n - 1 - self.z) if flow == 0 else self.z

    def neighbour(self, up):
        z = jnp.minimum(self.z + 1, self.n - 1) if up else jnp.maximum(self.z - 1, 0)
        return {"tp": z}

    def reduce_copy(self, flow, g, source):
        return pltpu.make_async_remote_copy(
            src_ref=source,
            dst_ref=self.inbox.at[self.rows(flow, g)],
            send_sem=self.red_send.at[flow, g],
            recv_sem=self.red_recv.at[flow, g],
            device_id=self.neighbour(flow == 1),
            device_id_type=MESH,
        )

    def back_copy(self, flow, g):
        rows = self.rows(flow, g)
        return pltpu.make_async_remote_copy(
            src_ref=self.out.at[rows],
            dst_ref=self.out.at[rows],
            send_sem=self.back_send.at[flow, g],
            recv_sem=self.back_recv.at[flow, g],
            device_id=self.neighbour(flow == 0),
            device_id_type=MESH,
        )

    def tick(self, t):
        n = self.n
        for flow in (0, 1):
            hop = self.hop(flow)
            g = t - hop * LAG

            @pl.when((g >= 0) & (g < self.chunks))
            def _():
                rows = self.rows(flow, g)

                @pl.when(hop == 0)
                def _():
                    self.reduce_copy(flow, g, self.parts.at[rows]).start()

                @pl.when(hop > 0)
                def _():
                    self.reduce_copy(flow, g, self.parts.at[rows]).wait_recv()
                    total = self.inbox[rows, :].astype(jnp.float32) + self.parts[rows, :].astype(
                        jnp.float32
                    )

                    @pl.when(hop < n - 1)
                    def _():
                        self.inbox[rows, :] = total.astype(jnp.bfloat16)
                        self.reduce_copy(flow, g, self.inbox.at[rows]).start()

                    @pl.when(hop == n - 1)
                    def _():
                        self.finish(g // self.per_segment, rows, total)
                        self.back_copy(flow, g).start()

        for flow in (0, 1):
            hop = self.hop(flow)
            back = t - (n - 1) * LAG - (n - 1 - hop) * LAG

            @pl.when((back >= 0) & (back < self.chunks) & (hop < n - 1))
            def _():
                self.back_copy(flow, back).wait_recv()

                @pl.when(hop > 0)
                def _():
                    self.back_copy(flow, back).start()

    def run(self, first, last):
        def step(t, carry):
            self.tick(t)
            return carry

        lax.fori_loop(first, last, step, 0)

    def drain(self):
        def step(g, carry):
            for flow in (0, 1):
                hop = self.hop(flow)

                @pl.when(hop < self.n - 1)
                def _():
                    self.reduce_copy(flow, g, self.parts.at[self.rows(flow, g)]).wait_send()

                @pl.when(hop > 0)
                def _():
                    self.back_copy(flow, g).wait_send()

            return carry

        lax.fori_loop(0, self.chunks, step, 0)


def line_scratch(rows, width, segments, segment_rows):
    chunks = segments * (segment_rows // (2 * CHUNK))
    return [VMEM((rows, width), jnp.bfloat16)] + [pltpu.SemaphoreType.DMA((2, chunks))] * 4


def line_cost(rows, width):
    return pl.CostEstimate(flops=rows * width, bytes_accessed=80 * rows * width, transcendentals=0)


def mean_of(values):
    return jnp.mean(values, axis=-1, keepdims=True)


def norm_back(total, values, gain, gain_sums):
    root = lax.rsqrt(mean_of(values * values) + norm_eps)
    standard = values * root
    terms = total * standard
    gain_sums[...] += functools.reduce(
        lambda a, b: a + b, [terms[low : low + 8] for low in range(0, CHUNK, 8)]
    )
    scaled = total * gain
    return root * (scaled - standard * mean_of(scaled * standard))


def turn(first, second, cosine, sine):
    return jnp.concatenate([first * cosine - second * sine, second * cosine + first * sine], 0)


def turn_back(first, second, cosine, sine):
    return jnp.concatenate([first * cosine + second * sine, second * cosine - first * sine], 0)


def fill_bias(bias, order_ref, length_ref, m, me, n):
    rows = bias.shape[1]
    span = rows // 2
    lane = lax.broadcasted_iota(jnp.int32, (1, rows), 1)
    query = jnp.where(
        lane < span,
        order_ref[m, 2 * me] * span + lane,
        order_ref[m, 2 * me + 1] * span + lane - span,
    )
    within = lax.broadcasted_iota(jnp.int32, (span, rows), 0)
    for block in range(2 * n):
        key = order_ref[m, block] * span + within
        allowed = (key <= query) & (key < length_ref[m])
        bias[block * span : (block + 1) * span, :] = jnp.where(allowed, 0.0, neg_big)


def cut(rows, parts):
    tiles = rows // 16
    ends = [tiles * i // parts * 16 for i in range(parts + 1)]
    return [(low, high - low) for low, high in zip(ends[:-1], ends[1:])]


class Gather:
    def __init__(self, source, whole, low, length, block_rows, fsdp, n, sems):
        self.source, self.whole = source, whole
        self.low, self.length, self.block_rows = low, length, block_rows
        self.fsdp, self.n = fsdp, n
        self.f, self.me = lax.axis_index("fsdp"), lax.axis_index("ctx")
        self.across = lax.rem(self.me + n // 2, n)
        self.other = self.me + 1 - 2 * lax.rem(self.me, 2)
        self.sems = sems
        self.first = max(16, min(length - 16, length * 6 // 160 * 16))

    def at(self, f, ctx, low=0, length=None):
        start = (f * self.n + ctx) * self.block_rows + self.low + low
        return self.whole.at[
            pl.ds(pl.multiple_of(start, 16), self.length if length is None else length)
        ]

    def copy(self, kind, source, target, where):
        return pltpu.make_async_remote_copy(
            src_ref=source,
            dst_ref=target,
            send_sem=self.sems.at[0, kind],
            recv_sem=self.sems.at[1, kind],
            device_id=where,
            device_id_type=MESH,
        )

    def own(self):
        return self.source.at[pl.ds(self.low, self.length)]

    def ahead(self, j):
        return lax.rem(self.f + j, self.fsdp)

    def behind(self, j):
        return lax.rem(self.f + self.fsdp - j, self.fsdp)

    def to_across(self):
        return self.copy(0, self.own(), self.at(self.f, self.me), {"ctx": self.across})

    def to_other(self):
        return self.copy(1, self.own(), self.at(self.f, self.me), {"ctx": self.other})

    def across_to_other(self):
        at = self.at(self.f, self.across)
        return self.copy(2, at, at, {"ctx": self.other})

    def to_ahead(self, j):
        return self.copy(3 * j, self.own(), self.at(self.f, self.me), {"fsdp": self.ahead(j)})

    def behind_to_other(self, j):
        at = self.at(self.behind(j), self.me)
        return self.copy(3 * j + 1, at, at, {"ctx": self.other})

    def corner_to_other(self, j):
        at = self.at(self.behind(j), self.across)
        return self.copy(3 * j + 2, at, at, {"ctx": self.other})

    def across_to_ahead(self, j):
        at = self.at(self.f, self.across, 0, self.first)
        return self.copy(3 * self.fsdp + 2 * j - 2, at, at, {"fsdp": self.ahead(j)})

    def behind_to_across(self, j):
        at = self.at(self.behind(j), self.me, self.first, self.length - self.first)
        return self.copy(3 * self.fsdp + 2 * j - 1, at, at, {"ctx": self.across})

    def local(self):
        return pltpu.make_async_copy(self.own(), self.at(self.f, self.me), self.sems.at[2, 0])

    def start(self):
        self.start_across()
        self.start_ahead()

    def start_across(self):
        self.to_across().start()

    def start_ahead(self):
        for j in range(1, self.fsdp):
            self.to_ahead(j).start()
        self.to_other().start()
        self.local().start()

    def forward(self):
        self.forward_across()
        self.forward_behind()

    def forward_across(self):
        self.to_across().wait_recv()
        for j in range(1, self.fsdp):
            self.across_to_ahead(j).start()
        self.across_to_other().start()

    def forward_behind(self):
        for j in range(1, self.fsdp):
            self.to_ahead(j).wait_recv()
            self.behind_to_across(j).start()
            self.behind_to_other(j).start()

    def corner(self):
        for j in range(1, self.fsdp):
            self.across_to_ahead(j).wait_recv()
            self.behind_to_across(j).wait_recv()
            self.corner_to_other(j).start()

    def finish(self):
        self.local().wait()
        self.to_other().wait_recv()
        self.across_to_other().wait_recv()
        for j in range(1, self.fsdp):
            self.behind_to_other(j).wait_recv()
            self.corner_to_other(j).wait_recv()

    def drain(self):
        self.to_across().wait_send()
        self.to_other().wait_send()
        self.across_to_other().wait_send()
        for j in range(1, self.fsdp):
            self.to_ahead(j).wait_send()
            self.behind_to_other(j).wait_send()
            self.corner_to_other(j).wait_send()
            self.across_to_ahead(j).wait_send()
            self.behind_to_across(j).wait_send()


def gather_sems(fsdp):
    return pltpu.SemaphoreType.DMA((3, 5 * fsdp - 2))


def front_body(
    n,
    tp,
    fsdp,
    groups,
    token_ref,
    in_ref,
    tail_ref,
    out_weight_ref,
    gate_up_ref,
    down_ref,
    cos_ref,
    sin_ref,
    cotangent_ref,
    order_ref,
    length_ref,
    in_whole_ref,
    out_whole_ref,
    pair_whole_ref,
    normal_out_ref,
    grad_out_ref,
    gain_ref,
    q_ref,
    kv_ref,
    full_ref,
    low_ref,
    log_ref,
    residual_ref,
    out_ref,
    in_whole,
    out_whole,
    normal_ref,
    in_pack,
    out_pack,
    pair_pack,
    staged,
    proj,
    bias,
    parts,
    load_sem,
    save_sem,
    send_sem,
    recv_sem,
    in_sems,
    out_sems,
    pair_sems,
    inbox,
    *sems,
):
    z = lax.axis_index("tp")
    f = lax.axis_index("fsdp")
    me = lax.axis_index("ctx")
    peers = line_greet(tp, z)
    barrier = pltpu.get_barrier_semaphore()
    for step in range(1, n):
        pl.semaphore_signal(
            barrier, inc=1, device_id={"ctx": lax.rem(me + step, n)}, device_id_type=MESH
        )
    for step in range(1, fsdp):
        pl.semaphore_signal(
            barrier, inc=1, device_id={"fsdp": lax.rem(f + step, fsdp)}, device_id_type=MESH
        )

    seqs, _, rows = q_ref.shape
    dim = HEAD_DIMENSION
    half = dim // 2
    group_width = (GROUP + 2) * dim
    in_width = groups * group_width
    heads = groups * GROUP
    width = token_ref.shape[1]
    tile = 512 if width % 512 == 0 else width
    block = in_ref.shape[0]
    pair_width = gate_up_ref.shape[1]
    whole_tiles = in_width // 128 * 128

    ranges = cut(block, pair_sems.shape[0])

    def loads(i):
        low, length = ranges[i]
        return [
            pltpu.make_async_copy(
                source.at[pl.ds(low, length)],
                staged.at[i % 2, pl.ds(0, length), pl.ds(first, source.shape[1])],
                load_sem.at[i % 2, at],
            )
            for at, (source, first) in enumerate(((gate_up_ref, 0), (down_ref, pair_width)))
        ]

    for load in loads(0):
        load.start()
    cotangent = pltpu.make_async_copy(cotangent_ref, parts, load_sem.at[2, 0])
    grad_out = pltpu.make_async_copy(parts, grad_out_ref, load_sem.at[2, 1])
    cotangent.start()
    in_pack[:, :whole_tiles] = in_ref[:, :whole_tiles].astype(jnp.bfloat16)
    in_pack[:, whole_tiles:] = tail_ref[...]
    out_pack[...] = out_weight_ref[...].astype(jnp.bfloat16)
    pl.semaphore_wait(barrier, peers + n - 1 + fsdp - 1)

    def gathers(source, whole, sems):
        return [
            Gather(source, whole, low, length, block, fsdp, n, sems.at[i])
            for i, (low, length) in enumerate(cut(block, sems.shape[0]))
        ]

    first = gathers(in_pack, in_whole, in_sems)
    outer = gathers(out_pack, out_whole, out_sems)
    pair = gathers(pair_pack, pair_whole_ref, pair_sems)
    for piece in first:
        piece.start()
    for i, (low, length) in enumerate(ranges):
        if i + 1 < len(ranges):
            for load in loads(i + 1):
                load.start()
        for load in loads(i):
            load.wait()
        pair_pack[low : low + length, :] = staged[i % 2, :length, :].astype(jnp.bfloat16)

    cotangent.wait()
    span = rows // 2

    def keep(at, carry):
        own = pl.ds(pl.multiple_of(at * span, CHUNK), span)
        m = at // 2
        position = order_ref[m, 2 * me + lax.rem(at, 2)] * span + lax.broadcasted_iota(
            jnp.int32, (span, width), 0
        )
        parts[own, :] = jnp.where(
            position < length_ref[m], parts[own, :].astype(jnp.float32), 0.0
        ).astype(jnp.bfloat16)
        return carry

    lax.fori_loop(0, 2 * seqs, keep, 0)
    grad_out.start()
    for piece in first:
        piece.forward()
    for piece in outer:
        piece.start()
    for piece in first:
        piece.corner()
    for piece in first:
        piece.finish()
    for piece in outer:
        piece.forward()
    for piece in pair:
        piece.start_ahead()
    saves = [
        pltpu.make_async_copy(in_whole, in_whole_ref, save_sem.at[0]),
        pltpu.make_async_copy(normal_ref, normal_out_ref, save_sem.at[1]),
        pltpu.make_async_copy(out_whole, out_whole_ref, save_sem.at[2]),
    ]
    saves[0].start()

    turned = in_whole[:, whole_tiles : whole_tiles + 128].astype(jnp.float32).T
    gain_ref[...] = turned[in_width - whole_tiles : in_width - whole_tiles + 8]

    def columns_of(m):
        return pl.ds(pl.multiple_of(m * rows, 128), rows)

    def rows_of(m):
        return pl.ds(pl.multiple_of(m * rows, CHUNK), rows)

    def copy(m, step):
        return pltpu.make_async_remote_copy(
            src_ref=kv_ref.at[m, me],
            dst_ref=kv_ref.at[m, me],
            send_sem=send_sem.at[m, step - 1],
            recv_sem=recv_sem.at[m, step - 1],
            device_id={"ctx": lax.rem(me + step, n)},
            device_id_type=MESH,
        )

    def project(m, carry):
        values = token_ref[rows_of(m), :].astype(jnp.float32)
        root = lax.rsqrt(mean_of(values * values) + norm_eps)
        normal_ref[rows_of(m), :] = (values * root * gain_ref[0:1, :]).astype(jnp.bfloat16)
        proj[m] = jnp.dot(
            normal_ref[rows_of(m), :],
            in_whole[:, :in_width],
            preferred_element_type=jnp.float32,
        ).T
        for g in range(groups):
            col = g * group_width + GROUP * dim
            kv_ref[m, me, g, :dim, :] = turn(
                proj[m, col : col + half, :],
                proj[m, col + half : col + dim, :],
                cos_ref[m],
                sin_ref[m],
            ).astype(jnp.bfloat16)
            kv_ref[m, me, g, dim:, :] = proj[m, col + dim : col + 2 * dim, :].astype(jnp.bfloat16)
        for step in range(1, n):
            copy(m, step).start()
        return carry

    lax.fori_loop(0, seqs, project, 0)
    for piece in pair:
        piece.start_across()
    saves[1].start()

    def finish(segment, at, total):
        values = token_ref[at, :].astype(jnp.float32) + total
        residual_ref[at, :] = values.astype(jnp.bfloat16)
        root = lax.rsqrt(mean_of(values * values) + norm_eps)
        out_ref[at, :] = (values * root * gain_ref[1:2, :]).astype(jnp.bfloat16)

    line = Line(tp, z, seqs, rows, parts, inbox, out_ref, sems, finish)

    def head(m, at):
        g = at // GROUP
        h = at % GROUP
        low = pl.ds(pl.multiple_of(at * dim, 16), dim)
        col = pl.multiple_of(g * group_width + h * dim, 8)
        query = turn(
            proj[m, pl.ds(col, half), :],
            proj[m, pl.ds(pl.multiple_of(col + half, 8), half), :],
            cos_ref[m],
            sin_ref[m],
        ).astype(jnp.bfloat16)
        q_ref[m, low, :] = query
        scores = [
            lax.dot_general(
                kv_ref[m, j, g, :dim, :],
                query,
                (((0,), (0,)), ((), ())),
                preferred_element_type=jnp.float32,
            )
            * (log2_e * dim**-0.5)
            + bias[j * rows : (j + 1) * rows, :]
            for j in range(n)
        ]
        top = functools.reduce(jnp.maximum, [jnp.max(s, axis=0, keepdims=True) for s in scores])
        total = jnp.zeros_like(top)
        out = jnp.zeros((dim, rows), jnp.float32)
        for j in range(n):
            weights = jnp.exp2(scores[j] - top)
            total += jnp.sum(weights, axis=0, keepdims=True)
            out += jnp.dot(
                kv_ref[m, j, g, dim:, :],
                weights.astype(jnp.bfloat16),
                preferred_element_type=jnp.float32,
            )
        out = out / total
        full_ref[m, low, :] = out
        low_ref[low, columns_of(m)] = out.astype(jnp.bfloat16)
        log_ref[m, at] = top + jnp.log2(total)

    def ready(m):
        fill_bias(bias, order_ref, length_ref, m, me, n)
        for step in range(1, n):
            copy(m, step).wait_recv()

    def product(m):
        left = low_ref[:, columns_of(m)].T
        for low in range(0, width, tile):
            parts[rows_of(m), low : low + tile] = lax.dot_general(
                left,
                out_whole[low : low + tile, :],
                (((1,), (1,)), ((), ())),
                preferred_element_type=jnp.float32,
            ).astype(jnp.bfloat16)

    def sequence(m, carry):
        ready(m)

        def item(at, inner):
            line.tick((m - 1) * heads + at)
            head(m, at)
            return inner

        lax.fori_loop(0, heads, item, 0)
        product(m)
        return carry

    def opening(at, carry):
        head(0, at)
        return carry

    ready(0)
    lax.fori_loop(0, heads, opening, 0)
    grad_out.wait()
    for piece in outer:
        piece.corner()
    for piece in outer:
        piece.finish()
    saves[2].start()
    product(0)
    pair[0].forward_behind()
    lax.fori_loop(1, 2, sequence, 0)
    for piece in pair[1:2]:
        piece.forward_behind()
    lax.fori_loop(2, seqs, sequence, 0)
    at = (seqs - 1) * heads
    for piece in pair[2:3]:
        piece.forward_behind()
    pair[0].forward_across()
    line.run(at, at + 2)
    for piece in pair[3:]:
        piece.forward_behind()
    line.run(at + 2, at + 4)
    for piece in pair[1:2]:
        piece.forward_across()
    line.run(at + 4, at + 10)
    for piece in pair[2:3]:
        piece.forward_across()
    line.run(at + 10, at + 16)
    for piece in pair[3:]:
        piece.forward_across()
    line.run(at + 16, line.ticks)
    for piece in pair:
        piece.corner()
    for piece in pair:
        piece.finish()
    line.drain()
    for piece in first + outer + pair:
        piece.drain()
    for save in saves:
        save.wait()

    def drain(m, carry):
        for step in range(1, n):
            copy(m, step).wait_send()
        return carry

    lax.fori_loop(0, seqs, drain, 0)


def front(
    tokens, cotangent, in_weight, tail, out_weight, gate_up, down, where, seqs, n, tp, fsdp, ident
):
    all_rows, model_width = tokens.shape
    cosine, sine, orders, lengths = where
    rows = all_rows // seqs
    block, in_width = in_weight.shape
    groups = in_width // ((GROUP + 2) * HEAD_DIMENSION)
    heads = groups * GROUP
    shards = n * fsdp
    dim = HEAD_DIMENSION
    padded = in_width // 128 * 128 + tail.shape[1]
    out_width = out_weight.shape[1]
    pair_width = gate_up.shape[1] + down.shape[1]
    pieces = min(4, block // 32)
    longest = max(length for _, length in cut(block, pieces))
    shape = jax.ShapeDtypeStruct
    low, wide = jnp.bfloat16, jnp.float32
    vmem = pl.BlockSpec(memory_space=VMEM)
    hbm = pl.BlockSpec(memory_space=pl.ANY)
    smem = pl.BlockSpec(memory_space=pltpu.SMEM)
    dma = pltpu.SemaphoreType.DMA
    gather_sems = (3, 5 * fsdp - 2)
    return pl.pallas_call(
        functools.partial(front_body, n, tp, fsdp, groups),
        out_shape=(
            shape((shards * block, padded), low),
            shape((shards * block, out_width), low),
            shape((shards * block, pair_width), low),
            shape((all_rows, model_width), low),
            shape((all_rows, model_width), low),
            shape((8, model_width), wide),
            shape((seqs, heads * dim, rows), low),
            shape((seqs, n, groups, 2 * dim, rows), low),
            shape((seqs, heads * dim, rows), wide),
            shape((heads * dim, all_rows), low),
            shape((seqs, heads, 1, rows), wide),
            shape((all_rows, model_width), low),
            shape((all_rows, model_width), low),
        ),
        in_specs=[vmem] * 4 + [hbm] * 2 + [vmem] * 2 + [hbm] + [smem] * 2,
        out_specs=(hbm,) * 5 + (vmem,) * 8,
        scratch_shapes=[
            VMEM((shards * block, padded), low),
            VMEM((shards * block, out_width), low),
            VMEM((all_rows, model_width), low),
            VMEM((block, padded), low),
            VMEM((block, out_width), low),
            VMEM((block, pair_width), low),
            VMEM((2, longest, pair_width), wide),
            VMEM((seqs, in_width, rows), wide),
            VMEM((n * rows, rows), wide),
            VMEM((all_rows, model_width), low),
            dma((3, 2)),
            dma((3,)),
            dma((seqs, n - 1)),
            dma((seqs, n - 1)),
            dma((min(2, pieces),) + gather_sems),
            dma((1,) + gather_sems),
            dma((pieces,) + gather_sems),
        ]
        + line_scratch(all_rows, model_width, seqs, rows),
        compiler_params=pltpu.CompilerParams(
            collective_id=ident, has_side_effects=True, vmem_limit_bytes=60 * 2**20
        ),
        cost_estimate=line_cost(all_rows, model_width),
        name="front",
    )(tokens, in_weight, tail, out_weight, gate_up, down, cosine, sine, cotangent, orders, lengths)


def back_one_body(
    n,
    tp,
    groups,
    late,
    gate_ref,
    up_ref,
    pair_ref,
    gain_ref,
    log_ref,
    cos_ref,
    sin_ref,
    inner_from,
    residual_from,
    grad_out_from,
    weight_from,
    q_from,
    kv_from,
    full_from,
    early_from,
    order_ref,
    length_ref,
    grad_to,
    mixed_to,
    proj_ref,
    gain_sums,
    out_ref,
    parts,
    weights,
    inner_ref,
    residual_ref,
    grad_out_ref,
    out_proj,
    q_ref,
    kv_ref,
    full_ref,
    grads,
    sums,
    bias,
    outbox,
    kv_inbox,
    load_sem,
    save_sem,
    weight_sem,
    send_sem,
    recv_sem,
    inbox,
    *sems,
):
    z = lax.axis_index("tp")
    me = lax.axis_index("ctx")
    seqs, _, rows = q_ref.shape
    all_rows = seqs * rows
    units = inner_ref.shape[1]
    tile = weights.shape[1]
    pieces = out_ref.shape[1] // tile
    loads = [
        pltpu.make_async_copy(source, target, load_sem.at[at])
        for at, (source, target) in enumerate(
            (
                (residual_from, residual_ref),
                (grad_out_from, grad_out_ref),
                (inner_from, inner_ref),
                (weight_from, out_proj),
                (q_from, q_ref),
                (kv_from, kv_ref),
                (full_from, full_ref),
            )
        )
    ]

    early_rows = all_rows - late * rows
    saves = [
        pltpu.make_async_copy(early_from, mixed_to.at[pl.ds(0, early_rows)], save_sem.at[0]),
        pltpu.make_async_copy(out_ref.at[pl.ds(0, all_rows)], grad_to, save_sem.at[1]),
        pltpu.make_async_copy(
            out_ref.at[pl.ds(all_rows, late * rows)],
            mixed_to.at[pl.ds(early_rows, late * rows)],
            save_sem.at[2],
        ),
    ]

    def tile_of(at):
        return pl.ds(pl.multiple_of(at * tile, tile), tile)

    def fetch(at):
        slot = lax.rem(at, 2)
        return pltpu.make_async_copy(
            pair_ref.at[tile_of(lax.rem(at, pieces)), pl.ds(0, 2 * units)],
            weights.at[slot],
            weight_sem.at[slot],
        )

    def fetch_down(at):
        slot = lax.rem(at, 2)
        return pltpu.make_async_copy(
            pair_ref.at[tile_of(at), pl.ds(2 * units, units)],
            weights.at[slot, :, pl.ds(0, units)],
            weight_sem.at[slot],
        )

    fetch(0).start()
    for load in loads:
        load.start()
    saves[0].start()
    peers = line_greet(tp, z)
    barrier = pltpu.get_barrier_semaphore()
    for step in range(1, n):
        pl.semaphore_signal(
            barrier, inc=1, device_id={"ctx": lax.rem(me + step, n)}, device_id_type=MESH
        )
    pl.semaphore_wait(barrier, peers + n - 1)

    dim = HEAD_DIMENSION
    half = dim // 2
    scale = dim**-0.5
    group_width = (GROUP + 2) * dim
    heads = groups * GROUP
    gain_sums[...] = jnp.zeros_like(gain_sums)

    def finish(segment, at, total):
        @pl.when(segment < seqs)
        def _():
            grad = norm_back(
                total, residual_ref[at, :].astype(jnp.float32), gain_ref[1:2, :], gain_sums
            )
            out_ref[at, :] = (grad_out_ref[at, :].astype(jnp.float32) + grad).astype(jnp.bfloat16)

        @pl.when(segment >= seqs)
        def _():
            start = pl.multiple_of(at.start - late * rows, CHUNK)
            out_ref[at, :] = (
                residual_ref[pl.ds(start, CHUNK), :].astype(jnp.float32) + total
            ).astype(jnp.bfloat16)

    line = Line(tp, z, seqs + late, rows, parts, inbox, out_ref, sems, finish)

    def copy(m, step):
        to = lax.rem(me + step, n)
        return pltpu.make_async_remote_copy(
            src_ref=outbox.at[m, to],
            dst_ref=kv_inbox.at[m, step - 1],
            send_sem=send_sem.at[m, step - 1],
            recv_sem=recv_sem.at[m, step - 1],
            device_id={"ctx": to},
            device_id_type=MESH,
        )

    def columns(m):
        return pl.ds(pl.multiple_of(m * rows, 128), rows)

    def attended_grads(m):
        grads[...] = (
            jnp.dot(
                out_ref[pl.ds(pl.multiple_of(m * rows, CHUNK), rows), :],
                out_proj[...],
                preferred_element_type=jnp.float32,
            )
            .T.astype(jnp.bfloat16)
        )
        fill_bias(bias, order_ref, length_ref, m, me, n)

    def head(m, at):
        g = at // GROUP
        h = at % GROUP
        low = pl.ds(pl.multiple_of(at * dim, 16), dim)
        query = q_ref[m, low, :]
        grad = grads[low, :]
        delta = jnp.sum(
            grad.astype(jnp.float32) * full_ref[m, low, :], axis=0, keepdims=True
        )
        log_total = log_ref[m, at]
        query_sum = jnp.zeros((dim, rows), jnp.float32)

        @pl.when(h == 0)
        def _():
            sums[...] = jnp.zeros_like(sums)

        for j in range(n):
            keys = kv_ref[m, j, g, :dim, :]
            values = kv_ref[m, j, g, dim:, :]
            scores = lax.dot_general(
                keys, query, (((0,), (0,)), ((), ())), preferred_element_type=jnp.float32
            )
            probs = jnp.exp2(
                scores * (log2_e * scale) + (bias[j * rows : (j + 1) * rows, :] - log_total)
            )
            grad_probs = lax.dot_general(
                values, grad, (((0,), (0,)), ((), ())), preferred_element_type=jnp.float32
            )
            grad_scores = (probs * (grad_probs - delta)).astype(jnp.bfloat16)
            query_sum += jnp.dot(keys, grad_scores, preferred_element_type=jnp.float32)
            sums[j, :dim, :] += lax.dot_general(
                query, grad_scores, (((1,), (1,)), ((), ())), preferred_element_type=jnp.float32
            )
            sums[j, dim:, :] += lax.dot_general(
                grad,
                probs.astype(jnp.bfloat16),
                (((1,), (1,)), ((), ())),
                preferred_element_type=jnp.float32,
            )
        query_sum = query_sum * scale
        col = pl.ds(pl.multiple_of(g * group_width + h * dim, 16), dim)
        proj_ref[col, columns(m)] = turn_back(
            query_sum[:half], query_sum[half:], cos_ref[m], sin_ref[m]
        ).astype(jnp.bfloat16)

        @pl.when(h == GROUP - 1)
        def _():
            for j in range(n):
                outbox[m, j, g, :dim, :] = (sums[j, :dim, :] * scale).astype(jnp.bfloat16)
                outbox[m, j, g, dim:, :] = sums[j, dim:, :].astype(jnp.bfloat16)

    def gather(m):
        for step in range(1, n):
            copy(m, step).wait_recv()
        for g in range(groups):
            total = outbox[m, me, g].astype(jnp.float32)
            for step in range(1, n):
                total += kv_inbox[m, step - 1, g].astype(jnp.float32)
            col = g * group_width + GROUP * dim
            proj_ref[col : col + dim, columns(m)] = turn_back(
                total[:half], total[half:dim], cos_ref[m], sin_ref[m]
            ).astype(jnp.bfloat16)
            proj_ref[col + dim : col + 2 * dim, columns(m)] = total[dim:].astype(jnp.bfloat16)
        for step in range(1, n):
            copy(m, step).wait_send()

    contract = (((1,), (1,)), ((), ()))

    def leave(m, tile_at):
        at = m * pieces + tile_at
        own = pl.ds(pl.multiple_of(m * rows, CHUNK), rows)
        slot = lax.rem(at, 2)

        @pl.when(at + 1 < seqs * pieces)
        def _():
            fetch(at + 1).start()

        fetch(at).wait()
        parts[own, tile_of(tile_at)] = (
            lax.dot_general(
                gate_ref[own, :],
                weights[slot, :, :units],
                contract,
                preferred_element_type=jnp.float32,
            )
            + lax.dot_general(
                up_ref[own, :],
                weights[slot, :, units:],
                contract,
                preferred_element_type=jnp.float32,
            )
        ).astype(jnp.bfloat16)

    def first_leave(tile_at, carry):
        leave(0, tile_at)
        return carry

    lax.fori_loop(0, pieces, first_leave, 0)
    for load in loads:
        load.wait()
    ticks_ahead = line.per_segment

    def next_leave(m, carry):
        def item(tile_at, inner):
            @pl.when(tile_at < ticks_ahead)
            def _():
                line.tick((m - 1) * ticks_ahead + tile_at)

            leave(m, tile_at)
            return inner

        lax.fori_loop(0, pieces, item, 0)
        return carry

    lax.fori_loop(1, seqs, next_leave, 0)
    at_tick = (seqs - 1) * ticks_ahead
    fetch_down(0).start()

    def expand(at, carry):
        @pl.when(at < ticks_ahead)
        def _():
            line.tick(at_tick + at)

        @pl.when(at + 1 < pieces)
        def _():
            fetch_down(at + 1).start()

        fetch_down(at).wait()
        parts[pl.ds(all_rows, late * rows), tile_of(at)] = lax.dot_general(
            inner_ref[pl.ds((seqs - late) * rows, late * rows), :],
            weights[lax.rem(at, 2), :, :units],
            contract,
            preferred_element_type=jnp.float32,
        ).astype(jnp.bfloat16)
        return carry

    lax.fori_loop(0, pieces, expand, 0)
    opened = max(seqs * ticks_ahead, line.ready(1))
    line.run(seqs * ticks_ahead, opened)

    def sequence(m, carry):
        first = opened + m * (heads + 1)
        line.tick(first)
        attended_grads(m)

        def item(at, inner):
            line.tick(first + 1 + at)
            head(m, at)
            return inner

        lax.fori_loop(0, heads, item, 0)
        for step in range(1, n):
            copy(m, step).start()

        @pl.when(m > 0)
        def _():
            gather(m - 1)

        return carry

    lax.fori_loop(0, seqs, sequence, 0)
    saves[1].start()
    line.run(opened + seqs * (heads + 1), line.ticks)

    saves[2].start()
    gather(seqs - 1)
    line.drain()
    for save in saves:
        save.wait()


def back_one(
    inner,
    grad_gate,
    grad_up,
    pair_whole,
    mixed_early,
    residual,
    grad_out,
    gains,
    out_whole,
    queries,
    key_values,
    full,
    log_total,
    where,
    n,
    tp,
    ident,
):
    seqs, width, rows = queries.shape
    groups = key_values.shape[2]
    all_rows, model_width = residual.shape
    late = seqs - mixed_early.shape[0] // rows
    cosine, sine, orders, lengths = where
    units = inner.shape[1]
    line_rows = all_rows + late * rows
    vmem = pl.BlockSpec(memory_space=VMEM)
    hbm = pl.BlockSpec(memory_space=pl.ANY)
    smem = pl.BlockSpec(memory_space=pltpu.SMEM)
    shape = jax.ShapeDtypeStruct
    return pl.pallas_call(
        functools.partial(back_one_body, n, tp, groups, late),
        out_shape=(
            shape((all_rows, model_width), jnp.bfloat16),
            shape((all_rows, model_width), jnp.bfloat16),
            shape((groups * (GROUP + 2) * HEAD_DIMENSION, all_rows), jnp.bfloat16),
            shape((8, model_width), jnp.float32),
        ),
        in_specs=[vmem] * 2 + [hbm] + [vmem] * 4 + [hbm] * 8 + [smem] * 2,
        out_specs=(hbm,) * 2 + (vmem,) * 2,
        scratch_shapes=[
            VMEM((line_rows, model_width), jnp.bfloat16),
            VMEM((line_rows, model_width), jnp.bfloat16),
            VMEM((2, 256, 2 * units), jnp.bfloat16),
            VMEM((all_rows, units), jnp.bfloat16),
            VMEM((all_rows, model_width), jnp.bfloat16),
            VMEM((all_rows, model_width), jnp.bfloat16),
            VMEM((model_width, width), jnp.bfloat16),
            VMEM(queries.shape, jnp.bfloat16),
            VMEM(key_values.shape, jnp.bfloat16),
            VMEM(full.shape, jnp.float32),
            VMEM((width, rows), jnp.bfloat16),
            VMEM((n, 2 * HEAD_DIMENSION, rows), jnp.float32),
            VMEM((n * rows, rows), jnp.float32),
            VMEM((seqs, n, groups, 2 * HEAD_DIMENSION, rows), jnp.bfloat16),
            VMEM((seqs, n - 1, groups, 2 * HEAD_DIMENSION, rows), jnp.bfloat16),
            pltpu.SemaphoreType.DMA((7,)),
            pltpu.SemaphoreType.DMA((3,)),
            pltpu.SemaphoreType.DMA((2,)),
            pltpu.SemaphoreType.DMA((seqs, n - 1)),
            pltpu.SemaphoreType.DMA((seqs, n - 1)),
        ]
        + line_scratch(line_rows, model_width, seqs + late, rows),
        compiler_params=pltpu.CompilerParams(
            collective_id=ident, has_side_effects=True, vmem_limit_bytes=60 * 2**20
        ),
        cost_estimate=line_cost(line_rows, model_width),
        name="back_one",
    )(
        grad_gate,
        grad_up,
        pair_whole,
        gains,
        log_total,
        cosine,
        sine,
        inner,
        residual,
        grad_out,
        out_whole,
        queries,
        key_values,
        full,
        mixed_early,
        orders,
        lengths,
    )


def back_two_body(
    tp,
    seqs,
    skip,
    proj_ref,
    weight_ref,
    gain_ref,
    token_from,
    residual_grad_from,
    out_ref,
    gain_sums,
    token_ref,
    residual_grad_ref,
    parts,
    load_sem,
    inbox,
    *sems,
):
    z = lax.axis_index("tp")
    loads = [
        pltpu.make_async_copy(token_from, token_ref, load_sem.at[0]),
        pltpu.make_async_copy(
            residual_grad_from.at[pl.ds(0, residual_grad_ref.shape[0])],
            residual_grad_ref,
            load_sem.at[1],
        ),
    ]
    for load in loads:
        load.start()
    pl.semaphore_wait(pltpu.get_barrier_semaphore(), line_greet(tp, z))
    gain_sums[...] = jnp.zeros_like(gain_sums)
    rows = token_ref.shape[0] // seqs
    width = weight_ref.shape[0]
    tile = 512 if width % 512 == 0 else width

    def finish(segment, at, total):
        values = token_ref[at, :].astype(jnp.float32)
        grad = norm_back(total, values, gain_ref[0:1, :], gain_sums)
        out_ref[at, :] = (residual_grad_ref[at, :].astype(jnp.float32) + grad).astype(jnp.bfloat16)

    line = Line(tp, z, seqs, rows, parts, inbox, out_ref, sems, finish)

    def product(m):
        left = proj_ref[:, m * rows : (m + 1) * rows].T
        for low in range(0, width, tile):
            parts[m * rows : (m + 1) * rows, low : low + tile] = lax.dot_general(
                left,
                weight_ref[low : low + tile, skip : skip + proj_ref.shape[0]],
                (((1,), (1,)), ((), ())),
                preferred_element_type=jnp.float32,
            ).astype(jnp.bfloat16)

    for m in range(seqs):
        product(m)
        line.run(2 * m, 2 * m + 2)
        if m == 0:
            for load in loads:
                load.wait()
    line.run(2 * seqs, line.ticks)
    line.drain()


def back_two(projected, first_whole, tokens, residual_grad, gains, skip, seqs, tp, ident):
    rows, width = tokens.shape
    vmem = pl.BlockSpec(memory_space=VMEM)
    hbm = pl.BlockSpec(memory_space=pl.ANY)
    shape = jax.ShapeDtypeStruct
    return pl.pallas_call(
        functools.partial(back_two_body, tp, seqs, skip),
        out_shape=(shape((rows, width), jnp.bfloat16), shape((8, width), jnp.float32)),
        in_specs=[vmem] * 3 + [hbm] * 2,
        out_specs=(vmem,) * 2,
        scratch_shapes=[VMEM((rows, width), jnp.bfloat16)] * 3
        + [pltpu.SemaphoreType.DMA((2,))]
        + line_scratch(rows, width, seqs, rows // seqs),
        compiler_params=pltpu.CompilerParams(
            collective_id=ident, has_side_effects=True, vmem_limit_bytes=56 * 2**20
        ),
        cost_estimate=line_cost(rows, width),
        name="back_two",
    )(projected, first_whole, gains, tokens, residual_grad)


def hidden_body(
    tp,
    seqs,
    early,
    normal_ref,
    grad_out_ref,
    residual_ref,
    whole_ref,
    grads_ref,
    inner_ref,
    gate_ref,
    up_ref,
    out_ref,
    residual,
    turned,
    staged,
    columns,
    weights,
    parts,
    load_sem,
    column_sem,
    weight_sem,
    store_sem,
    inbox,
    *sems,
):
    z = lax.axis_index("tp")
    rows, units = inner_ref.shape
    width = normal_ref.shape[1]
    tile = staged.shape[2]
    pieces = width // tile
    steps = units // tile
    early_rows = parts.shape[0]

    def columns_of(at):
        return pl.ds(pl.multiple_of(at * tile, tile), tile)

    def fetch_columns(at):
        slot = lax.rem(at, 2)
        return [
            pltpu.make_async_copy(
                whole_ref.at[:, columns_of(kind * steps + lax.rem(at, steps))],
                columns.at[slot, kind],
                column_sem.at[slot, kind],
            )
            for kind in range(3)
        ]

    def fetch(at):
        slot = lax.rem(at, 2)
        return pltpu.make_async_copy(
            whole_ref.at[columns_of(at), pl.ds(2 * units, units)],
            weights.at[slot],
            weight_sem.at[slot],
        )

    load = pltpu.make_async_copy(
        residual_ref.at[pl.ds(0, early_rows)], residual, load_sem.at[0]
    )
    for copy in fetch_columns(0):
        copy.start()
    load.start()
    pl.semaphore_wait(pltpu.get_barrier_semaphore(), line_greet(tp, z))

    def finish(segment, at, total):
        out_ref[at, :] = (residual[at, :].astype(jnp.float32) + total).astype(jnp.bfloat16)

    line = Line(tp, z, early, rows // seqs, parts, inbox, out_ref, sems, finish)

    early_opening = rows // seqs

    def units_of(at, low, high):
        slot = lax.rem(at, 2)

        @pl.when(at + 1 < 2 * steps)
        def _():
            for copy in fetch_columns(at + 1):
                copy.start()

        for copy in fetch_columns(at):
            copy.wait()

        def product(left, kind):
            return jnp.dot(
                left[low:high, :], columns[slot, kind], preferred_element_type=jnp.float32
            )

        gate = product(normal_ref, 0)
        up = product(normal_ref, 1)
        grad_inner = product(grad_out_ref, 2)
        sigmoid = jax.nn.sigmoid(gate)
        silu = gate * sigmoid
        to = columns_of(lax.rem(at, steps))
        inner_ref[low:high, to] = (silu * up).astype(jnp.bfloat16)
        gate_ref[low:high, to] = (
            grad_inner * up * sigmoid * (1.0 + gate * (1.0 - sigmoid))
        ).astype(jnp.bfloat16)
        up_ref[low:high, to] = (grad_inner * silu).astype(jnp.bfloat16)

    def opening(at, carry):
        units_of(at, 0, early_opening)
        return carry

    fetch(0).start()
    lax.fori_loop(0, steps, opening, 0)

    def expand(low, high):
        def item(at, carry):
            @pl.when(at + 1 < pieces)
            def _():
                fetch(at + 1).start()

            fetch(at).wait()
            parts[low:high, columns_of(at)] = lax.dot_general(
                inner_ref[low:high, :],
                weights[lax.rem(at, 2)],
                (((1,), (1,)), ((), ())),
                preferred_element_type=jnp.float32,
            ).astype(jnp.bfloat16)
            return carry

        lax.fori_loop(0, pieces, item, 0)

    expand(0, early_opening)
    load.wait()

    def others(at, carry):
        line.tick(at)
        units_of(steps + at, early_opening, rows)
        return carry

    if early_rows > early_opening:
        fetch(0).start()
    lax.fori_loop(0, steps, others, 0)
    if early_rows > early_opening:
        expand(early_opening, early_rows)
    turned[...] = normal_ref[...].T

    def store(at):
        slot = lax.rem(at, 2)
        return pltpu.make_async_copy(
            staged.at[slot], grads_ref.at[:, columns_of(at)], store_sem.at[slot]
        )

    for kind, right in enumerate((gate_ref, up_ref, inner_ref)):
        if kind == 2:
            turned[...] = grad_out_ref[...].T

        def gradient(step, carry):
            at = kind * steps + step
            line.tick(steps + at)

            @pl.when(at >= 2)
            def _():
                store(at - 2).wait()

            staged[lax.rem(at, 2)] = jnp.dot(
                turned[...], right[:, columns_of(step)], preferred_element_type=jnp.float32
            ).astype(jnp.bfloat16)
            store(at).start()
            return carry

        lax.fori_loop(0, steps, gradient, 0)

    store(3 * steps - 2).wait()
    store(3 * steps - 1).wait()
    line.run(4 * steps, line.ticks)
    line.drain()


def hidden_units(normal, grad_out, residual, whole, seqs, early, tp, ident):
    all_rows, width = normal.shape
    columns = whole.shape[1]
    units = columns // 3
    rows = all_rows // seqs
    tile = 256
    low = jnp.bfloat16
    shape = jax.ShapeDtypeStruct
    vmem = pl.BlockSpec(memory_space=VMEM)
    hbm = pl.BlockSpec(memory_space=pl.ANY)
    dma = pltpu.SemaphoreType.DMA
    return pl.pallas_call(
        functools.partial(hidden_body, tp, seqs, early),
        out_shape=(shape((width, columns), low),)
        + (shape((all_rows, units), low),) * 3
        + (shape((early * rows, width), low),),
        in_specs=[vmem] * 2 + [hbm] * 2,
        out_specs=(hbm,) + (vmem,) * 4,
        scratch_shapes=[
            VMEM((early * rows, width), low),
            VMEM((width, all_rows), low),
            VMEM((2, width, tile), low),
            VMEM((2, 3, width, tile), low),
            VMEM((2, tile, units), low),
            VMEM((early * rows, width), low),
            dma((1,)),
            dma((2, 3)),
            dma((2,)),
            dma((2,)),
        ]
        + line_scratch(early * rows, width, early, rows),
        compiler_params=pltpu.CompilerParams(
            collective_id=ident, has_side_effects=True, vmem_limit_bytes=60 * 2**20
        ),
        cost_estimate=pl.CostEstimate(
            flops=4 * all_rows * width * columns,
            bytes_accessed=40 * all_rows * width,
            transcendentals=all_rows * units,
        ),
        name="hidden_units",
    )(normal, grad_out, residual, whole)


def first_grads_body(normal_ref, proj_ref, residual_ref, attended_ref, out_ref):
    split = attended_ref.shape[0]
    contract = (((1,), (1,)), ((), ()))
    for left, right, low in ((residual_ref, attended_ref, 0), (normal_ref, proj_ref, split)):
        out_ref[:, low : low + right.shape[0]] = lax.dot_general(
            left[...].T, right[...], contract, preferred_element_type=jnp.float32
        ).astype(jnp.bfloat16)


def first_grads_of(normal, projected, residual_grad, attended):
    rows, width = normal.shape
    columns = projected.shape[0] + attended.shape[0]
    tile = 512 if width % 512 == 0 else width
    vmem = pl.BlockSpec(memory_space=VMEM)
    left = pl.BlockSpec((rows, tile), lambda i: (0, i))
    return pl.pallas_call(
        first_grads_body,
        grid=(width // tile,),
        out_shape=jax.ShapeDtypeStruct((width, columns), jnp.bfloat16),
        in_specs=[left, vmem, left, vmem],
        out_specs=pl.BlockSpec((tile, columns), lambda i: (i, 0)),
        compiler_params=pltpu.CompilerParams(vmem_limit_bytes=48 * 2**20),
        cost_estimate=pl.CostEstimate(
            flops=2 * rows * width * columns,
            bytes_accessed=2 * (2 * rows * width + (rows + width) * columns),
            transcendentals=0,
        ),
        name="first_grads",
    )(normal, projected, residual_grad, attended)


def gain_body(ctx_size, tp, x_ref, o_ref, inbox, tp_inbox, send_sem, recv_sem, tp_send, tp_recv):
    shards = x_ref.shape[0]
    me = lax.axis_index("fsdp") * ctx_size + lax.axis_index("ctx")
    z = lax.axis_index("tp")

    def to(step):
        other = lax.rem(me + step, shards)
        return other, {"fsdp": other // ctx_size, "ctx": lax.rem(other, ctx_size)}

    barrier = pltpu.get_barrier_semaphore()
    for step in range(1, shards):
        pl.semaphore_signal(barrier, inc=1, device_id=to(step)[1], device_id_type=MESH)
    for step in range(1, tp):
        pl.semaphore_signal(
            barrier, inc=1, device_id={"tp": lax.rem(z + step, tp)}, device_id_type=MESH
        )
    pl.semaphore_wait(barrier, shards - 1 + tp - 1)

    def copy(step):
        other, where = to(step)
        return pltpu.make_async_remote_copy(
            src_ref=x_ref.at[other],
            dst_ref=inbox.at[step - 1],
            send_sem=send_sem.at[step - 1],
            recv_sem=recv_sem.at[step - 1],
            device_id=where,
            device_id_type=MESH,
        )

    def tp_copy(step):
        return pltpu.make_async_remote_copy(
            src_ref=tp_inbox.at[0],
            dst_ref=tp_inbox.at[step],
            send_sem=tp_send.at[step - 1],
            recv_sem=tp_recv.at[step - 1],
            device_id={"tp": lax.rem(z + step, tp)},
            device_id_type=MESH,
        )

    for step in range(1, shards):
        copy(step).start()
    total = x_ref[me]
    for step in range(1, shards):
        copy(step).wait()
        total += inbox[step - 1]
    tp_inbox[0] = total
    for step in range(1, tp):
        tp_copy(step).start()
    for step in range(1, tp):
        tp_copy(step).wait()
        total += tp_inbox[step]
    o_ref[...] = total


def gain_sum(partial, shards, ctx_size, tp, ident):
    two, width = partial.shape
    own = width // shards
    padded = -(-own // 128) * 128
    pieces = jnp.pad(
        partial.reshape(two, shards, own).transpose(1, 0, 2),
        ((0, 0), (0, 8 - two), (0, padded - own)),
    )
    total = pl.pallas_call(
        functools.partial(gain_body, ctx_size, tp),
        out_shape=jax.ShapeDtypeStruct((8, padded), jnp.float32),
        in_specs=[pl.BlockSpec(memory_space=VMEM)],
        out_specs=pl.BlockSpec(memory_space=VMEM),
        scratch_shapes=[
            VMEM((shards - 1, 8, padded), jnp.float32),
            VMEM((tp, 8, padded), jnp.float32),
            pltpu.SemaphoreType.DMA((shards - 1,)),
            pltpu.SemaphoreType.DMA((shards - 1,)),
            pltpu.SemaphoreType.DMA((tp - 1,)),
            pltpu.SemaphoreType.DMA((tp - 1,)),
        ],
        compiler_params=pltpu.CompilerParams(collective_id=ident, has_side_effects=True),
        name="gain_sum",
    )(pieces)
    return total[:two, :own]


def dot(spec, left, right):
    return jnp.einsum(spec, left, right, preferred_element_type=jnp.float32)


def on_device(
    tokens,
    out_cotangent,
    seq_lengths,
    span_order,
    attention_input_weight,
    attention_input_first,
    attention_input_squared,
    attend_out,
    attend_out_moment,
    attend_out_second,
    gate_up,
    gate_up_moment,
    gate_up_second,
    down_weight,
    down_weight_moment,
    down_weight_second,
    norm_gains,
    norm_gains_moment,
    norm_gains_second,
):
    low = jnp.bfloat16
    micro_count, slot_count, row_count, model_width = tokens.shape
    seqs = micro_count * slot_count
    ctx_size = lax.axis_size("ctx")
    tp_size = lax.axis_size("tp")
    sequence_length = row_count * ctx_size
    span_len = sequence_length // (2 * ctx_size)
    hidden = down_weight.shape[0]
    out_width = attend_out.shape[0]
    in_width = attention_input_weight.shape[1]
    shards = ("fsdp", "ctx")

    ahead = in_width // 128 * 128
    tail = jnp.concatenate([attention_input_weight[:, ahead:], norm_gains.T], 1).astype(low)
    tail = jnp.pad(tail, ((0, 0), (0, -tail.shape[1] % 128)))

    orders = span_order.reshape(seqs, 2 * ctx_size)
    lengths = seq_lengths.reshape(seqs)
    within = jnp.arange(sequence_length, dtype=jnp.int32)
    block_ids = jnp.arange(2 * ctx_size, dtype=jnp.int32)
    table = jnp.where(
        block_ids[None, None, :] == (within // span_len)[None, :, None], orders[:, None, :], 0
    )
    pos_all = jnp.sum(table, -1) * span_len + within % span_len
    pos_here = lax.dynamic_slice_in_dim(pos_all, lax.axis_index("ctx") * row_count, row_count, 1)
    half_width = HEAD_DIMENSION // 2
    inverse = rope_base ** (-(jnp.arange(half_width, dtype=jnp.float32) * 2.0 / HEAD_DIMENSION))
    angles = pos_here.astype(jnp.float32)[:, None, :] * inverse[None, :, None]
    cosine, sine = jnp.cos(angles), jnp.sin(angles)
    where = (cosine, sine, orders, lengths)

    all_rows = seqs * row_count
    token_rows = tokens.reshape(all_rows, model_width)
    (
        in_whole,
        out_whole,
        pair_whole,
        first_normal,
        grad_out,
        gains,
        queries,
        key_values,
        attended_full,
        attended,
        log_total,
        residual,
        second_normal,
    ) = front(
        token_rows,
        out_cotangent.reshape(all_rows, model_width),
        attention_input_weight,
        tail,
        attend_out.T,
        gate_up,
        down_weight.T,
        where,
        seqs,
        ctx_size,
        tp_size,
        lax.axis_size("fsdp"),
        1,
    )

    early = 1
    second_grads, inner, grad_gate, grad_up, mixed_early = hidden_units(
        second_normal, grad_out, residual, pair_whole, seqs, early, tp_size, 2
    )
    inner, second_grads = lax.optimization_barrier((inner, second_grads))
    second_share = lax.psum_scatter(second_grads, shards, scatter_dimension=0, tiled=True)

    grad_residual, mixed, grad_projected, second_gain = back_one(
        inner,
        grad_gate,
        grad_up,
        pair_whole,
        mixed_early,
        residual,
        grad_out,
        gains,
        out_whole,
        queries,
        key_values,
        attended_full,
        log_total,
        where,
        ctx_size,
        tp_size,
        4,
    )
    first_grads = first_grads_of(
        first_normal, grad_projected, grad_residual, attended
    )
    grad_projected, first_grads, second_share = lax.optimization_barrier(
        (grad_projected, first_grads, second_share)
    )
    first_share = lax.psum_scatter(first_grads, shards, scatter_dimension=0, tiled=True)
    input_grad, first_gain = back_two(
        grad_projected,
        in_whole,
        token_rows,
        grad_residual,
        gains,
        0,
        seqs,
        tp_size,
        5,
    )
    gain_share = gain_sum(
        jnp.stack([first_gain.sum(0), second_gain.sum(0)]),
        lax.axis_size("fsdp") * ctx_size,
        ctx_size,
        tp_size,
        7,
    )

    gradients = (
        first_share[:, out_width:],
        first_share[:, :out_width].T,
        second_share[:, : 2 * hidden],
        second_share[:, 2 * hidden :].T,
        gain_share,
    )
    masters = (attention_input_weight, attend_out, gate_up, down_weight, norm_gains)
    firsts = (
        attention_input_first,
        attend_out_moment,
        gate_up_moment,
        down_weight_moment,
        norm_gains_moment,
    )
    seconds = (
        attention_input_squared,
        attend_out_second,
        gate_up_second,
        down_weight_second,
        norm_gains_second,
    )
    results = [mixed.reshape(tokens.shape), input_grad.reshape(tokens.shape).astype(jnp.float32)]
    for at in range(5):
        updated = adam_update(
            masters[at],
            firsts[at],
            seconds[at],
            gradients[at].astype(jnp.float32),
            learn_rates[at],
            decay_flags[at],
        )
        results.extend(updated)
        if at < 4:
            results.append(updated[2].astype(low))
    return tuple(results)


def solution(mesh):
    rows = P(None, "fsdp", "ctx", None)
    upper = P(("fsdp", "ctx"), "tp")
    lower = P("tp", ("fsdp", "ctx"))
    gain = P(None, ("fsdp", "ctx"))
    return jax.shard_map(
        on_device,
        mesh=mesh,
        in_specs=(rows, rows, P(None, "fsdp"), P(None, "fsdp", None))
        + (upper,) * 3
        + (lower,) * 3
        + (upper,) * 3
        + (lower,) * 3
        + (gain,) * 3,
        out_specs=(rows, rows)
        + (upper,) * 4
        + (lower,) * 4
        + (upper,) * 4
        + (lower,) * 4
        + (gain,) * 3,
        check_vma=False,
    )
```

```python
import functools

import jax
import jax.numpy as jnp
from jax import lax
from jax.experimental import pallas as pl
from jax.experimental.pallas import tpu as pltpu
from jax.sharding import PartitionSpec as P

QUERY_HEADS = 32
KEY_VALUE_HEADS = 8
HEAD_DIMENSION = 80
STEP = 10
GROUP = QUERY_HEADS // KEY_VALUE_HEADS

rope_base = 1000000.0
norm_eps = 1e-05
beta_one = 0.9
beta_two = 0.95
adam_eps = 1e-08
weight_decay = 0.1
learn_rates = (0.1, 0.5, 0.05, 0.04, 0.8)
decay_flags = (1.0, 1.0, 1.0, 1.0, 0.0)
neg_big = -1e30
log2_e = 1.4426950408889634
MESH = pl.DeviceIdType.MESH
VMEM = pltpu.VMEM
CHUNK = 16
LAG = 2


def adam_update(weight, moment, second, gradient, learn_rate, decay_flag):
    moment = beta_one * moment + (1.0 - beta_one) * gradient
    second = beta_two * second + (1.0 - beta_two) * gradient * gradient
    moment_hat = moment / (1.0 - beta_one**STEP)
    second_hat = second / (1.0 - beta_two**STEP)
    weight = weight - learn_rate * (
        moment_hat / (jnp.sqrt(second_hat) + adam_eps) + decay_flag * weight_decay * weight
    )
    return (moment, second, weight)


def line_greet(n, z):
    barrier = pltpu.get_barrier_semaphore()

    @pl.when(z > 0)
    def _():
        pl.semaphore_signal(barrier, inc=1, device_id={"tp": z - 1}, device_id_type=MESH)

    @pl.when(z < n - 1)
    def _():
        pl.semaphore_signal(barrier, inc=1, device_id={"tp": z + 1}, device_id_type=MESH)

    return (z > 0).astype(jnp.int32) + (z < n - 1).astype(jnp.int32)


class Line:
    def __init__(self, n, z, segments, segment_rows, parts, inbox, out, sems, finish):
        self.n, self.z = n, z
        self.segment_rows = segment_rows
        self.per_segment = segment_rows // (2 * CHUNK)
        self.chunks = segments * self.per_segment
        self.parts, self.inbox, self.out = parts, inbox, out
        self.red_send, self.red_recv, self.back_send, self.back_recv = sems
        self.finish = finish
        self.ticks = self.chunks + 2 * (n - 1) * LAG

    def ready(self, segments):
        return segments * self.per_segment + 2 * (self.n - 1) * LAG

    def rows(self, flow, g):
        start = (
            (g // self.per_segment) * self.segment_rows
            + flow * (self.segment_rows // 2)
            + (g % self.per_segment) * CHUNK
        )
        return pl.ds(pl.multiple_of(start, CHUNK), CHUNK)

    def hop(self, flow):
        return (self.n - 1 - self.z) if flow == 0 else self.z

    def neighbour(self, up):
        z = jnp.minimum(self.z + 1, self.n - 1) if up else jnp.maximum(self.z - 1, 0)
        return {"tp": z}

    def reduce_copy(self, flow, g, source):
        return pltpu.make_async_remote_copy(
            src_ref=source,
            dst_ref=self.inbox.at[self.rows(flow, g)],
            send_sem=self.red_send.at[flow, g],
            recv_sem=self.red_recv.at[flow, g],
            device_id=self.neighbour(flow == 1),
            device_id_type=MESH,
        )

    def back_copy(self, flow, g):
        rows = self.rows(flow, g)
        return pltpu.make_async_remote_copy(
            src_ref=self.out.at[rows],
            dst_ref=self.out.at[rows],
            send_sem=self.back_send.at[flow, g],
            recv_sem=self.back_recv.at[flow, g],
            device_id=self.neighbour(flow == 0),
            device_id_type=MESH,
        )

    def tick(self, t):
        n = self.n
        for flow in (0, 1):

            @pl.when((self.hop(flow) == 0) & (t >= 0) & (t < self.chunks))
            def _():
                self.reduce_copy(flow, t, self.parts.at[self.rows(flow, t)]).start()

        for flow in (0, 1):
            hop = self.hop(flow)
            g = t - hop * LAG

            @pl.when((hop > 0) & (g >= 0) & (g < self.chunks))
            def _():
                rows = self.rows(flow, g)
                self.reduce_copy(flow, g, self.parts.at[rows]).wait_recv()
                total = self.inbox[rows, :].astype(jnp.float32) + self.parts[rows, :].astype(
                    jnp.float32
                )

                @pl.when(hop < n - 1)
                def _():
                    self.inbox[rows, :] = total.astype(jnp.bfloat16)
                    self.reduce_copy(flow, g, self.inbox.at[rows]).start()

                @pl.when(hop == n - 1)
                def _():
                    self.finish(g // self.per_segment, rows, total)
                    self.back_copy(flow, g).start()

        for flow in (0, 1):
            hop = self.hop(flow)
            back = t - (n - 1) * LAG - (n - 1 - hop) * LAG

            @pl.when((back >= 0) & (back < self.chunks) & (hop < n - 1))
            def _():
                self.back_copy(flow, back).wait_recv()

                @pl.when(hop > 0)
                def _():
                    self.back_copy(flow, back).start()

    def run(self, first, last):
        def step(t, carry):
            self.tick(t)
            return carry

        lax.fori_loop(first, last, step, 0)

    def drain(self):
        def step(g, carry):
            for flow in (0, 1):
                hop = self.hop(flow)

                @pl.when(hop < self.n - 1)
                def _():
                    self.reduce_copy(flow, g, self.parts.at[self.rows(flow, g)]).wait_send()

                @pl.when(hop > 0)
                def _():
                    self.back_copy(flow, g).wait_send()

            return carry

        lax.fori_loop(0, self.chunks, step, 0)


def line_scratch(rows, width, segments, segment_rows):
    chunks = segments * (segment_rows // (2 * CHUNK))
    return [VMEM((rows, width), jnp.bfloat16)] + [pltpu.SemaphoreType.DMA((2, chunks))] * 4


def line_cost(rows, width):
    return pl.CostEstimate(flops=rows * width, bytes_accessed=80 * rows * width, transcendentals=0)


def mean_of(values):
    return jnp.mean(values, axis=-1, keepdims=True)


def norm_back(total, values, gain, gain_sums):
    root = lax.rsqrt(mean_of(values * values) + norm_eps)
    standard = values * root
    terms = total * standard
    gain_sums[...] += functools.reduce(
        lambda a, b: a + b, [terms[low : low + 8] for low in range(0, CHUNK, 8)]
    )
    scaled = total * gain
    return root * (scaled - standard * mean_of(scaled * standard))


def turn(first, second, cosine, sine):
    return jnp.concatenate([first * cosine - second * sine, second * cosine + first * sine], 0)


def turn_back(first, second, cosine, sine):
    return jnp.concatenate([first * cosine + second * sine, second * cosine - first * sine], 0)


def fill_bias(bias, order_ref, length_ref, m, me, n):
    rows = bias.shape[1]
    span = rows // 2
    lane = lax.broadcasted_iota(jnp.int32, (1, rows), 1)
    query = jnp.where(
        lane < span,
        order_ref[m, 2 * me] * span + lane,
        order_ref[m, 2 * me + 1] * span + lane - span,
    )
    within = lax.broadcasted_iota(jnp.int32, (span, rows), 0)
    for block in range(2 * n):
        key = order_ref[m, block] * span + within
        allowed = (key <= query) & (key < length_ref[m])
        bias[block * span : (block + 1) * span, :] = jnp.where(allowed, 0.0, neg_big)


def cut(rows, parts):
    tiles = rows // 16
    ends = [tiles * i // parts * 16 for i in range(parts + 1)]
    return [(low, high - low) for low, high in zip(ends[:-1], ends[1:])]


class Gather:
    def __init__(self, source, whole, low, length, block_rows, fsdp, n, sems):
        self.source, self.whole = source, whole
        self.low, self.length, self.block_rows = low, length, block_rows
        self.fsdp, self.n = fsdp, n
        self.f, self.me = lax.axis_index("fsdp"), lax.axis_index("ctx")
        self.across = lax.rem(self.me + n // 2, n)
        self.other = self.me + 1 - 2 * lax.rem(self.me, 2)
        self.sems = sems
        self.first = max(16, min(length - 16, length * 6 // 160 * 16))

    def at(self, f, ctx, low=0, length=None):
        start = (f * self.n + ctx) * self.block_rows + self.low + low
        return self.whole.at[
            pl.ds(pl.multiple_of(start, 16), self.length if length is None else length)
        ]

    def copy(self, kind, source, target, where):
        return pltpu.make_async_remote_copy(
            src_ref=source,
            dst_ref=target,
            send_sem=self.sems.at[0, kind],
            recv_sem=self.sems.at[1, kind],
            device_id=where,
            device_id_type=MESH,
        )

    def own(self):
        return self.source.at[pl.ds(self.low, self.length)]

    def ahead(self, j):
        return lax.rem(self.f + j, self.fsdp)

    def behind(self, j):
        return lax.rem(self.f + self.fsdp - j, self.fsdp)

    def to_across(self):
        return self.copy(0, self.own(), self.at(self.f, self.me), {"ctx": self.across})

    def to_other(self):
        return self.copy(1, self.own(), self.at(self.f, self.me), {"ctx": self.other})

    def across_to_other(self):
        at = self.at(self.f, self.across)
        return self.copy(2, at, at, {"ctx": self.other})

    def to_ahead(self, j):
        return self.copy(3 * j, self.own(), self.at(self.f, self.me), {"fsdp": self.ahead(j)})

    def behind_to_other(self, j):
        at = self.at(self.behind(j), self.me)
        return self.copy(3 * j + 1, at, at, {"ctx": self.other})

    def corner_to_other(self, j):
        at = self.at(self.behind(j), self.across)
        return self.copy(3 * j + 2, at, at, {"ctx": self.other})

    def across_to_ahead(self, j):
        at = self.at(self.f, self.across, 0, self.first)
        return self.copy(3 * self.fsdp + 2 * j - 2, at, at, {"fsdp": self.ahead(j)})

    def behind_to_across(self, j):
        at = self.at(self.behind(j), self.me, self.first, self.length - self.first)
        return self.copy(3 * self.fsdp + 2 * j - 1, at, at, {"ctx": self.across})

    def local(self):
        return pltpu.make_async_copy(self.own(), self.at(self.f, self.me), self.sems.at[2, 0])

    def start(self):
        self.start_across()
        self.start_ahead()

    def start_across(self):
        self.to_across().start()

    def start_ahead(self):
        for j in range(1, self.fsdp):
            self.to_ahead(j).start()
        self.to_other().start()
        self.local().start()

    def forward(self):
        self.forward_across()
        self.forward_behind()

    def forward_across(self):
        self.to_across().wait_recv()
        for j in range(1, self.fsdp):
            self.across_to_ahead(j).start()
        self.across_to_other().start()

    def forward_behind(self):
        for j in range(1, self.fsdp):
            self.to_ahead(j).wait_recv()
            self.behind_to_across(j).start()
            self.behind_to_other(j).start()

    def corner(self):
        for j in range(1, self.fsdp):
            self.across_to_ahead(j).wait_recv()
            self.behind_to_across(j).wait_recv()
            self.corner_to_other(j).start()

    def finish(self):
        self.local().wait()
        self.to_other().wait_recv()
        self.across_to_other().wait_recv()
        for j in range(1, self.fsdp):
            self.behind_to_other(j).wait_recv()
            self.corner_to_other(j).wait_recv()

    def drain(self):
        self.to_across().wait_send()
        self.to_other().wait_send()
        self.across_to_other().wait_send()
        for j in range(1, self.fsdp):
            self.to_ahead(j).wait_send()
            self.behind_to_other(j).wait_send()
            self.corner_to_other(j).wait_send()
            self.across_to_ahead(j).wait_send()
            self.behind_to_across(j).wait_send()


def gather_sems(fsdp):
    return pltpu.SemaphoreType.DMA((3, 5 * fsdp - 2))


def front_body(
    n,
    tp,
    fsdp,
    groups,
    token_ref,
    in_ref,
    tail_ref,
    out_weight_ref,
    gate_up_ref,
    down_ref,
    cos_ref,
    sin_ref,
    cotangent_ref,
    order_ref,
    length_ref,
    in_whole_ref,
    out_whole_ref,
    pair_whole_ref,
    normal_out_ref,
    grad_out_ref,
    gain_ref,
    q_ref,
    kv_ref,
    full_ref,
    low_ref,
    log_ref,
    residual_ref,
    out_ref,
    in_whole,
    out_whole,
    normal_ref,
    in_pack,
    out_pack,
    pair_pack,
    staged,
    proj,
    bias,
    parts,
    load_sem,
    save_sem,
    send_sem,
    recv_sem,
    in_sems,
    out_sems,
    pair_sems,
    inbox,
    *sems,
):
    z = lax.axis_index("tp")
    f = lax.axis_index("fsdp")
    me = lax.axis_index("ctx")
    peers = line_greet(tp, z)
    barrier = pltpu.get_barrier_semaphore()
    for step in range(1, n):
        pl.semaphore_signal(
            barrier, inc=1, device_id={"ctx": lax.rem(me + step, n)}, device_id_type=MESH
        )
    for step in range(1, fsdp):
        pl.semaphore_signal(
            barrier, inc=1, device_id={"fsdp": lax.rem(f + step, fsdp)}, device_id_type=MESH
        )

    seqs, _, rows = q_ref.shape
    dim = HEAD_DIMENSION
    half = dim // 2
    group_width = (GROUP + 2) * dim
    in_width = groups * group_width
    heads = groups * GROUP
    width = token_ref.shape[1]
    tile = 512 if width % 512 == 0 else width
    block = in_ref.shape[0]
    pair_width = gate_up_ref.shape[1]
    whole_tiles = in_width // 128 * 128

    ranges = cut(block, pair_sems.shape[0])

    def loads(i):
        low, length = ranges[i]
        return [
            pltpu.make_async_copy(
                source.at[pl.ds(low, length)],
                staged.at[i % 2, pl.ds(0, length), pl.ds(first, source.shape[1])],
                load_sem.at[i % 2, at],
            )
            for at, (source, first) in enumerate(((gate_up_ref, 0), (down_ref, pair_width)))
        ]

    for load in loads(0):
        load.start()
    cotangent = pltpu.make_async_copy(cotangent_ref, parts, load_sem.at[2, 0])
    grad_out = pltpu.make_async_copy(parts, grad_out_ref, load_sem.at[2, 1])
    cotangent.start()
    in_pack[:, :whole_tiles] = in_ref[:, :whole_tiles].astype(jnp.bfloat16)
    in_pack[:, whole_tiles:] = tail_ref[...]
    out_pack[...] = out_weight_ref[...].astype(jnp.bfloat16)
    pl.semaphore_wait(barrier, peers + n - 1 + fsdp - 1)

    def gathers(source, whole, sems):
        return [
            Gather(source, whole, low, length, block, fsdp, n, sems.at[i])
            for i, (low, length) in enumerate(cut(block, sems.shape[0]))
        ]

    first = gathers(in_pack, in_whole, in_sems)
    outer = gathers(out_pack, out_whole, out_sems)
    pair = gathers(pair_pack, pair_whole_ref, pair_sems)
    for piece in first:
        piece.start()
    for i, (low, length) in enumerate(ranges):
        if i + 1 < len(ranges):
            for load in loads(i + 1):
                load.start()
        for load in loads(i):
            load.wait()
        pair_pack[low : low + length, :] = staged[i % 2, :length, :].astype(jnp.bfloat16)

    cotangent.wait()
    span = rows // 2

    def keep(at, carry):
        own = pl.ds(pl.multiple_of(at * span, CHUNK), span)
        m = at // 2
        position = order_ref[m, 2 * me + lax.rem(at, 2)] * span + lax.broadcasted_iota(
            jnp.int32, (span, width), 0
        )
        parts[own, :] = jnp.where(
            position < length_ref[m], parts[own, :].astype(jnp.float32), 0.0
        ).astype(jnp.bfloat16)
        return carry

    lax.fori_loop(0, 2 * seqs, keep, 0)
    grad_out.start()
    for piece in first:
        piece.forward()
    for piece in outer:
        piece.start()
    for piece in first:
        piece.corner()
    for piece in first:
        piece.finish()
    for piece in outer:
        piece.forward()
    for piece in pair:
        piece.start_ahead()
    saves = [
        pltpu.make_async_copy(in_whole, in_whole_ref, save_sem.at[0]),
        pltpu.make_async_copy(normal_ref, normal_out_ref, save_sem.at[1]),
        pltpu.make_async_copy(out_whole, out_whole_ref, save_sem.at[2]),
    ]
    saves[0].start()

    turned = in_whole[:, whole_tiles : whole_tiles + 128].astype(jnp.float32).T
    gain_ref[...] = turned[in_width - whole_tiles : in_width - whole_tiles + 8]

    def columns_of(m):
        return pl.ds(pl.multiple_of(m * rows, 128), rows)

    def rows_of(m):
        return pl.ds(pl.multiple_of(m * rows, CHUNK), rows)

    def copy(m, step):
        return pltpu.make_async_remote_copy(
            src_ref=kv_ref.at[m, me],
            dst_ref=kv_ref.at[m, me],
            send_sem=send_sem.at[m, step - 1],
            recv_sem=recv_sem.at[m, step - 1],
            device_id={"ctx": lax.rem(me + step, n)},
            device_id_type=MESH,
        )

    def project(m, carry):
        values = token_ref[rows_of(m), :].astype(jnp.float32)
        root = lax.rsqrt(mean_of(values * values) + norm_eps)
        normal_ref[rows_of(m), :] = (values * root * gain_ref[0:1, :]).astype(jnp.bfloat16)
        proj[m] = jnp.dot(
            normal_ref[rows_of(m), :],
            in_whole[:, :in_width],
            preferred_element_type=jnp.float32,
        ).T
        for g in range(groups):
            col = g * group_width + GROUP * dim
            kv_ref[m, me, g, :dim, :] = turn(
                proj[m, col : col + half, :],
                proj[m, col + half : col + dim, :],
                cos_ref[m],
                sin_ref[m],
            ).astype(jnp.bfloat16)
            kv_ref[m, me, g, dim:, :] = proj[m, col + dim : col + 2 * dim, :].astype(jnp.bfloat16)
        for step in range(1, n):
            copy(m, step).start()
        return carry

    lax.fori_loop(0, seqs, project, 0)
    for piece in pair:
        piece.start_across()
    saves[1].start()

    def finish(segment, at, total):
        values = token_ref[at, :].astype(jnp.float32) + total
        residual_ref[at, :] = values.astype(jnp.bfloat16)
        root = lax.rsqrt(mean_of(values * values) + norm_eps)
        out_ref[at, :] = (values * root * gain_ref[1:2, :]).astype(jnp.bfloat16)

    line = Line(tp, z, seqs, rows, parts, inbox, out_ref, sems, finish)

    def head(m, at):
        g = at // GROUP
        h = at % GROUP
        low = pl.ds(pl.multiple_of(at * dim, 16), dim)
        col = pl.multiple_of(g * group_width + h * dim, 8)
        query = turn(
            proj[m, pl.ds(col, half), :],
            proj[m, pl.ds(pl.multiple_of(col + half, 8), half), :],
            cos_ref[m],
            sin_ref[m],
        ).astype(jnp.bfloat16)
        q_ref[m, low, :] = query
        scores = [
            lax.dot_general(
                kv_ref[m, j, g, :dim, :],
                query,
                (((0,), (0,)), ((), ())),
                preferred_element_type=jnp.float32,
            )
            * (log2_e * dim**-0.5)
            + bias[j * rows : (j + 1) * rows, :]
            for j in range(n)
        ]
        top = functools.reduce(jnp.maximum, [jnp.max(s, axis=0, keepdims=True) for s in scores])
        total = jnp.zeros_like(top)
        out = jnp.zeros((dim, rows), jnp.float32)
        for j in range(n):
            weights = jnp.exp2(scores[j] - top)
            total += jnp.sum(weights, axis=0, keepdims=True)
            out += jnp.dot(
                kv_ref[m, j, g, dim:, :],
                weights.astype(jnp.bfloat16),
                preferred_element_type=jnp.float32,
            )
        out = out / total
        full_ref[m, low, :] = out
        low_ref[low, columns_of(m)] = out.astype(jnp.bfloat16)
        log_ref[m, at] = top + jnp.log2(total)

    def ready(m):
        fill_bias(bias, order_ref, length_ref, m, me, n)
        for step in range(1, n):
            copy(m, step).wait_recv()

    def product(m):
        left = low_ref[:, columns_of(m)].T
        for low in range(0, width, tile):
            parts[rows_of(m), low : low + tile] = lax.dot_general(
                left,
                out_whole[low : low + tile, :],
                (((1,), (1,)), ((), ())),
                preferred_element_type=jnp.float32,
            ).astype(jnp.bfloat16)

    def sequence(m, carry):
        ready(m)

        def item(at, inner):
            line.tick((m - 1) * heads + at)
            head(m, at)
            return inner

        lax.fori_loop(0, heads, item, 0)
        product(m)
        return carry

    def opening(at, carry):
        head(0, at)
        return carry

    ready(0)
    lax.fori_loop(0, heads, opening, 0)
    grad_out.wait()
    for piece in outer:
        piece.corner()
    for piece in outer:
        piece.finish()
    saves[2].start()
    product(0)
    pair[0].forward_behind()
    lax.fori_loop(1, 2, sequence, 0)
    for piece in pair[1:2]:
        piece.forward_behind()
    lax.fori_loop(2, seqs, sequence, 0)
    at = (seqs - 1) * heads
    for piece in pair[2:3]:
        piece.forward_behind()
    pair[0].forward_across()
    line.run(at, at + 2)
    for piece in pair[3:]:
        piece.forward_behind()
    line.run(at + 2, at + 4)
    for piece in pair[1:2]:
        piece.forward_across()
    line.run(at + 4, at + 10)
    for piece in pair[2:3]:
        piece.forward_across()
    line.run(at + 10, at + 16)
    for piece in pair[3:]:
        piece.forward_across()
    line.run(at + 16, line.ticks)
    for piece in pair:
        piece.corner()
    for piece in pair:
        piece.finish()
    line.drain()
    for piece in first + outer + pair:
        piece.drain()
    for save in saves:
        save.wait()

    def drain(m, carry):
        for step in range(1, n):
            copy(m, step).wait_send()
        return carry

    lax.fori_loop(0, seqs, drain, 0)


def front(
    tokens, cotangent, in_weight, tail, out_weight, gate_up, down, where, seqs, n, tp, fsdp, ident
):
    all_rows, model_width = tokens.shape
    cosine, sine, orders, lengths = where
    rows = all_rows // seqs
    block, in_width = in_weight.shape
    groups = in_width // ((GROUP + 2) * HEAD_DIMENSION)
    heads = groups * GROUP
    shards = n * fsdp
    dim = HEAD_DIMENSION
    padded = in_width // 128 * 128 + tail.shape[1]
    out_width = out_weight.shape[1]
    pair_width = gate_up.shape[1] + down.shape[1]
    pieces = min(4, block // 32)
    longest = max(length for _, length in cut(block, pieces))
    shape = jax.ShapeDtypeStruct
    low, wide = jnp.bfloat16, jnp.float32
    vmem = pl.BlockSpec(memory_space=VMEM)
    hbm = pl.BlockSpec(memory_space=pl.ANY)
    smem = pl.BlockSpec(memory_space=pltpu.SMEM)
    dma = pltpu.SemaphoreType.DMA
    gather_sems = (3, 5 * fsdp - 2)
    return pl.pallas_call(
        functools.partial(front_body, n, tp, fsdp, groups),
        out_shape=(
            shape((shards * block, padded), low),
            shape((shards * block, out_width), low),
            shape((shards * block, pair_width), low),
            shape((all_rows, model_width), low),
            shape((all_rows, model_width), low),
            shape((8, model_width), wide),
            shape((seqs, heads * dim, rows), low),
            shape((seqs, n, groups, 2 * dim, rows), low),
            shape((seqs, heads * dim, rows), wide),
            shape((heads * dim, all_rows), low),
            shape((seqs, heads, 1, rows), wide),
            shape((all_rows, model_width), low),
            shape((all_rows, model_width), low),
        ),
        in_specs=[vmem] * 4 + [hbm] * 2 + [vmem] * 2 + [hbm] + [smem] * 2,
        out_specs=(hbm,) * 5 + (vmem,) * 8,
        scratch_shapes=[
            VMEM((shards * block, padded), low),
            VMEM((shards * block, out_width), low),
            VMEM((all_rows, model_width), low),
            VMEM((block, padded), low),
            VMEM((block, out_width), low),
            VMEM((block, pair_width), low),
            VMEM((2, longest, pair_width), wide),
            VMEM((seqs, in_width, rows), wide),
            VMEM((n * rows, rows), wide),
            VMEM((all_rows, model_width), low),
            dma((3, 2)),
            dma((3,)),
            dma((seqs, n - 1)),
            dma((seqs, n - 1)),
            dma((min(2, pieces),) + gather_sems),
            dma((1,) + gather_sems),
            dma((pieces,) + gather_sems),
        ]
        + line_scratch(all_rows, model_width, seqs, rows),
        compiler_params=pltpu.CompilerParams(
            collective_id=ident, has_side_effects=True, vmem_limit_bytes=60 * 2**20
        ),
        cost_estimate=line_cost(all_rows, model_width),
        name="front",
    )(tokens, in_weight, tail, out_weight, gate_up, down, cosine, sine, cotangent, orders, lengths)


def back_one_body(
    n,
    tp,
    groups,
    late,
    gate_ref,
    up_ref,
    pair_ref,
    gain_ref,
    log_ref,
    cos_ref,
    sin_ref,
    inner_from,
    residual_from,
    grad_out_from,
    weight_from,
    q_from,
    kv_from,
    full_from,
    early_from,
    order_ref,
    length_ref,
    grad_to,
    mixed_to,
    proj_ref,
    gain_sums,
    out_ref,
    parts,
    weights,
    inner_ref,
    residual_ref,
    grad_out_ref,
    out_proj,
    q_ref,
    kv_ref,
    full_ref,
    grads,
    sums,
    bias,
    outbox,
    kv_inbox,
    load_sem,
    save_sem,
    weight_sem,
    send_sem,
    recv_sem,
    inbox,
    *sems,
):
    z = lax.axis_index("tp")
    me = lax.axis_index("ctx")
    seqs, _, rows = q_ref.shape
    all_rows = seqs * rows
    units = inner_ref.shape[1]
    tile = weights.shape[1]
    pieces = out_ref.shape[1] // tile
    loads = [
        pltpu.make_async_copy(source, target, load_sem.at[at])
        for at, (source, target) in enumerate(
            (
                (inner_from, inner_ref),
                (residual_from, residual_ref),
                (grad_out_from, grad_out_ref),
                (weight_from, out_proj),
                (q_from, q_ref),
                (kv_from, kv_ref),
                (full_from, full_ref),
            )
        )
    ]

    early_rows = all_rows - late * rows
    saves = [
        pltpu.make_async_copy(early_from, mixed_to.at[pl.ds(0, early_rows)], save_sem.at[0]),
        pltpu.make_async_copy(out_ref.at[pl.ds(rows, all_rows)], grad_to, save_sem.at[1]),
        pltpu.make_async_copy(
            out_ref.at[pl.ds(0, rows)], mixed_to.at[pl.ds(early_rows, rows)], save_sem.at[2]
        ),
    ]
    if late > 1:
        saves.append(
            pltpu.make_async_copy(
                out_ref.at[pl.ds(rows + all_rows, (late - 1) * rows)],
                mixed_to.at[pl.ds(early_rows + rows, (late - 1) * rows)],
                save_sem.at[3],
            )
        )

    def tile_of(at):
        return pl.ds(pl.multiple_of(at * tile, tile), tile)

    def fetch(at):
        slot = lax.rem(at, 2)
        return pltpu.make_async_copy(
            pair_ref.at[tile_of(lax.rem(at, pieces)), pl.ds(0, 2 * units)],
            weights.at[slot],
            weight_sem.at[slot],
        )

    def fetch_down(at):
        slot = lax.rem(at, 2)
        return pltpu.make_async_copy(
            pair_ref.at[tile_of(at), pl.ds(2 * units, units)],
            weights.at[slot, :, pl.ds(0, units)],
            weight_sem.at[slot],
        )

    fetch_down(0).start()
    for load in loads:
        load.start()
    saves[0].start()
    peers = line_greet(tp, z)
    barrier = pltpu.get_barrier_semaphore()
    for step in range(1, n):
        pl.semaphore_signal(
            barrier, inc=1, device_id={"ctx": lax.rem(me + step, n)}, device_id_type=MESH
        )
    pl.semaphore_wait(barrier, peers + n - 1)

    dim = HEAD_DIMENSION
    half = dim // 2
    scale = dim**-0.5
    group_width = (GROUP + 2) * dim
    heads = groups * GROUP
    gain_sums[...] = jnp.zeros_like(gain_sums)

    ahead = rows
    first_late = seqs - late

    def finish(segment, at, total):
        is_grad = (segment >= 1) & (segment <= seqs)

        @pl.when(is_grad)
        def _():
            own = pl.ds(pl.multiple_of(at.start - ahead, CHUNK), CHUNK)
            grad = norm_back(
                total, residual_ref[own, :].astype(jnp.float32), gain_ref[1:2, :], gain_sums
            )
            out_ref[at, :] = (grad_out_ref[own, :].astype(jnp.float32) + grad).astype(jnp.bfloat16)

        @pl.when(jnp.logical_not(is_grad))
        def _():
            moved = jnp.where(segment == 0, first_late * rows, (first_late - seqs) * rows)
            own = pl.ds(pl.multiple_of(at.start + moved, CHUNK), CHUNK)
            out_ref[at, :] = (residual_ref[own, :].astype(jnp.float32) + total).astype(jnp.bfloat16)

    line = Line(tp, z, seqs + late, rows, parts, inbox, out_ref, sems, finish)

    def copy(m, step):
        to = lax.rem(me + step, n)
        return pltpu.make_async_remote_copy(
            src_ref=outbox.at[m, to],
            dst_ref=kv_inbox.at[m, step - 1],
            send_sem=send_sem.at[m, step - 1],
            recv_sem=recv_sem.at[m, step - 1],
            device_id={"ctx": to},
            device_id_type=MESH,
        )

    def columns(m):
        return pl.ds(pl.multiple_of(m * rows, 128), rows)

    def attended_grads(m):
        grads[...] = (
            jnp.dot(
                out_ref[pl.ds(pl.multiple_of(ahead + m * rows, CHUNK), rows), :],
                out_proj[...],
                preferred_element_type=jnp.float32,
            )
            .T.astype(jnp.bfloat16)
        )
        fill_bias(bias, order_ref, length_ref, m, me, n)

    def head(m, at):
        g = at // GROUP
        h = at % GROUP
        low = pl.ds(pl.multiple_of(at * dim, 16), dim)
        query = q_ref[m, low, :]
        grad = grads[low, :]
        delta = jnp.sum(
            grad.astype(jnp.float32) * full_ref[m, low, :], axis=0, keepdims=True
        )
        log_total = log_ref[m, at]
        query_sum = jnp.zeros((dim, rows), jnp.float32)

        @pl.when(h == 0)
        def _():
            sums[...] = jnp.zeros_like(sums)

        for j in range(n):
            keys = kv_ref[m, j, g, :dim, :]
            values = kv_ref[m, j, g, dim:, :]
            scores = lax.dot_general(
                keys, query, (((0,), (0,)), ((), ())), preferred_element_type=jnp.float32
            )
            probs = jnp.exp2(
                scores * (log2_e * scale) + (bias[j * rows : (j + 1) * rows, :] - log_total)
            )
            grad_probs = lax.dot_general(
                values, grad, (((0,), (0,)), ((), ())), preferred_element_type=jnp.float32
            )
            grad_scores = (probs * (grad_probs - delta)).astype(jnp.bfloat16)
            query_sum += jnp.dot(keys, grad_scores, preferred_element_type=jnp.float32)
            sums[j, :dim, :] += lax.dot_general(
                query, grad_scores, (((1,), (1,)), ((), ())), preferred_element_type=jnp.float32
            )
            sums[j, dim:, :] += lax.dot_general(
                grad,
                probs.astype(jnp.bfloat16),
                (((1,), (1,)), ((), ())),
                preferred_element_type=jnp.float32,
            )
        query_sum = query_sum * scale
        col = pl.ds(pl.multiple_of(g * group_width + h * dim, 16), dim)
        proj_ref[col, columns(m)] = turn_back(
            query_sum[:half], query_sum[half:], cos_ref[m], sin_ref[m]
        ).astype(jnp.bfloat16)

        @pl.when(h == GROUP - 1)
        def _():
            for j in range(n):
                outbox[m, j, g, :dim, :] = (sums[j, :dim, :] * scale).astype(jnp.bfloat16)
                outbox[m, j, g, dim:, :] = sums[j, dim:, :].astype(jnp.bfloat16)

    def gather(m):
        for step in range(1, n):
            copy(m, step).wait_recv()
        for g in range(groups):
            total = outbox[m, me, g].astype(jnp.float32)
            for step in range(1, n):
                total += kv_inbox[m, step - 1, g].astype(jnp.float32)
            col = g * group_width + GROUP * dim
            proj_ref[col : col + dim, columns(m)] = turn_back(
                total[:half], total[half:dim], cos_ref[m], sin_ref[m]
            ).astype(jnp.bfloat16)
            proj_ref[col + dim : col + 2 * dim, columns(m)] = total[dim:].astype(jnp.bfloat16)
        for step in range(1, n):
            copy(m, step).wait_send()

    contract = (((1,), (1,)), ((), ()))
    ticks_ahead = line.per_segment

    def leave(m, tile_at):
        at = m * pieces + tile_at
        own = pl.ds(pl.multiple_of(m * rows, CHUNK), rows)
        slot = lax.rem(at, 2)

        @pl.when(at + 1 < seqs * pieces)
        def _():
            fetch(at + 1).start()

        fetch(at).wait()
        parts[pl.ds(pl.multiple_of(ahead + m * rows, CHUNK), rows), tile_of(tile_at)] = (
            lax.dot_general(
                gate_ref[own, :],
                weights[slot, :, :units],
                contract,
                preferred_element_type=jnp.float32,
            )
            + lax.dot_general(
                up_ref[own, :],
                weights[slot, :, units:],
                contract,
                preferred_element_type=jnp.float32,
            )
        ).astype(jnp.bfloat16)

    def expand(low, count, to, first_tick):
        def item(at, carry):
            if first_tick is not None:

                @pl.when(at < ticks_ahead)
                def _():
                    line.tick(first_tick + at)

            @pl.when(at + 1 < pieces)
            def _():
                fetch_down(at + 1).start()

            fetch_down(at).wait()
            parts[pl.ds(to, count * rows), tile_of(at)] = lax.dot_general(
                inner_ref[pl.ds(low * rows, count * rows), :],
                weights[lax.rem(at, 2), :, :units],
                contract,
                preferred_element_type=jnp.float32,
            ).astype(jnp.bfloat16)
            return carry

        lax.fori_loop(0, pieces, item, 0)

    loads[0].wait()
    expand(first_late, 1, 0, None)
    fetch(0).start()
    for load in loads[1:]:
        load.wait()

    def next_leave(m, carry):
        def item(tile_at, inner):
            @pl.when(tile_at < ticks_ahead)
            def _():
                line.tick(m * ticks_ahead + tile_at)

            leave(m, tile_at)
            return inner

        lax.fori_loop(0, pieces, item, 0)
        return carry

    lax.fori_loop(0, seqs, next_leave, 0)
    done = seqs * ticks_ahead
    if late > 1:
        fetch_down(0).start()
        expand(first_late + 1, late - 1, rows + all_rows, done)
        done += ticks_ahead
    opened = max(done, line.ready(2))
    line.run(done, opened)
    stride = max(heads // 2 + 1, -(-(line.ready(seqs + 1) - opened) // (seqs - 1)))

    def sequence(m, carry):
        first = opened + m * stride
        line.tick(first)
        attended_grads(m)

        def item(at, inner):
            @pl.when(lax.rem(at, 2) == 0)
            def _():
                line.tick(first + 1 + at // 2)

            head(m, at)
            return inner

        lax.fori_loop(0, heads, item, 0)
        line.run(first + 1 + heads // 2, first + stride)
        for step in range(1, n):
            copy(m, step).start()

        @pl.when(m > 0)
        def _():
            gather(m - 1)

        return carry

    lax.fori_loop(0, seqs, sequence, 0)
    saves[1].start()
    line.run(opened + seqs * stride, line.ticks)

    for save in saves[2:]:
        save.start()
    gather(seqs - 1)
    line.drain()
    for save in saves:
        save.wait()


def back_one(
    inner,
    grad_gate,
    grad_up,
    pair_whole,
    mixed_early,
    residual,
    grad_out,
    gains,
    out_whole,
    queries,
    key_values,
    full,
    log_total,
    where,
    n,
    tp,
    ident,
):
    seqs, width, rows = queries.shape
    groups = key_values.shape[2]
    all_rows, model_width = residual.shape
    late = seqs - mixed_early.shape[0] // rows
    cosine, sine, orders, lengths = where
    units = inner.shape[1]
    line_rows = all_rows + late * rows
    vmem = pl.BlockSpec(memory_space=VMEM)
    hbm = pl.BlockSpec(memory_space=pl.ANY)
    smem = pl.BlockSpec(memory_space=pltpu.SMEM)
    shape = jax.ShapeDtypeStruct
    return pl.pallas_call(
        functools.partial(back_one_body, n, tp, groups, late),
        out_shape=(
            shape((all_rows, model_width), jnp.bfloat16),
            shape((all_rows, model_width), jnp.bfloat16),
            shape((groups * (GROUP + 2) * HEAD_DIMENSION, all_rows), jnp.bfloat16),
            shape((8, model_width), jnp.float32),
        ),
        in_specs=[vmem] * 2 + [hbm] + [vmem] * 4 + [hbm] * 8 + [smem] * 2,
        out_specs=(hbm,) * 2 + (vmem,) * 2,
        scratch_shapes=[
            VMEM((line_rows, model_width), jnp.bfloat16),
            VMEM((line_rows, model_width), jnp.bfloat16),
            VMEM((2, 256, 2 * units), jnp.bfloat16),
            VMEM((all_rows, units), jnp.bfloat16),
            VMEM((all_rows, model_width), jnp.bfloat16),
            VMEM((all_rows, model_width), jnp.bfloat16),
            VMEM((model_width, width), jnp.bfloat16),
            VMEM(queries.shape, jnp.bfloat16),
            VMEM(key_values.shape, jnp.bfloat16),
            VMEM(full.shape, jnp.float32),
            VMEM((width, rows), jnp.bfloat16),
            VMEM((n, 2 * HEAD_DIMENSION, rows), jnp.float32),
            VMEM((n * rows, rows), jnp.float32),
            VMEM((seqs, n, groups, 2 * HEAD_DIMENSION, rows), jnp.bfloat16),
            VMEM((seqs, n - 1, groups, 2 * HEAD_DIMENSION, rows), jnp.bfloat16),
            pltpu.SemaphoreType.DMA((7,)),
            pltpu.SemaphoreType.DMA((4,)),
            pltpu.SemaphoreType.DMA((2,)),
            pltpu.SemaphoreType.DMA((seqs, n - 1)),
            pltpu.SemaphoreType.DMA((seqs, n - 1)),
        ]
        + line_scratch(line_rows, model_width, seqs + late, rows),
        compiler_params=pltpu.CompilerParams(
            collective_id=ident, has_side_effects=True, vmem_limit_bytes=60 * 2**20
        ),
        cost_estimate=line_cost(line_rows, model_width),
        name="back_one",
    )(
        grad_gate,
        grad_up,
        pair_whole,
        gains,
        log_total,
        cosine,
        sine,
        inner,
        residual,
        grad_out,
        out_whole,
        queries,
        key_values,
        full,
        mixed_early,
        orders,
        lengths,
    )


def back_two_body(
    n,
    fsdp,
    tp,
    seqs,
    skip,
    proj_ref,
    weight_ref,
    gain_ref,
    second_gain_ref,
    token_from,
    residual_grad_from,
    out_ref,
    gains_to,
    gain_sums,
    token_ref,
    residual_grad_ref,
    parts,
    mine,
    box,
    tp_mine,
    tp_box,
    load_sem,
    gain_sem,
    tp_sem,
    inbox,
    *sems,
):
    z = lax.axis_index("tp")
    loads = [
        pltpu.make_async_copy(token_from, token_ref, load_sem.at[0]),
        pltpu.make_async_copy(
            residual_grad_from.at[pl.ds(0, residual_grad_ref.shape[0])],
            residual_grad_ref,
            load_sem.at[1],
        ),
    ]
    for load in loads:
        load.start()
    me = lax.axis_index("fsdp") * n + lax.axis_index("ctx")
    shards = n * fsdp

    def shard_at(step):
        other = lax.rem(me + step, shards)
        return {"fsdp": other // n, "ctx": lax.rem(other, n)}

    def line_at(step):
        return {"tp": lax.rem(z + step, tp)}

    barrier = pltpu.get_barrier_semaphore()
    for step in range(1, shards):
        pl.semaphore_signal(barrier, inc=1, device_id=shard_at(step), device_id_type=MESH)
    for step in range(1, tp):
        pl.semaphore_signal(barrier, inc=1, device_id=line_at(step), device_id_type=MESH)
    pl.semaphore_wait(barrier, shards - 1 + tp - 1)
    gain_sums[...] = jnp.zeros_like(gain_sums)
    rows = token_ref.shape[0] // seqs
    width = weight_ref.shape[0]
    tile = 512 if width % 512 == 0 else width

    def finish(segment, at, total):
        values = token_ref[at, :].astype(jnp.float32)
        grad = norm_back(total, values, gain_ref[0:1, :], gain_sums)
        out_ref[at, :] = (residual_grad_ref[at, :].astype(jnp.float32) + grad).astype(jnp.bfloat16)

    line = Line(tp, z, seqs, rows, parts, inbox, out_ref, sems, finish)

    def product(m):
        left = proj_ref[:, m * rows : (m + 1) * rows].T
        for low in range(0, width, tile):
            parts[m * rows : (m + 1) * rows, low : low + tile] = lax.dot_general(
                left,
                weight_ref[low : low + tile, skip : skip + proj_ref.shape[0]],
                (((1,), (1,)), ((), ())),
                preferred_element_type=jnp.float32,
            ).astype(jnp.bfloat16)

    for m in range(seqs):
        product(m)
        line.run(2 * m, 2 * m + 2)
        if m == 0:
            for load in loads:
                load.wait()
    finished = line.chunks + (tp - 1) * LAG
    line.run(2 * seqs, finished)
    mine[...] = jnp.zeros_like(mine)
    mine[0:1, :] = jnp.sum(gain_sums[...], axis=0, keepdims=True)
    mine[1:2, :] = jnp.sum(second_gain_ref[...], axis=0, keepdims=True)

    def copy(source, boxes, sem, step, where):
        return pltpu.make_async_remote_copy(
            src_ref=source,
            dst_ref=boxes.at[step - 1],
            send_sem=sem.at[0, step - 1],
            recv_sem=sem.at[1, step - 1],
            device_id=where,
            device_id_type=MESH,
        )

    for step in range(1, shards):
        copy(mine, box, gain_sem, step, shard_at(step)).start()
    line.run(finished, line.ticks)
    total = mine[...]
    for step in range(1, shards):
        copy(mine, box, gain_sem, step, shard_at(step)).wait()
        total += box[step - 1]
    tp_mine[...] = total
    for step in range(1, tp):
        copy(tp_mine, tp_box, tp_sem, step, line_at(step)).start()
    for step in range(1, tp):
        copy(tp_mine, tp_box, tp_sem, step, line_at(step)).wait()
        total += tp_box[step - 1]
    gains_to[...] = total
    line.drain()


def back_two(
    projected, first_whole, tokens, residual_grad, gains, second_gain, skip, seqs, n, fsdp, tp, ident
):
    rows, width = tokens.shape
    vmem = pl.BlockSpec(memory_space=VMEM)
    hbm = pl.BlockSpec(memory_space=pl.ANY)
    shape = jax.ShapeDtypeStruct
    return pl.pallas_call(
        functools.partial(back_two_body, n, fsdp, tp, seqs, skip),
        out_shape=(shape((rows, width), jnp.bfloat16), shape((8, width), jnp.float32)),
        in_specs=[vmem] * 4 + [hbm] * 2,
        out_specs=(vmem,) * 2,
        scratch_shapes=[VMEM((8, width), jnp.float32)]
        + [VMEM((rows, width), jnp.bfloat16)] * 3
        + [
            VMEM((8, width), jnp.float32),
            VMEM((n * fsdp - 1, 8, width), jnp.float32),
            VMEM((8, width), jnp.float32),
            VMEM((tp - 1, 8, width), jnp.float32),
            pltpu.SemaphoreType.DMA((2,)),
            pltpu.SemaphoreType.DMA((2, n * fsdp - 1)),
            pltpu.SemaphoreType.DMA((2, tp - 1)),
        ]
        + line_scratch(rows, width, seqs, rows // seqs),
        compiler_params=pltpu.CompilerParams(
            collective_id=ident, has_side_effects=True, vmem_limit_bytes=56 * 2**20
        ),
        cost_estimate=line_cost(rows, width),
        name="back_two",
    )(projected, first_whole, gains, second_gain, tokens, residual_grad)


def hidden_body(
    tp,
    seqs,
    early,
    normal_ref,
    grad_out_ref,
    residual_ref,
    whole_ref,
    grads_ref,
    inner_ref,
    gate_ref,
    up_ref,
    out_ref,
    residual,
    turned,
    staged,
    columns,
    weights,
    parts,
    load_sem,
    column_sem,
    weight_sem,
    store_sem,
    inbox,
    *sems,
):
    z = lax.axis_index("tp")
    rows, units = inner_ref.shape
    width = normal_ref.shape[1]
    tile = staged.shape[2]
    pieces = width // tile
    steps = units // tile
    early_rows = parts.shape[0]

    def columns_of(at):
        return pl.ds(pl.multiple_of(at * tile, tile), tile)

    def fetch_columns(at):
        slot = lax.rem(at, 2)
        return [
            pltpu.make_async_copy(
                whole_ref.at[:, columns_of(kind * steps + lax.rem(at, steps))],
                columns.at[slot, kind],
                column_sem.at[slot, kind],
            )
            for kind in range(3)
        ]

    def fetch(at):
        slot = lax.rem(at, 2)
        return pltpu.make_async_copy(
            whole_ref.at[columns_of(at), pl.ds(2 * units, units)],
            weights.at[slot],
            weight_sem.at[slot],
        )

    load = pltpu.make_async_copy(
        residual_ref.at[pl.ds(0, early_rows)], residual, load_sem.at[0]
    )
    for copy in fetch_columns(0):
        copy.start()
    load.start()
    pl.semaphore_wait(pltpu.get_barrier_semaphore(), line_greet(tp, z))

    def finish(segment, at, total):
        out_ref[at, :] = (residual[at, :].astype(jnp.float32) + total).astype(jnp.bfloat16)

    line = Line(tp, z, early, rows // seqs, parts, inbox, out_ref, sems, finish)

    early_opening = rows // seqs

    def units_of(at, low, high):
        slot = lax.rem(at, 2)

        @pl.when(at + 1 < 2 * steps)
        def _():
            for copy in fetch_columns(at + 1):
                copy.start()

        for copy in fetch_columns(at):
            copy.wait()

        def product(left, kind):
            return jnp.dot(
                left[low:high, :], columns[slot, kind], preferred_element_type=jnp.float32
            )

        gate = product(normal_ref, 0)
        up = product(normal_ref, 1)
        grad_inner = product(grad_out_ref, 2)
        sigmoid = jax.nn.sigmoid(gate)
        silu = gate * sigmoid
        to = columns_of(lax.rem(at, steps))
        inner_ref[low:high, to] = (silu * up).astype(jnp.bfloat16)
        gate_ref[low:high, to] = (
            grad_inner * up * sigmoid * (1.0 + gate * (1.0 - sigmoid))
        ).astype(jnp.bfloat16)
        up_ref[low:high, to] = (grad_inner * silu).astype(jnp.bfloat16)

    def opening(at, carry):
        units_of(at, 0, early_opening)
        return carry

    fetch(0).start()
    lax.fori_loop(0, steps, opening, 0)

    def expand(low, high):
        def item(at, carry):
            @pl.when(at + 1 < pieces)
            def _():
                fetch(at + 1).start()

            fetch(at).wait()
            parts[low:high, columns_of(at)] = lax.dot_general(
                inner_ref[low:high, :],
                weights[lax.rem(at, 2)],
                (((1,), (1,)), ((), ())),
                preferred_element_type=jnp.float32,
            ).astype(jnp.bfloat16)
            return carry

        lax.fori_loop(0, pieces, item, 0)

    expand(0, early_opening)
    load.wait()

    def others(at, carry):
        line.tick(at)
        units_of(steps + at, early_opening, rows)
        return carry

    if early_rows > early_opening:
        fetch(0).start()
    lax.fori_loop(0, steps, others, 0)
    if early_rows > early_opening:
        expand(early_opening, early_rows)
    turned[...] = normal_ref[...].T

    def store(at):
        slot = lax.rem(at, 2)
        return pltpu.make_async_copy(
            staged.at[slot], grads_ref.at[:, columns_of(at)], store_sem.at[slot]
        )

    for kind, right in enumerate((gate_ref, up_ref, inner_ref)):
        if kind == 2:
            turned[...] = grad_out_ref[...].T

        def gradient(step, carry):
            at = kind * steps + step
            line.tick(steps + at)

            @pl.when(at >= 2)
            def _():
                store(at - 2).wait()

            staged[lax.rem(at, 2)] = jnp.dot(
                turned[...], right[:, columns_of(step)], preferred_element_type=jnp.float32
            ).astype(jnp.bfloat16)
            store(at).start()
            return carry

        lax.fori_loop(0, steps, gradient, 0)

    store(3 * steps - 2).wait()
    store(3 * steps - 1).wait()
    line.run(4 * steps, line.ticks)
    line.drain()


def hidden_units(normal, grad_out, residual, whole, seqs, early, tp, ident):
    all_rows, width = normal.shape
    columns = whole.shape[1]
    units = columns // 3
    rows = all_rows // seqs
    tile = 256
    low = jnp.bfloat16
    shape = jax.ShapeDtypeStruct
    vmem = pl.BlockSpec(memory_space=VMEM)
    hbm = pl.BlockSpec(memory_space=pl.ANY)
    dma = pltpu.SemaphoreType.DMA
    return pl.pallas_call(
        functools.partial(hidden_body, tp, seqs, early),
        out_shape=(shape((width, columns), low),)
        + (shape((all_rows, units), low),) * 3
        + (shape((early * rows, width), low),),
        in_specs=[vmem] * 2 + [hbm] * 2,
        out_specs=(hbm,) + (vmem,) * 4,
        scratch_shapes=[
            VMEM((early * rows, width), low),
            VMEM((width, all_rows), low),
            VMEM((2, width, tile), low),
            VMEM((2, 3, width, tile), low),
            VMEM((2, tile, units), low),
            VMEM((early * rows, width), low),
            dma((1,)),
            dma((2, 3)),
            dma((2,)),
            dma((2,)),
        ]
        + line_scratch(early * rows, width, early, rows),
        compiler_params=pltpu.CompilerParams(
            collective_id=ident, has_side_effects=True, vmem_limit_bytes=60 * 2**20
        ),
        cost_estimate=pl.CostEstimate(
            flops=4 * all_rows * width * columns,
            bytes_accessed=40 * all_rows * width,
            transcendentals=all_rows * units,
        ),
        name="hidden_units",
    )(normal, grad_out, residual, whole)


def first_grads_body(normal_ref, proj_ref, residual_ref, attended_ref, out_ref):
    split = attended_ref.shape[0]
    contract = (((1,), (1,)), ((), ()))
    for left, right, low in ((residual_ref, attended_ref, 0), (normal_ref, proj_ref, split)):
        out_ref[:, low : low + right.shape[0]] = lax.dot_general(
            left[...].T, right[...], contract, preferred_element_type=jnp.float32
        ).astype(jnp.bfloat16)


def first_grads_of(normal, projected, residual_grad, attended):
    rows, width = normal.shape
    columns = projected.shape[0] + attended.shape[0]
    tile = 512 if width % 512 == 0 else width
    vmem = pl.BlockSpec(memory_space=VMEM)
    left = pl.BlockSpec((rows, tile), lambda i: (0, i))
    return pl.pallas_call(
        first_grads_body,
        grid=(width // tile,),
        out_shape=jax.ShapeDtypeStruct((width, columns), jnp.bfloat16),
        in_specs=[left, vmem, left, vmem],
        out_specs=pl.BlockSpec((tile, columns), lambda i: (i, 0)),
        compiler_params=pltpu.CompilerParams(vmem_limit_bytes=48 * 2**20),
        cost_estimate=pl.CostEstimate(
            flops=2 * rows * width * columns,
            bytes_accessed=2 * (2 * rows * width + (rows + width) * columns),
            transcendentals=0,
        ),
        name="first_grads",
    )(normal, projected, residual_grad, attended)


def on_device(
    tokens,
    out_cotangent,
    seq_lengths,
    span_order,
    attention_input_weight,
    attention_input_first,
    attention_input_squared,
    attend_out,
    attend_out_moment,
    attend_out_second,
    gate_up,
    gate_up_moment,
    gate_up_second,
    down_weight,
    down_weight_moment,
    down_weight_second,
    norm_gains,
    norm_gains_moment,
    norm_gains_second,
):
    low = jnp.bfloat16
    micro_count, slot_count, row_count, model_width = tokens.shape
    seqs = micro_count * slot_count
    ctx_size = lax.axis_size("ctx")
    tp_size = lax.axis_size("tp")
    sequence_length = row_count * ctx_size
    span_len = sequence_length // (2 * ctx_size)
    hidden = down_weight.shape[0]
    out_width = attend_out.shape[0]
    in_width = attention_input_weight.shape[1]
    shards = ("fsdp", "ctx")

    ahead = in_width // 128 * 128
    tail = jnp.concatenate([attention_input_weight[:, ahead:], norm_gains.T], 1).astype(low)
    tail = jnp.pad(tail, ((0, 0), (0, -tail.shape[1] % 128)))

    orders = span_order.reshape(seqs, 2 * ctx_size)
    lengths = seq_lengths.reshape(seqs)
    within = jnp.arange(sequence_length, dtype=jnp.int32)
    block_ids = jnp.arange(2 * ctx_size, dtype=jnp.int32)
    table = jnp.where(
        block_ids[None, None, :] == (within // span_len)[None, :, None], orders[:, None, :], 0
    )
    pos_all = jnp.sum(table, -1) * span_len + within % span_len
    pos_here = lax.dynamic_slice_in_dim(pos_all, lax.axis_index("ctx") * row_count, row_count, 1)
    half_width = HEAD_DIMENSION // 2
    inverse = rope_base ** (-(jnp.arange(half_width, dtype=jnp.float32) * 2.0 / HEAD_DIMENSION))
    angles = pos_here.astype(jnp.float32)[:, None, :] * inverse[None, :, None]
    cosine, sine = jnp.cos(angles), jnp.sin(angles)
    where = (cosine, sine, orders, lengths)

    all_rows = seqs * row_count
    token_rows = tokens.reshape(all_rows, model_width)
    (
        in_whole,
        out_whole,
        pair_whole,
        first_normal,
        grad_out,
        gains,
        queries,
        key_values,
        attended_full,
        attended,
        log_total,
        residual,
        second_normal,
    ) = front(
        token_rows,
        out_cotangent.reshape(all_rows, model_width),
        attention_input_weight,
        tail,
        attend_out.T,
        gate_up,
        down_weight.T,
        where,
        seqs,
        ctx_size,
        tp_size,
        lax.axis_size("fsdp"),
        1,
    )

    early = 1
    second_grads, inner, grad_gate, grad_up, mixed_early = hidden_units(
        second_normal, grad_out, residual, pair_whole, seqs, early, tp_size, 2
    )
    inner, second_grads = lax.optimization_barrier((inner, second_grads))
    second_share = lax.psum_scatter(second_grads, shards, scatter_dimension=0, tiled=True)

    grad_residual, mixed, grad_projected, second_gain = back_one(
        inner,
        grad_gate,
        grad_up,
        pair_whole,
        mixed_early,
        residual,
        grad_out,
        gains,
        out_whole,
        queries,
        key_values,
        attended_full,
        log_total,
        where,
        ctx_size,
        tp_size,
        4,
    )
    first_grads = first_grads_of(
        first_normal, grad_projected, grad_residual, attended
    )
    grad_projected, first_grads, second_share = lax.optimization_barrier(
        (grad_projected, first_grads, second_share)
    )
    first_share = lax.psum_scatter(first_grads, shards, scatter_dimension=0, tiled=True)
    fsdp_size = lax.axis_size("fsdp")
    input_grad, gain_grads = back_two(
        grad_projected,
        in_whole,
        token_rows,
        grad_residual,
        gains,
        second_gain,
        0,
        seqs,
        ctx_size,
        fsdp_size,
        tp_size,
        5,
    )
    own = norm_gains.shape[1]
    shard = lax.axis_index("fsdp") * ctx_size + lax.axis_index("ctx")
    gain_share = lax.dynamic_slice_in_dim(gain_grads[:2], shard * own, own, 1)

    gradients = (
        first_share[:, out_width:],
        first_share[:, :out_width].T,
        second_share[:, : 2 * hidden],
        second_share[:, 2 * hidden :].T,
        gain_share,
    )
    masters = (attention_input_weight, attend_out, gate_up, down_weight, norm_gains)
    firsts = (
        attention_input_first,
        attend_out_moment,
        gate_up_moment,
        down_weight_moment,
        norm_gains_moment,
    )
    seconds = (
        attention_input_squared,
        attend_out_second,
        gate_up_second,
        down_weight_second,
        norm_gains_second,
    )
    results = [mixed.reshape(tokens.shape), input_grad.reshape(tokens.shape).astype(jnp.float32)]
    for at in range(5):
        updated = adam_update(
            masters[at],
            firsts[at],
            seconds[at],
            gradients[at].astype(jnp.float32),
            learn_rates[at],
            decay_flags[at],
        )
        results.extend(updated)
        if at < 4:
            results.append(updated[2].astype(low))
    return tuple(results)


def solution(mesh):
    rows = P(None, "fsdp", "ctx", None)
    upper = P(("fsdp", "ctx"), "tp")
    lower = P("tp", ("fsdp", "ctx"))
    gain = P(None, ("fsdp", "ctx"))
    return jax.shard_map(
        on_device,
        mesh=mesh,
        in_specs=(rows, rows, P(None, "fsdp"), P(None, "fsdp", None))
        + (upper,) * 3
        + (lower,) * 3
        + (upper,) * 3
        + (lower,) * 3
        + (gain,) * 3,
        out_specs=(rows, rows)
        + (upper,) * 4
        + (lower,) * 4
        + (upper,) * 4
        + (lower,) * 4
        + (gain,) * 3,
        check_vma=False,
    )
```

```python
import functools

import jax
import jax.numpy as jnp
from jax import lax
from jax.experimental import pallas as pl
from jax.experimental.pallas import tpu as pltpu
from jax.sharding import PartitionSpec as P

QUERY_HEADS = 32
KEY_VALUE_HEADS = 8
HEAD_DIMENSION = 80
STEP = 10
GROUP = QUERY_HEADS // KEY_VALUE_HEADS

rope_base = 1000000.0
norm_eps = 1e-05
beta_one = 0.9
beta_two = 0.95
adam_eps = 1e-08
weight_decay = 0.1
learn_rates = (0.1, 0.5, 0.05, 0.04, 0.8)
decay_flags = (1.0, 1.0, 1.0, 1.0, 0.0)
neg_big = -1e30
log2_e = 1.4426950408889634
MESH = pl.DeviceIdType.MESH
VMEM = pltpu.VMEM
CHUNK = 16
LAG = 2


def adam_update(weight, moment, second, gradient, learn_rate, decay_flag):
    moment = beta_one * moment + (1.0 - beta_one) * gradient
    second = beta_two * second + (1.0 - beta_two) * gradient * gradient
    moment_hat = moment / (1.0 - beta_one**STEP)
    second_hat = second / (1.0 - beta_two**STEP)
    weight = weight - learn_rate * (
        moment_hat / (jnp.sqrt(second_hat) + adam_eps) + decay_flag * weight_decay * weight
    )
    return (moment, second, weight)


def line_greet(n, z):
    barrier = pltpu.get_barrier_semaphore()

    @pl.when(z > 0)
    def _():
        pl.semaphore_signal(barrier, inc=1, device_id={"tp": z - 1}, device_id_type=MESH)

    @pl.when(z < n - 1)
    def _():
        pl.semaphore_signal(barrier, inc=1, device_id={"tp": z + 1}, device_id_type=MESH)

    return (z > 0).astype(jnp.int32) + (z < n - 1).astype(jnp.int32)


class Line:
    def __init__(
        self, n, z, segments, segment_rows, parts, inbox, out, sems, finish, lag=LAG
    ):
        self.n, self.z, self.lag = n, z, lag
        self.segment_rows = segment_rows
        self.per_segment = segment_rows // (2 * CHUNK)
        self.chunks = segments * self.per_segment
        self.parts, self.inbox, self.out = parts, inbox, out
        self.red_send, self.red_recv, self.back_send, self.back_recv = sems
        self.finish = finish
        self.ticks = self.chunks + 2 * (n - 1) * self.lag

    def ready(self, segments):
        return segments * self.per_segment + 2 * (self.n - 1) * self.lag

    def rows(self, flow, g):
        start = (
            (g // self.per_segment) * self.segment_rows
            + flow * (self.segment_rows // 2)
            + (g % self.per_segment) * CHUNK
        )
        return pl.ds(pl.multiple_of(start, CHUNK), CHUNK)

    def hop(self, flow):
        return (self.n - 1 - self.z) if flow == 0 else self.z

    def neighbour(self, up):
        z = jnp.minimum(self.z + 1, self.n - 1) if up else jnp.maximum(self.z - 1, 0)
        return {"tp": z}

    def reduce_copy(self, flow, g, source):
        return pltpu.make_async_remote_copy(
            src_ref=source,
            dst_ref=self.inbox.at[self.rows(flow, g)],
            send_sem=self.red_send.at[flow, g],
            recv_sem=self.red_recv.at[flow, g],
            device_id=self.neighbour(flow == 1),
            device_id_type=MESH,
        )

    def back_copy(self, flow, g):
        rows = self.rows(flow, g)
        return pltpu.make_async_remote_copy(
            src_ref=self.out.at[rows],
            dst_ref=self.out.at[rows],
            send_sem=self.back_send.at[flow, g],
            recv_sem=self.back_recv.at[flow, g],
            device_id=self.neighbour(flow == 0),
            device_id_type=MESH,
        )

    def tick(self, t):
        n = self.n
        for flow in (0, 1):

            @pl.when((self.hop(flow) == 0) & (t >= 0) & (t < self.chunks))
            def _():
                self.reduce_copy(flow, t, self.parts.at[self.rows(flow, t)]).start()

        for flow in (0, 1):
            hop = self.hop(flow)
            g = t - hop * self.lag

            @pl.when((hop > 0) & (g >= 0) & (g < self.chunks))
            def _():
                rows = self.rows(flow, g)
                self.reduce_copy(flow, g, self.parts.at[rows]).wait_recv()
                total = self.inbox[rows, :].astype(jnp.float32) + self.parts[rows, :].astype(
                    jnp.float32
                )

                @pl.when(hop < n - 1)
                def _():
                    self.inbox[rows, :] = total.astype(jnp.bfloat16)
                    self.reduce_copy(flow, g, self.inbox.at[rows]).start()

                @pl.when(hop == n - 1)
                def _():
                    self.finish(g // self.per_segment, rows, total)
                    self.back_copy(flow, g).start()

        for flow in (0, 1):
            hop = self.hop(flow)
            back = t - (n - 1) * self.lag - (n - 1 - hop) * self.lag

            @pl.when((back >= 0) & (back < self.chunks) & (hop < n - 1))
            def _():
                self.back_copy(flow, back).wait_recv()

                @pl.when(hop > 0)
                def _():
                    self.back_copy(flow, back).start()

    def run(self, first, last):
        def step(t, carry):
            self.tick(t)
            return carry

        lax.fori_loop(first, last, step, 0)

    def drain(self):
        def step(g, carry):
            for flow in (0, 1):
                hop = self.hop(flow)

                @pl.when(hop < self.n - 1)
                def _():
                    self.reduce_copy(flow, g, self.parts.at[self.rows(flow, g)]).wait_send()

                @pl.when(hop > 0)
                def _():
                    self.back_copy(flow, g).wait_send()

            return carry

        lax.fori_loop(0, self.chunks, step, 0)


def line_scratch(rows, width, segments, segment_rows):
    chunks = segments * (segment_rows // (2 * CHUNK))
    return [VMEM((rows, width), jnp.bfloat16)] + [pltpu.SemaphoreType.DMA((2, chunks))] * 4


def line_cost(rows, width):
    return pl.CostEstimate(flops=rows * width, bytes_accessed=80 * rows * width, transcendentals=0)


def mean_of(values):
    return jnp.mean(values, axis=-1, keepdims=True)


def norm_back(total, values, gain, gain_sums):
    root = lax.rsqrt(mean_of(values * values) + norm_eps)
    standard = values * root
    terms = total * standard
    gain_sums[...] += functools.reduce(
        lambda a, b: a + b, [terms[low : low + 8] for low in range(0, CHUNK, 8)]
    )
    scaled = total * gain
    return root * (scaled - standard * mean_of(scaled * standard))


def turn(first, second, cosine, sine):
    return jnp.concatenate([first * cosine - second * sine, second * cosine + first * sine], 0)


def turn_back(first, second, cosine, sine):
    return jnp.concatenate([first * cosine + second * sine, second * cosine - first * sine], 0)


def fill_bias(bias, order_ref, length_ref, m, me, n):
    rows = bias.shape[1]
    span = rows // 2
    lane = lax.broadcasted_iota(jnp.int32, (1, rows), 1)
    query = jnp.where(
        lane < span,
        order_ref[m, 2 * me] * span + lane,
        order_ref[m, 2 * me + 1] * span + lane - span,
    )
    within = lax.broadcasted_iota(jnp.int32, (span, rows), 0)
    for block in range(2 * n):
        key = order_ref[m, block] * span + within
        allowed = (key <= query) & (key < length_ref[m])
        bias[block * span : (block + 1) * span, :] = jnp.where(allowed, 0.0, neg_big)


def cut(rows, parts):
    tiles = rows // 16
    ends = [tiles * i // parts * 16 for i in range(parts + 1)]
    return [(low, high - low) for low, high in zip(ends[:-1], ends[1:])]


class Gather:
    def __init__(self, source, whole, low, length, block_rows, fsdp, n, sems):
        self.source, self.whole = source, whole
        self.low, self.length, self.block_rows = low, length, block_rows
        self.fsdp, self.n = fsdp, n
        self.f, self.me = lax.axis_index("fsdp"), lax.axis_index("ctx")
        self.across = lax.rem(self.me + n // 2, n)
        self.other = self.me + 1 - 2 * lax.rem(self.me, 2)
        self.sems = sems
        self.first = max(16, min(length - 16, length * 6 // 160 * 16))

    def at(self, f, ctx, low=0, length=None):
        start = (f * self.n + ctx) * self.block_rows + self.low + low
        return self.whole.at[
            pl.ds(pl.multiple_of(start, 16), self.length if length is None else length)
        ]

    def copy(self, kind, source, target, where):
        return pltpu.make_async_remote_copy(
            src_ref=source,
            dst_ref=target,
            send_sem=self.sems.at[0, kind],
            recv_sem=self.sems.at[1, kind],
            device_id=where,
            device_id_type=MESH,
        )

    def own(self):
        return self.source.at[pl.ds(self.low, self.length)]

    def ahead(self, j):
        return lax.rem(self.f + j, self.fsdp)

    def behind(self, j):
        return lax.rem(self.f + self.fsdp - j, self.fsdp)

    def to_across(self):
        return self.copy(0, self.own(), self.at(self.f, self.me), {"ctx": self.across})

    def to_other(self):
        return self.copy(1, self.own(), self.at(self.f, self.me), {"ctx": self.other})

    def across_to_other(self):
        at = self.at(self.f, self.across)
        return self.copy(2, at, at, {"ctx": self.other})

    def to_ahead(self, j):
        return self.copy(3 * j, self.own(), self.at(self.f, self.me), {"fsdp": self.ahead(j)})

    def behind_to_other(self, j):
        at = self.at(self.behind(j), self.me)
        return self.copy(3 * j + 1, at, at, {"ctx": self.other})

    def corner_to_other(self, j):
        at = self.at(self.behind(j), self.across)
        return self.copy(3 * j + 2, at, at, {"ctx": self.other})

    def across_to_ahead(self, j):
        at = self.at(self.f, self.across, 0, self.first)
        return self.copy(3 * self.fsdp + 2 * j - 2, at, at, {"fsdp": self.ahead(j)})

    def behind_to_across(self, j):
        at = self.at(self.behind(j), self.me, self.first, self.length - self.first)
        return self.copy(3 * self.fsdp + 2 * j - 1, at, at, {"ctx": self.across})

    def local(self):
        return pltpu.make_async_copy(self.own(), self.at(self.f, self.me), self.sems.at[2, 0])

    def start(self):
        self.start_across()
        self.start_ahead()

    def start_across(self):
        self.to_across().start()

    def start_ahead(self):
        for j in range(1, self.fsdp):
            self.to_ahead(j).start()
        self.to_other().start()
        self.local().start()

    def forward(self):
        self.forward_across()
        self.forward_behind()

    def forward_across(self):
        self.to_across().wait_recv()
        for j in range(1, self.fsdp):
            self.across_to_ahead(j).start()
        self.across_to_other().start()

    def forward_behind(self):
        for j in range(1, self.fsdp):
            self.to_ahead(j).wait_recv()
            self.behind_to_across(j).start()
            self.behind_to_other(j).start()

    def corner(self):
        for j in range(1, self.fsdp):
            self.across_to_ahead(j).wait_recv()
            self.behind_to_across(j).wait_recv()
            self.corner_to_other(j).start()

    def finish(self):
        self.local().wait()
        self.to_other().wait_recv()
        self.across_to_other().wait_recv()
        for j in range(1, self.fsdp):
            self.behind_to_other(j).wait_recv()
            self.corner_to_other(j).wait_recv()

    def drain(self):
        self.to_across().wait_send()
        self.to_other().wait_send()
        self.across_to_other().wait_send()
        for j in range(1, self.fsdp):
            self.to_ahead(j).wait_send()
            self.behind_to_other(j).wait_send()
            self.corner_to_other(j).wait_send()
            self.across_to_ahead(j).wait_send()
            self.behind_to_across(j).wait_send()


def gather_sems(fsdp):
    return pltpu.SemaphoreType.DMA((3, 5 * fsdp - 2))


def front_body(
    n,
    tp,
    fsdp,
    groups,
    token_ref,
    in_ref,
    tail_ref,
    out_weight_ref,
    gate_up_ref,
    down_ref,
    cos_ref,
    sin_ref,
    cotangent_ref,
    order_ref,
    length_ref,
    in_whole_ref,
    out_whole_ref,
    pair_whole_ref,
    normal_out_ref,
    grad_out_ref,
    gain_ref,
    q_ref,
    kv_ref,
    full_ref,
    low_ref,
    log_ref,
    residual_ref,
    out_ref,
    in_whole,
    out_whole,
    normal_ref,
    in_pack,
    out_pack,
    pair_pack,
    staged,
    proj,
    bias,
    parts,
    load_sem,
    save_sem,
    send_sem,
    recv_sem,
    in_sems,
    out_sems,
    pair_sems,
    inbox,
    *sems,
):
    z = lax.axis_index("tp")
    f = lax.axis_index("fsdp")
    me = lax.axis_index("ctx")
    peers = line_greet(tp, z)
    barrier = pltpu.get_barrier_semaphore()
    for step in range(1, n):
        pl.semaphore_signal(
            barrier, inc=1, device_id={"ctx": lax.rem(me + step, n)}, device_id_type=MESH
        )
    for step in range(1, fsdp):
        pl.semaphore_signal(
            barrier, inc=1, device_id={"fsdp": lax.rem(f + step, fsdp)}, device_id_type=MESH
        )

    seqs, _, rows = q_ref.shape
    dim = HEAD_DIMENSION
    half = dim // 2
    group_width = (GROUP + 2) * dim
    in_width = groups * group_width
    heads = groups * GROUP
    width = token_ref.shape[1]
    tile = 512 if width % 512 == 0 else width
    block = in_ref.shape[0]
    pair_width = gate_up_ref.shape[1]
    whole_tiles = in_width // 128 * 128

    ranges = cut(block, pair_sems.shape[0])

    def loads(i):
        low, length = ranges[i]
        return [
            pltpu.make_async_copy(
                source.at[pl.ds(low, length)],
                staged.at[i % 2, pl.ds(0, length), pl.ds(first, source.shape[1])],
                load_sem.at[i % 2, at],
            )
            for at, (source, first) in enumerate(((gate_up_ref, 0), (down_ref, pair_width)))
        ]

    for load in loads(0):
        load.start()
    cotangent = pltpu.make_async_copy(cotangent_ref, parts, load_sem.at[2, 0])
    grad_out = pltpu.make_async_copy(parts, grad_out_ref, load_sem.at[2, 1])
    cotangent.start()
    in_pack[:, :whole_tiles] = in_ref[:, :whole_tiles].astype(jnp.bfloat16)
    in_pack[:, whole_tiles:] = tail_ref[...]
    out_pack[...] = out_weight_ref[...].astype(jnp.bfloat16)
    pl.semaphore_wait(barrier, peers + n - 1 + fsdp - 1)

    def gathers(source, whole, sems):
        return [
            Gather(source, whole, low, length, block, fsdp, n, sems.at[i])
            for i, (low, length) in enumerate(cut(block, sems.shape[0]))
        ]

    first = gathers(in_pack, in_whole, in_sems)
    outer = gathers(out_pack, out_whole, out_sems)
    pair = gathers(pair_pack, pair_whole_ref, pair_sems)
    for piece in first:
        piece.start()
    for i, (low, length) in enumerate(ranges):
        if i + 1 < len(ranges):
            for load in loads(i + 1):
                load.start()
        for load in loads(i):
            load.wait()
        pair_pack[low : low + length, :] = staged[i % 2, :length, :].astype(jnp.bfloat16)

    cotangent.wait()
    span = rows // 2

    def keep(at, carry):
        own = pl.ds(pl.multiple_of(at * span, CHUNK), span)
        m = at // 2
        position = order_ref[m, 2 * me + lax.rem(at, 2)] * span + lax.broadcasted_iota(
            jnp.int32, (span, width), 0
        )
        parts[own, :] = jnp.where(
            position < length_ref[m], parts[own, :].astype(jnp.float32), 0.0
        ).astype(jnp.bfloat16)
        return carry

    lax.fori_loop(0, 2 * seqs, keep, 0)
    grad_out.start()
    for piece in first:
        piece.forward()
    for piece in outer:
        piece.start()
    for piece in first:
        piece.corner()
    for piece in first:
        piece.finish()
    for piece in outer:
        piece.forward()
    for piece in pair:
        piece.start_ahead()
    saves = [
        pltpu.make_async_copy(in_whole, in_whole_ref, save_sem.at[0]),
        pltpu.make_async_copy(normal_ref, normal_out_ref, save_sem.at[1]),
        pltpu.make_async_copy(out_whole, out_whole_ref, save_sem.at[2]),
    ]
    saves[0].start()

    turned = in_whole[:, whole_tiles : whole_tiles + 128].astype(jnp.float32).T
    gain_ref[...] = turned[in_width - whole_tiles : in_width - whole_tiles + 8]

    def columns_of(m):
        return pl.ds(pl.multiple_of(m * rows, 128), rows)

    def rows_of(m):
        return pl.ds(pl.multiple_of(m * rows, CHUNK), rows)

    def copy(m, step):
        return pltpu.make_async_remote_copy(
            src_ref=kv_ref.at[m, me],
            dst_ref=kv_ref.at[m, me],
            send_sem=send_sem.at[m, step - 1],
            recv_sem=recv_sem.at[m, step - 1],
            device_id={"ctx": lax.rem(me + step, n)},
            device_id_type=MESH,
        )

    def project(m, carry):
        values = token_ref[rows_of(m), :].astype(jnp.float32)
        root = lax.rsqrt(mean_of(values * values) + norm_eps)
        normal_ref[rows_of(m), :] = (values * root * gain_ref[0:1, :]).astype(jnp.bfloat16)
        proj[m] = jnp.dot(
            normal_ref[rows_of(m), :],
            in_whole[:, :in_width],
            preferred_element_type=jnp.float32,
        ).T
        for g in range(groups):
            col = g * group_width + GROUP * dim
            kv_ref[m, me, g, :dim, :] = turn(
                proj[m, col : col + half, :],
                proj[m, col + half : col + dim, :],
                cos_ref[m],
                sin_ref[m],
            ).astype(jnp.bfloat16)
            kv_ref[m, me, g, dim:, :] = proj[m, col + dim : col + 2 * dim, :].astype(jnp.bfloat16)
        for step in range(1, n):
            copy(m, step).start()
        return carry

    lax.fori_loop(0, seqs, project, 0)
    for piece in pair:
        piece.start_across()
    saves[1].start()

    def finish(segment, at, total):
        values = token_ref[at, :].astype(jnp.float32) + total
        residual_ref[at, :] = values.astype(jnp.bfloat16)
        root = lax.rsqrt(mean_of(values * values) + norm_eps)
        out_ref[at, :] = (values * root * gain_ref[1:2, :]).astype(jnp.bfloat16)

    line = Line(tp, z, seqs, rows, parts, inbox, out_ref, sems, finish)

    def head(m, at):
        g = at // GROUP
        h = at % GROUP
        low = pl.ds(pl.multiple_of(at * dim, 16), dim)
        col = pl.multiple_of(g * group_width + h * dim, 8)
        query = turn(
            proj[m, pl.ds(col, half), :],
            proj[m, pl.ds(pl.multiple_of(col + half, 8), half), :],
            cos_ref[m],
            sin_ref[m],
        ).astype(jnp.bfloat16)
        q_ref[m, low, :] = query
        scores = [
            lax.dot_general(
                kv_ref[m, j, g, :dim, :],
                query,
                (((0,), (0,)), ((), ())),
                preferred_element_type=jnp.float32,
            )
            * (log2_e * dim**-0.5)
            + bias[j * rows : (j + 1) * rows, :]
            for j in range(n)
        ]
        top = functools.reduce(jnp.maximum, [jnp.max(s, axis=0, keepdims=True) for s in scores])
        total = jnp.zeros_like(top)
        out = jnp.zeros((dim, rows), jnp.float32)
        for j in range(n):
            weights = jnp.exp2(scores[j] - top)
            total += jnp.sum(weights, axis=0, keepdims=True)
            out += jnp.dot(
                kv_ref[m, j, g, dim:, :],
                weights.astype(jnp.bfloat16),
                preferred_element_type=jnp.float32,
            )
        out = out / total
        full_ref[m, low, :] = out
        low_ref[low, columns_of(m)] = out.astype(jnp.bfloat16)
        log_ref[m, at] = top + jnp.log2(total)

    def ready(m):
        fill_bias(bias, order_ref, length_ref, m, me, n)
        for step in range(1, n):
            copy(m, step).wait_recv()

    def product(m):
        left = low_ref[:, columns_of(m)].T
        for low in range(0, width, tile):
            parts[rows_of(m), low : low + tile] = lax.dot_general(
                left,
                out_whole[low : low + tile, :],
                (((1,), (1,)), ((), ())),
                preferred_element_type=jnp.float32,
            ).astype(jnp.bfloat16)

    def sequence(m, carry):
        ready(m)

        def item(at, inner):
            line.tick((m - 1) * heads + at)
            head(m, at)
            return inner

        lax.fori_loop(0, heads, item, 0)
        product(m)
        return carry

    def opening(at, carry):
        head(0, at)
        return carry

    ready(0)
    lax.fori_loop(0, heads, opening, 0)
    grad_out.wait()
    for piece in outer:
        piece.corner()
    for piece in outer:
        piece.finish()
    saves[2].start()
    product(0)
    pair[0].forward_behind()
    lax.fori_loop(1, 2, sequence, 0)
    for piece in pair[1:2]:
        piece.forward_behind()
    lax.fori_loop(2, seqs, sequence, 0)
    at = (seqs - 1) * heads
    for piece in pair[2:3]:
        piece.forward_behind()
    pair[0].forward_across()
    line.run(at, at + 2)
    for piece in pair[3:]:
        piece.forward_behind()
    line.run(at + 2, at + 4)
    for piece in pair[1:2]:
        piece.forward_across()
    line.run(at + 4, at + 10)
    for piece in pair[2:3]:
        piece.forward_across()
    line.run(at + 10, at + 16)
    for piece in pair[3:]:
        piece.forward_across()
    line.run(at + 16, line.ticks)
    for piece in pair:
        piece.corner()
    for piece in pair:
        piece.finish()
    line.drain()
    for piece in first + outer + pair:
        piece.drain()
    for save in saves:
        save.wait()

    def drain(m, carry):
        for step in range(1, n):
            copy(m, step).wait_send()
        return carry

    lax.fori_loop(0, seqs, drain, 0)


def front(
    tokens, cotangent, in_weight, tail, out_weight, gate_up, down, where, seqs, n, tp, fsdp, ident
):
    all_rows, model_width = tokens.shape
    cosine, sine, orders, lengths = where
    rows = all_rows // seqs
    block, in_width = in_weight.shape
    groups = in_width // ((GROUP + 2) * HEAD_DIMENSION)
    heads = groups * GROUP
    shards = n * fsdp
    dim = HEAD_DIMENSION
    padded = in_width // 128 * 128 + tail.shape[1]
    out_width = out_weight.shape[1]
    pair_width = gate_up.shape[1] + down.shape[1]
    pieces = min(4, block // 32)
    longest = max(length for _, length in cut(block, pieces))
    shape = jax.ShapeDtypeStruct
    low, wide = jnp.bfloat16, jnp.float32
    vmem = pl.BlockSpec(memory_space=VMEM)
    hbm = pl.BlockSpec(memory_space=pl.ANY)
    smem = pl.BlockSpec(memory_space=pltpu.SMEM)
    dma = pltpu.SemaphoreType.DMA
    gather_sems = (3, 5 * fsdp - 2)
    return pl.pallas_call(
        functools.partial(front_body, n, tp, fsdp, groups),
        out_shape=(
            shape((shards * block, padded), low),
            shape((shards * block, out_width), low),
            shape((shards * block, pair_width), low),
            shape((all_rows, model_width), low),
            shape((all_rows, model_width), low),
            shape((8, model_width), wide),
            shape((seqs, heads * dim, rows), low),
            shape((seqs, n, groups, 2 * dim, rows), low),
            shape((seqs, heads * dim, rows), wide),
            shape((heads * dim, all_rows), low),
            shape((seqs, heads, 1, rows), wide),
            shape((all_rows, model_width), low),
            shape((all_rows, model_width), low),
        ),
        in_specs=[vmem] * 4 + [hbm] * 2 + [vmem] * 2 + [hbm] + [smem] * 2,
        out_specs=(hbm,) * 5 + (vmem,) * 8,
        scratch_shapes=[
            VMEM((shards * block, padded), low),
            VMEM((shards * block, out_width), low),
            VMEM((all_rows, model_width), low),
            VMEM((block, padded), low),
            VMEM((block, out_width), low),
            VMEM((block, pair_width), low),
            VMEM((2, longest, pair_width), wide),
            VMEM((seqs, in_width, rows), wide),
            VMEM((n * rows, rows), wide),
            VMEM((all_rows, model_width), low),
            dma((3, 2)),
            dma((3,)),
            dma((seqs, n - 1)),
            dma((seqs, n - 1)),
            dma((min(2, pieces),) + gather_sems),
            dma((1,) + gather_sems),
            dma((pieces,) + gather_sems),
        ]
        + line_scratch(all_rows, model_width, seqs, rows),
        compiler_params=pltpu.CompilerParams(
            collective_id=ident, has_side_effects=True, vmem_limit_bytes=60 * 2**20
        ),
        cost_estimate=line_cost(all_rows, model_width),
        name="front",
    )(tokens, in_weight, tail, out_weight, gate_up, down, cosine, sine, cotangent, orders, lengths)


def back_one_body(
    n,
    tp,
    groups,
    late,
    gate_ref,
    up_ref,
    pair_ref,
    gain_ref,
    log_ref,
    cos_ref,
    sin_ref,
    inner_from,
    residual_from,
    grad_out_from,
    weight_from,
    q_from,
    kv_from,
    full_from,
    early_from,
    order_ref,
    length_ref,
    grad_to,
    mixed_to,
    proj_ref,
    gain_sums,
    out_ref,
    parts,
    weights,
    inner_ref,
    residual_ref,
    grad_out_ref,
    out_proj,
    q_ref,
    kv_ref,
    full_ref,
    grads,
    sums,
    bias,
    outbox,
    kv_inbox,
    load_sem,
    save_sem,
    weight_sem,
    send_sem,
    recv_sem,
    inbox,
    *sems,
):
    z = lax.axis_index("tp")
    me = lax.axis_index("ctx")
    seqs, _, rows = q_ref.shape
    all_rows = seqs * rows
    units = inner_ref.shape[1]
    tile = weights.shape[1]
    pieces = out_ref.shape[1] // tile
    loads = [
        pltpu.make_async_copy(source, target, load_sem.at[at])
        for at, (source, target) in enumerate(
            (
                (inner_from, inner_ref),
                (residual_from, residual_ref),
                (grad_out_from, grad_out_ref),
                (weight_from, out_proj),
                (q_from, q_ref),
                (kv_from, kv_ref),
                (full_from, full_ref),
            )
        )
    ]

    early_rows = all_rows - late * rows
    saves = [
        pltpu.make_async_copy(early_from, mixed_to.at[pl.ds(0, early_rows)], save_sem.at[0]),
        pltpu.make_async_copy(out_ref.at[pl.ds(rows, all_rows)], grad_to, save_sem.at[1]),
        pltpu.make_async_copy(
            out_ref.at[pl.ds(0, rows)], mixed_to.at[pl.ds(early_rows, rows)], save_sem.at[2]
        ),
    ]
    if late > 1:
        saves.append(
            pltpu.make_async_copy(
                out_ref.at[pl.ds(rows + all_rows, (late - 1) * rows)],
                mixed_to.at[pl.ds(early_rows + rows, (late - 1) * rows)],
                save_sem.at[3],
            )
        )

    def tile_of(at):
        return pl.ds(pl.multiple_of(at * tile, tile), tile)

    def fetch(at):
        slot = lax.rem(at, 2)
        return pltpu.make_async_copy(
            pair_ref.at[tile_of(lax.rem(at, pieces)), pl.ds(0, 2 * units)],
            weights.at[slot],
            weight_sem.at[slot],
        )

    def fetch_down(at):
        slot = lax.rem(at, 2)
        return pltpu.make_async_copy(
            pair_ref.at[tile_of(at), pl.ds(2 * units, units)],
            weights.at[slot, :, pl.ds(0, units)],
            weight_sem.at[slot],
        )

    fetch_down(0).start()
    for load in loads:
        load.start()
    saves[0].start()
    peers = line_greet(tp, z)
    barrier = pltpu.get_barrier_semaphore()
    for step in range(1, n):
        pl.semaphore_signal(
            barrier, inc=1, device_id={"ctx": lax.rem(me + step, n)}, device_id_type=MESH
        )
    pl.semaphore_wait(barrier, peers + n - 1)

    dim = HEAD_DIMENSION
    half = dim // 2
    scale = dim**-0.5
    group_width = (GROUP + 2) * dim
    heads = groups * GROUP
    gain_sums[...] = jnp.zeros_like(gain_sums)

    ahead = rows
    first_late = seqs - late

    def finish(segment, at, total):
        is_grad = (segment >= 1) & (segment <= seqs)

        @pl.when(is_grad)
        def _():
            own = pl.ds(pl.multiple_of(at.start - ahead, CHUNK), CHUNK)
            grad = norm_back(
                total, residual_ref[own, :].astype(jnp.float32), gain_ref[1:2, :], gain_sums
            )
            out_ref[at, :] = (grad_out_ref[own, :].astype(jnp.float32) + grad).astype(jnp.bfloat16)

        @pl.when(jnp.logical_not(is_grad))
        def _():
            moved = jnp.where(segment == 0, first_late * rows, (first_late - seqs) * rows)
            own = pl.ds(pl.multiple_of(at.start + moved, CHUNK), CHUNK)
            out_ref[at, :] = (residual_ref[own, :].astype(jnp.float32) + total).astype(jnp.bfloat16)

    line = Line(tp, z, seqs + late, rows, parts, inbox, out_ref, sems, finish)

    def copy(m, step):
        to = lax.rem(me + step, n)
        return pltpu.make_async_remote_copy(
            src_ref=outbox.at[m, to],
            dst_ref=kv_inbox.at[m, step - 1],
            send_sem=send_sem.at[m, step - 1],
            recv_sem=recv_sem.at[m, step - 1],
            device_id={"ctx": to},
            device_id_type=MESH,
        )

    def columns(m):
        return pl.ds(pl.multiple_of(m * rows, 128), rows)

    def attended_grads(m):
        grads[...] = (
            jnp.dot(
                out_ref[pl.ds(pl.multiple_of(ahead + m * rows, CHUNK), rows), :],
                out_proj[...],
                preferred_element_type=jnp.float32,
            )
            .T.astype(jnp.bfloat16)
        )
        fill_bias(bias, order_ref, length_ref, m, me, n)

    def head(m, at):
        g = at // GROUP
        h = at % GROUP
        low = pl.ds(pl.multiple_of(at * dim, 16), dim)
        query = q_ref[m, low, :]
        grad = grads[low, :]
        delta = jnp.sum(
            grad.astype(jnp.float32) * full_ref[m, low, :], axis=0, keepdims=True
        )
        log_total = log_ref[m, at]
        query_sum = jnp.zeros((dim, rows), jnp.float32)

        @pl.when(h == 0)
        def _():
            sums[...] = jnp.zeros_like(sums)

        for j in range(n):
            keys = kv_ref[m, j, g, :dim, :]
            values = kv_ref[m, j, g, dim:, :]
            scores = lax.dot_general(
                keys, query, (((0,), (0,)), ((), ())), preferred_element_type=jnp.float32
            )
            probs = jnp.exp2(
                scores * (log2_e * scale) + (bias[j * rows : (j + 1) * rows, :] - log_total)
            )
            grad_probs = lax.dot_general(
                values, grad, (((0,), (0,)), ((), ())), preferred_element_type=jnp.float32
            )
            grad_scores = (probs * (grad_probs - delta)).astype(jnp.bfloat16)
            query_sum += jnp.dot(keys, grad_scores, preferred_element_type=jnp.float32)
            sums[j, :dim, :] += lax.dot_general(
                query, grad_scores, (((1,), (1,)), ((), ())), preferred_element_type=jnp.float32
            )
            sums[j, dim:, :] += lax.dot_general(
                grad,
                probs.astype(jnp.bfloat16),
                (((1,), (1,)), ((), ())),
                preferred_element_type=jnp.float32,
            )
        query_sum = query_sum * scale
        col = pl.ds(pl.multiple_of(g * group_width + h * dim, 16), dim)
        proj_ref[col, columns(m)] = turn_back(
            query_sum[:half], query_sum[half:], cos_ref[m], sin_ref[m]
        ).astype(jnp.bfloat16)

        @pl.when(h == GROUP - 1)
        def _():
            for j in range(n):
                outbox[m, j, g, :dim, :] = (sums[j, :dim, :] * scale).astype(jnp.bfloat16)
                outbox[m, j, g, dim:, :] = sums[j, dim:, :].astype(jnp.bfloat16)

    def gather(m):
        for step in range(1, n):
            copy(m, step).wait_recv()
        for g in range(groups):
            total = outbox[m, me, g].astype(jnp.float32)
            for step in range(1, n):
                total += kv_inbox[m, step - 1, g].astype(jnp.float32)
            col = g * group_width + GROUP * dim
            proj_ref[col : col + dim, columns(m)] = turn_back(
                total[:half], total[half:dim], cos_ref[m], sin_ref[m]
            ).astype(jnp.bfloat16)
            proj_ref[col + dim : col + 2 * dim, columns(m)] = total[dim:].astype(jnp.bfloat16)
        for step in range(1, n):
            copy(m, step).wait_send()

    contract = (((1,), (1,)), ((), ()))
    ticks_ahead = line.per_segment

    def leave(m, tile_at):
        at = m * pieces + tile_at
        own = pl.ds(pl.multiple_of(m * rows, CHUNK), rows)
        slot = lax.rem(at, 2)

        @pl.when(at + 1 < seqs * pieces)
        def _():
            fetch(at + 1).start()

        fetch(at).wait()
        parts[pl.ds(pl.multiple_of(ahead + m * rows, CHUNK), rows), tile_of(tile_at)] = (
            lax.dot_general(
                gate_ref[own, :],
                weights[slot, :, :units],
                contract,
                preferred_element_type=jnp.float32,
            )
            + lax.dot_general(
                up_ref[own, :],
                weights[slot, :, units:],
                contract,
                preferred_element_type=jnp.float32,
            )
        ).astype(jnp.bfloat16)

    def expand(low, count, to, first_tick):
        def item(at, carry):
            if first_tick is not None:

                @pl.when(at < ticks_ahead)
                def _():
                    line.tick(first_tick + at)

            @pl.when(at + 1 < pieces)
            def _():
                fetch_down(at + 1).start()

            fetch_down(at).wait()
            parts[pl.ds(to, count * rows), tile_of(at)] = lax.dot_general(
                inner_ref[pl.ds(low * rows, count * rows), :],
                weights[lax.rem(at, 2), :, :units],
                contract,
                preferred_element_type=jnp.float32,
            ).astype(jnp.bfloat16)
            return carry

        lax.fori_loop(0, pieces, item, 0)

    loads[0].wait()
    expand(first_late, 1, 0, None)
    fetch(0).start()
    for load in loads[1:]:
        load.wait()

    def next_leave(m, carry):
        def item(tile_at, inner):
            @pl.when(tile_at < ticks_ahead)
            def _():
                line.tick(m * ticks_ahead + tile_at)

            leave(m, tile_at)
            return inner

        lax.fori_loop(0, pieces, item, 0)
        return carry

    lax.fori_loop(0, seqs, next_leave, 0)
    done = seqs * ticks_ahead
    if late > 1:
        fetch_down(0).start()
        expand(first_late + 1, late - 1, rows + all_rows, done)
        done += ticks_ahead
    opened = max(done, line.ready(2))
    line.run(done, opened)
    stride = max(heads // 2 + 1, -(-(line.ready(seqs + 1) - opened) // (seqs - 1)))

    def sequence(m, carry):
        first = opened + m * stride
        line.tick(first)
        attended_grads(m)

        def item(at, inner):
            @pl.when(lax.rem(at, 2) == 0)
            def _():
                line.tick(first + 1 + at // 2)

            head(m, at)
            return inner

        lax.fori_loop(0, heads, item, 0)
        line.run(first + 1 + heads // 2, first + stride)
        for step in range(1, n):
            copy(m, step).start()

        @pl.when(m > 0)
        def _():
            gather(m - 1)

        return carry

    lax.fori_loop(0, seqs, sequence, 0)
    saves[1].start()
    line.run(opened + seqs * stride, line.ticks)

    for save in saves[2:]:
        save.start()
    gather(seqs - 1)
    line.drain()
    for save in saves:
        save.wait()


def back_one(
    inner,
    grad_gate,
    grad_up,
    pair_whole,
    mixed_early,
    residual,
    grad_out,
    gains,
    out_whole,
    queries,
    key_values,
    full,
    log_total,
    where,
    n,
    tp,
    ident,
):
    seqs, width, rows = queries.shape
    groups = key_values.shape[2]
    all_rows, model_width = residual.shape
    late = seqs - mixed_early.shape[0] // rows
    cosine, sine, orders, lengths = where
    units = inner.shape[1]
    line_rows = all_rows + late * rows
    vmem = pl.BlockSpec(memory_space=VMEM)
    hbm = pl.BlockSpec(memory_space=pl.ANY)
    smem = pl.BlockSpec(memory_space=pltpu.SMEM)
    shape = jax.ShapeDtypeStruct
    return pl.pallas_call(
        functools.partial(back_one_body, n, tp, groups, late),
        out_shape=(
            shape((all_rows, model_width), jnp.bfloat16),
            shape((all_rows, model_width), jnp.bfloat16),
            shape((groups * (GROUP + 2) * HEAD_DIMENSION, all_rows), jnp.bfloat16),
            shape((8, model_width), jnp.float32),
        ),
        in_specs=[vmem] * 2 + [hbm] + [vmem] * 4 + [hbm] * 8 + [smem] * 2,
        out_specs=(hbm,) * 2 + (vmem,) * 2,
        scratch_shapes=[
            VMEM((line_rows, model_width), jnp.bfloat16),
            VMEM((line_rows, model_width), jnp.bfloat16),
            VMEM((2, 256, 2 * units), jnp.bfloat16),
            VMEM((all_rows, units), jnp.bfloat16),
            VMEM((all_rows, model_width), jnp.bfloat16),
            VMEM((all_rows, model_width), jnp.bfloat16),
            VMEM((model_width, width), jnp.bfloat16),
            VMEM(queries.shape, jnp.bfloat16),
            VMEM(key_values.shape, jnp.bfloat16),
            VMEM(full.shape, jnp.float32),
            VMEM((width, rows), jnp.bfloat16),
            VMEM((n, 2 * HEAD_DIMENSION, rows), jnp.float32),
            VMEM((n * rows, rows), jnp.float32),
            VMEM((seqs, n, groups, 2 * HEAD_DIMENSION, rows), jnp.bfloat16),
            VMEM((seqs, n - 1, groups, 2 * HEAD_DIMENSION, rows), jnp.bfloat16),
            pltpu.SemaphoreType.DMA((7,)),
            pltpu.SemaphoreType.DMA((4,)),
            pltpu.SemaphoreType.DMA((2,)),
            pltpu.SemaphoreType.DMA((seqs, n - 1)),
            pltpu.SemaphoreType.DMA((seqs, n - 1)),
        ]
        + line_scratch(line_rows, model_width, seqs + late, rows),
        compiler_params=pltpu.CompilerParams(
            collective_id=ident, has_side_effects=True, vmem_limit_bytes=60 * 2**20
        ),
        cost_estimate=line_cost(line_rows, model_width),
        name="back_one",
    )(
        grad_gate,
        grad_up,
        pair_whole,
        gains,
        log_total,
        cosine,
        sine,
        inner,
        residual,
        grad_out,
        out_whole,
        queries,
        key_values,
        full,
        mixed_early,
        orders,
        lengths,
    )


def back_two_body(
    n,
    fsdp,
    tp,
    seqs,
    skip,
    proj_ref,
    weight_ref,
    gain_ref,
    second_gain_ref,
    token_from,
    residual_grad_from,
    out_ref,
    gains_to,
    gain_sums,
    token_ref,
    residual_grad_ref,
    parts,
    mine,
    box,
    tp_mine,
    tp_box,
    load_sem,
    gain_sem,
    tp_sem,
    inbox,
    *sems,
):
    z = lax.axis_index("tp")
    loads = [
        pltpu.make_async_copy(token_from, token_ref, load_sem.at[0]),
        pltpu.make_async_copy(
            residual_grad_from.at[pl.ds(0, residual_grad_ref.shape[0])],
            residual_grad_ref,
            load_sem.at[1],
        ),
    ]
    for load in loads:
        load.start()
    me = lax.axis_index("fsdp") * n + lax.axis_index("ctx")
    shards = n * fsdp

    def shard_at(step):
        other = lax.rem(me + step, shards)
        return {"fsdp": other // n, "ctx": lax.rem(other, n)}

    def line_at(step):
        return {"tp": lax.rem(z + step, tp)}

    barrier = pltpu.get_barrier_semaphore()
    for step in range(1, shards):
        pl.semaphore_signal(barrier, inc=1, device_id=shard_at(step), device_id_type=MESH)
    for step in range(1, tp):
        pl.semaphore_signal(barrier, inc=1, device_id=line_at(step), device_id_type=MESH)
    pl.semaphore_wait(barrier, shards - 1 + tp - 1)
    gain_sums[...] = jnp.zeros_like(gain_sums)
    rows = token_ref.shape[0] // seqs
    width = weight_ref.shape[0]
    tile = 512 if width % 512 == 0 else width

    def finish(segment, at, total):
        values = token_ref[at, :].astype(jnp.float32)
        grad = norm_back(total, values, gain_ref[0:1, :], gain_sums)
        out_ref[at, :] = (residual_grad_ref[at, :].astype(jnp.float32) + grad).astype(jnp.bfloat16)

    line = Line(tp, z, seqs, rows, parts, inbox, out_ref, sems, finish)

    def product(m):
        left = proj_ref[:, m * rows : (m + 1) * rows].T
        for low in range(0, width, tile):
            parts[m * rows : (m + 1) * rows, low : low + tile] = lax.dot_general(
                left,
                weight_ref[low : low + tile, skip : skip + proj_ref.shape[0]],
                (((1,), (1,)), ((), ())),
                preferred_element_type=jnp.float32,
            ).astype(jnp.bfloat16)

    for m in range(seqs):
        product(m)
        line.run(2 * m, 2 * m + 2)
        if m == 0:
            for load in loads:
                load.wait()
    finished = line.chunks + (tp - 1) * line.lag
    line.run(2 * seqs, finished)
    mine[...] = jnp.zeros_like(mine)
    mine[0:1, :] = jnp.sum(gain_sums[...], axis=0, keepdims=True)
    mine[1:2, :] = jnp.sum(second_gain_ref[...], axis=0, keepdims=True)

    def copy(source, boxes, sem, step, where):
        return pltpu.make_async_remote_copy(
            src_ref=source,
            dst_ref=boxes.at[step - 1],
            send_sem=sem.at[0, step - 1],
            recv_sem=sem.at[1, step - 1],
            device_id=where,
            device_id_type=MESH,
        )

    for step in range(1, shards):
        copy(mine, box, gain_sem, step, shard_at(step)).start()
    line.run(finished, line.ticks)
    total = mine[...]
    for step in range(1, shards):
        copy(mine, box, gain_sem, step, shard_at(step)).wait()
        total += box[step - 1]
    tp_mine[...] = total
    for step in range(1, tp):
        copy(tp_mine, tp_box, tp_sem, step, line_at(step)).start()
    for step in range(1, tp):
        copy(tp_mine, tp_box, tp_sem, step, line_at(step)).wait()
        total += tp_box[step - 1]
    gains_to[...] = total
    line.drain()


def back_two(
    projected, first_whole, tokens, residual_grad, gains, second_gain, skip, seqs, n, fsdp, tp, ident
):
    rows, width = tokens.shape
    vmem = pl.BlockSpec(memory_space=VMEM)
    hbm = pl.BlockSpec(memory_space=pl.ANY)
    shape = jax.ShapeDtypeStruct
    return pl.pallas_call(
        functools.partial(back_two_body, n, fsdp, tp, seqs, skip),
        out_shape=(shape((rows, width), jnp.bfloat16), shape((8, width), jnp.float32)),
        in_specs=[vmem] * 4 + [hbm] * 2,
        out_specs=(vmem,) * 2,
        scratch_shapes=[VMEM((8, width), jnp.float32)]
        + [VMEM((rows, width), jnp.bfloat16)] * 3
        + [
            VMEM((8, width), jnp.float32),
            VMEM((n * fsdp - 1, 8, width), jnp.float32),
            VMEM((8, width), jnp.float32),
            VMEM((tp - 1, 8, width), jnp.float32),
            pltpu.SemaphoreType.DMA((2,)),
            pltpu.SemaphoreType.DMA((2, n * fsdp - 1)),
            pltpu.SemaphoreType.DMA((2, tp - 1)),
        ]
        + line_scratch(rows, width, seqs, rows // seqs),
        compiler_params=pltpu.CompilerParams(
            collective_id=ident, has_side_effects=True, vmem_limit_bytes=56 * 2**20
        ),
        cost_estimate=line_cost(rows, width),
        name="back_two",
    )(projected, first_whole, gains, second_gain, tokens, residual_grad)


def hidden_body(
    tp,
    seqs,
    early,
    normal_ref,
    grad_out_ref,
    residual_ref,
    whole_ref,
    grads_ref,
    inner_ref,
    gate_ref,
    up_ref,
    out_ref,
    residual,
    turned,
    staged,
    columns,
    weights,
    parts,
    load_sem,
    column_sem,
    weight_sem,
    store_sem,
    inbox,
    *sems,
):
    z = lax.axis_index("tp")
    rows, units = inner_ref.shape
    width = normal_ref.shape[1]
    tile = staged.shape[2]
    pieces = width // tile
    steps = units // tile
    early_rows = parts.shape[0]

    def columns_of(at):
        return pl.ds(pl.multiple_of(at * tile, tile), tile)

    def fetch_columns(at):
        slot = lax.rem(at, 2)
        return [
            pltpu.make_async_copy(
                whole_ref.at[:, columns_of(kind * steps + lax.rem(at, steps))],
                columns.at[slot, kind],
                column_sem.at[slot, kind],
            )
            for kind in range(3)
        ]

    def fetch(at):
        slot = lax.rem(at, 2)
        return pltpu.make_async_copy(
            whole_ref.at[columns_of(at), pl.ds(2 * units, units)],
            weights.at[slot],
            weight_sem.at[slot],
        )

    load = pltpu.make_async_copy(
        residual_ref.at[pl.ds(0, early_rows)], residual, load_sem.at[0]
    )
    for copy in fetch_columns(0):
        copy.start()
    load.start()
    pl.semaphore_wait(pltpu.get_barrier_semaphore(), line_greet(tp, z))

    def finish(segment, at, total):
        out_ref[at, :] = (residual[at, :].astype(jnp.float32) + total).astype(jnp.bfloat16)

    line = Line(tp, z, early, rows // seqs, parts, inbox, out_ref, sems, finish, LAG + 1)

    early_opening = rows // seqs

    def units_of(at, low, high):
        slot = lax.rem(at, 2)

        @pl.when(at + 1 < 2 * steps)
        def _():
            for copy in fetch_columns(at + 1):
                copy.start()

        for copy in fetch_columns(at):
            copy.wait()

        def product(left, kind):
            return jnp.dot(
                left[low:high, :], columns[slot, kind], preferred_element_type=jnp.float32
            )

        gate = product(normal_ref, 0)
        up = product(normal_ref, 1)
        grad_inner = product(grad_out_ref, 2)
        sigmoid = jax.nn.sigmoid(gate)
        silu = gate * sigmoid
        to = columns_of(lax.rem(at, steps))
        inner_ref[low:high, to] = (silu * up).astype(jnp.bfloat16)
        gate_ref[low:high, to] = (
            grad_inner * up * sigmoid * (1.0 + gate * (1.0 - sigmoid))
        ).astype(jnp.bfloat16)
        up_ref[low:high, to] = (grad_inner * silu).astype(jnp.bfloat16)

    def opening(at, carry):
        units_of(at, 0, early_opening)
        return carry

    fetch(0).start()
    lax.fori_loop(0, steps, opening, 0)

    def expand(low, high):
        def item(at, carry):
            @pl.when(at + 1 < pieces)
            def _():
                fetch(at + 1).start()

            fetch(at).wait()
            parts[low:high, columns_of(at)] = lax.dot_general(
                inner_ref[low:high, :],
                weights[lax.rem(at, 2)],
                (((1,), (1,)), ((), ())),
                preferred_element_type=jnp.float32,
            ).astype(jnp.bfloat16)
            return carry

        lax.fori_loop(0, pieces, item, 0)

    expand(0, early_opening)
    load.wait()

    def others(at, carry):
        line.tick(at)
        units_of(steps + at, early_opening, rows)
        return carry

    if early_rows > early_opening:
        fetch(0).start()
    lax.fori_loop(0, steps, others, 0)
    if early_rows > early_opening:
        expand(early_opening, early_rows)
    turned[...] = normal_ref[...].T

    def store(at):
        slot = lax.rem(at, 2)
        return pltpu.make_async_copy(
            staged.at[slot], grads_ref.at[:, columns_of(at)], store_sem.at[slot]
        )

    for kind, right in enumerate((gate_ref, up_ref, inner_ref)):
        if kind == 2:
            turned[...] = grad_out_ref[...].T

        def gradient(step, carry):
            at = kind * steps + step
            line.tick(steps + at)

            @pl.when(at >= 2)
            def _():
                store(at - 2).wait()

            staged[lax.rem(at, 2)] = jnp.dot(
                turned[...], right[:, columns_of(step)], preferred_element_type=jnp.float32
            ).astype(jnp.bfloat16)
            store(at).start()
            return carry

        lax.fori_loop(0, steps, gradient, 0)

    store(3 * steps - 2).wait()
    store(3 * steps - 1).wait()
    line.run(4 * steps, line.ticks)
    line.drain()


def hidden_units(normal, grad_out, residual, whole, seqs, early, tp, ident):
    all_rows, width = normal.shape
    columns = whole.shape[1]
    units = columns // 3
    rows = all_rows // seqs
    tile = 256
    low = jnp.bfloat16
    shape = jax.ShapeDtypeStruct
    vmem = pl.BlockSpec(memory_space=VMEM)
    hbm = pl.BlockSpec(memory_space=pl.ANY)
    dma = pltpu.SemaphoreType.DMA
    return pl.pallas_call(
        functools.partial(hidden_body, tp, seqs, early),
        out_shape=(shape((width, columns), low),)
        + (shape((all_rows, units), low),) * 3
        + (shape((early * rows, width), low),),
        in_specs=[vmem] * 2 + [hbm] * 2,
        out_specs=(hbm,) + (vmem,) * 4,
        scratch_shapes=[
            VMEM((early * rows, width), low),
            VMEM((width, all_rows), low),
            VMEM((2, width, tile), low),
            VMEM((2, 3, width, tile), low),
            VMEM((2, tile, units), low),
            VMEM((early * rows, width), low),
            dma((1,)),
            dma((2, 3)),
            dma((2,)),
            dma((2,)),
        ]
        + line_scratch(early * rows, width, early, rows),
        compiler_params=pltpu.CompilerParams(
            collective_id=ident, has_side_effects=True, vmem_limit_bytes=60 * 2**20
        ),
        cost_estimate=pl.CostEstimate(
            flops=4 * all_rows * width * columns,
            bytes_accessed=40 * all_rows * width,
            transcendentals=all_rows * units,
        ),
        name="hidden_units",
    )(normal, grad_out, residual, whole)


def first_grads_body(normal_ref, proj_ref, residual_ref, attended_ref, out_ref):
    split = attended_ref.shape[0]
    contract = (((1,), (1,)), ((), ()))
    for left, right, low in ((residual_ref, attended_ref, 0), (normal_ref, proj_ref, split)):
        out_ref[:, low : low + right.shape[0]] = lax.dot_general(
            left[...].T, right[...], contract, preferred_element_type=jnp.float32
        ).astype(jnp.bfloat16)


def first_grads_of(normal, projected, residual_grad, attended):
    rows, width = normal.shape
    columns = projected.shape[0] + attended.shape[0]
    tile = 512 if width % 512 == 0 else width
    vmem = pl.BlockSpec(memory_space=VMEM)
    left = pl.BlockSpec((rows, tile), lambda i: (0, i))
    return pl.pallas_call(
        first_grads_body,
        grid=(width // tile,),
        out_shape=jax.ShapeDtypeStruct((width, columns), jnp.bfloat16),
        in_specs=[left, vmem, left, vmem],
        out_specs=pl.BlockSpec((tile, columns), lambda i: (i, 0)),
        compiler_params=pltpu.CompilerParams(vmem_limit_bytes=48 * 2**20),
        cost_estimate=pl.CostEstimate(
            flops=2 * rows * width * columns,
            bytes_accessed=2 * (2 * rows * width + (rows + width) * columns),
            transcendentals=0,
        ),
        name="first_grads",
    )(normal, projected, residual_grad, attended)


def on_device(
    tokens,
    out_cotangent,
    seq_lengths,
    span_order,
    attention_input_weight,
    attention_input_first,
    attention_input_squared,
    attend_out,
    attend_out_moment,
    attend_out_second,
    gate_up,
    gate_up_moment,
    gate_up_second,
    down_weight,
    down_weight_moment,
    down_weight_second,
    norm_gains,
    norm_gains_moment,
    norm_gains_second,
):
    low = jnp.bfloat16
    micro_count, slot_count, row_count, model_width = tokens.shape
    seqs = micro_count * slot_count
    ctx_size = lax.axis_size("ctx")
    tp_size = lax.axis_size("tp")
    sequence_length = row_count * ctx_size
    span_len = sequence_length // (2 * ctx_size)
    hidden = down_weight.shape[0]
    out_width = attend_out.shape[0]
    in_width = attention_input_weight.shape[1]
    shards = ("fsdp", "ctx")

    ahead = in_width // 128 * 128
    tail = jnp.concatenate([attention_input_weight[:, ahead:], norm_gains.T], 1).astype(low)
    tail = jnp.pad(tail, ((0, 0), (0, -tail.shape[1] % 128)))

    orders = span_order.reshape(seqs, 2 * ctx_size)
    lengths = seq_lengths.reshape(seqs)
    within = jnp.arange(sequence_length, dtype=jnp.int32)
    block_ids = jnp.arange(2 * ctx_size, dtype=jnp.int32)
    table = jnp.where(
        block_ids[None, None, :] == (within // span_len)[None, :, None], orders[:, None, :], 0
    )
    pos_all = jnp.sum(table, -1) * span_len + within % span_len
    pos_here = lax.dynamic_slice_in_dim(pos_all, lax.axis_index("ctx") * row_count, row_count, 1)
    half_width = HEAD_DIMENSION // 2
    inverse = rope_base ** (-(jnp.arange(half_width, dtype=jnp.float32) * 2.0 / HEAD_DIMENSION))
    angles = pos_here.astype(jnp.float32)[:, None, :] * inverse[None, :, None]
    cosine, sine = jnp.cos(angles), jnp.sin(angles)
    where = (cosine, sine, orders, lengths)

    all_rows = seqs * row_count
    token_rows = tokens.reshape(all_rows, model_width)
    (
        in_whole,
        out_whole,
        pair_whole,
        first_normal,
        grad_out,
        gains,
        queries,
        key_values,
        attended_full,
        attended,
        log_total,
        residual,
        second_normal,
    ) = front(
        token_rows,
        out_cotangent.reshape(all_rows, model_width),
        attention_input_weight,
        tail,
        attend_out.T,
        gate_up,
        down_weight.T,
        where,
        seqs,
        ctx_size,
        tp_size,
        lax.axis_size("fsdp"),
        1,
    )

    early = 1
    second_grads, inner, grad_gate, grad_up, mixed_early = hidden_units(
        second_normal, grad_out, residual, pair_whole, seqs, early, tp_size, 2
    )
    inner, second_grads = lax.optimization_barrier((inner, second_grads))
    second_share = lax.psum_scatter(second_grads, shards, scatter_dimension=0, tiled=True)

    grad_residual, mixed, grad_projected, second_gain = back_one(
        inner,
        grad_gate,
        grad_up,
        pair_whole,
        mixed_early,
        residual,
        grad_out,
        gains,
        out_whole,
        queries,
        key_values,
        attended_full,
        log_total,
        where,
        ctx_size,
        tp_size,
        4,
    )
    first_grads = first_grads_of(
        first_normal, grad_projected, grad_residual, attended
    )
    grad_projected, first_grads, second_share = lax.optimization_barrier(
        (grad_projected, first_grads, second_share)
    )
    first_share = lax.psum_scatter(first_grads, shards, scatter_dimension=0, tiled=True)
    fsdp_size = lax.axis_size("fsdp")
    input_grad, gain_grads = back_two(
        grad_projected,
        in_whole,
        token_rows,
        grad_residual,
        gains,
        second_gain,
        0,
        seqs,
        ctx_size,
        fsdp_size,
        tp_size,
        5,
    )
    own = norm_gains.shape[1]
    shard = lax.axis_index("fsdp") * ctx_size + lax.axis_index("ctx")
    gain_share = lax.dynamic_slice_in_dim(gain_grads[:2], shard * own, own, 1)

    gradients = (
        first_share[:, out_width:],
        first_share[:, :out_width].T,
        second_share[:, : 2 * hidden],
        second_share[:, 2 * hidden :].T,
        gain_share,
    )
    masters = (attention_input_weight, attend_out, gate_up, down_weight, norm_gains)
    firsts = (
        attention_input_first,
        attend_out_moment,
        gate_up_moment,
        down_weight_moment,
        norm_gains_moment,
    )
    seconds = (
        attention_input_squared,
        attend_out_second,
        gate_up_second,
        down_weight_second,
        norm_gains_second,
    )
    results = [mixed.reshape(tokens.shape), input_grad.reshape(tokens.shape).astype(jnp.float32)]
    for at in range(5):
        updated = adam_update(
            masters[at],
            firsts[at],
            seconds[at],
            gradients[at].astype(jnp.float32),
            learn_rates[at],
            decay_flags[at],
        )
        results.extend(updated)
        if at < 4:
            results.append(updated[2].astype(low))
    return tuple(results)


def solution(mesh):
    rows = P(None, "fsdp", "ctx", None)
    upper = P(("fsdp", "ctx"), "tp")
    lower = P("tp", ("fsdp", "ctx"))
    gain = P(None, ("fsdp", "ctx"))
    return jax.shard_map(
        on_device,
        mesh=mesh,
        in_specs=(rows, rows, P(None, "fsdp"), P(None, "fsdp", None))
        + (upper,) * 3
        + (lower,) * 3
        + (upper,) * 3
        + (lower,) * 3
        + (gain,) * 3,
        out_specs=(rows, rows)
        + (upper,) * 4
        + (lower,) * 4
        + (upper,) * 4
        + (lower,) * 4
        + (gain,) * 3,
        check_vma=False,
    )
```
